32 devices in a mesh: rep: 2 (over x), grp: 8 (over z, y), loc: 2 (over core).
Axes of the slice: x: 2, y: 2, z: 4, core: 2. Of those that a mesh axis runs over, the one named last changes fastest.
Arguments:
- tokens: bfloat16 [4096, 2048], P(('rep', 'grp', 'loc')), parts along dimension 0, may hold values from -6 to 6
- cotangent: bfloat16 [4096, 2048], P(('rep', 'grp', 'loc')), parts along dimension 0, may hold values from -4 to 4
- expert_ids: int32 [4096, 8], P(('rep', 'grp', 'loc')), parts along dimension 0, may hold values from 0 to 31, as said below
- route_weights: bfloat16 [4096, 8], P(('rep', 'grp', 'loc')), parts along dimension 0, may hold values from 0.049804688 to 0.5
- gate_weight: bfloat16 [32, 2048, 384], P(('grp', 'loc')), may hold values from -0.125 to 0.125
- up_weight: bfloat16 [32, 2048, 384], P(('grp', 'loc')), may hold values from -0.125 to 0.125
- down_weight: bfloat16 [32, 384, 2048], P(('grp', 'loc')), may hold values from -0.3125 to 0.3125
Outputs:
- grad_tokens: bfloat16 [4096, 2048], P(('rep', 'grp', 'loc')), parts along dimension 0
- grad_weights: bfloat16 [4096, 8], P(('rep', 'grp', 'loc')), parts along dimension 0
The draws below stay inside these ranges and needn't reach their ends.
There are 2 independent parts, one for each index of `rep`. The reference program is written for one: setup_inputs(seed, part) draws one part's arguments, and reference() takes and returns one part's arrays. A program takes and returns all parts, laid end to end along the dimension named above; an argument that names none is the same for every part. Nothing has to cross between parts.
Inputs may be any that keep to these rules, and one draw needn't show every extreme that they name: `expert_ids`: each row names 8 distinct experts, two in each of exactly 4 groups (group = id // 4). In each device's aligned block of 128 rows at most 96 rows name any one group, and some groups reach 96 in every block; every expert of a group is named by exactly half of the block's rows that name the group. In all, at most 768 rows name any one expert, and some experts reach it.
All inputs are finite; a program needn't handle non-finite values.
Results may differ from the reference program's by a relative error of at most 0.009.
Values may be sent and summed in bfloat16 or wider, within the bound.
No kernel may reach another device: no remote copies, remote signals or barrier semaphores. Data moves between devices by JAX's collectives and lax.ppermute only.
A program may use at most 128 MiB of HBM per device.

```python
import math
import jax
import jax.numpy as jnp
from jax import lax

D = 2048
FF = 384
TOP = 8
TOP_GROUPS = 4
TOK_DEV = 128
GROUP_EXP = 4
GROUPS = 8
EXPERTS = 32
TOKENS = 2048
CAP_G = 96
CAP_E = 768


def draw_expert_ids(key, part):
    key = jax.random.fold_in(key, 17)
    group_total = GROUPS
    block_total = TOKENS // TOK_DEV
    per_block = TOK_DEV
    hot_total = group_total // 4
    cold_total = group_total - hot_total
    cold_pairs = 5 * per_block // 4
    base_pairs = cold_pairs // cold_total
    rem_pairs = cold_pairs % cold_total
    key_order, key_kind, key_tokens, key_slots = jax.random.split(key, 4)
    group_order = jax.random.permutation(key_order, group_total).astype(jnp.int32)
    rank_iota = jnp.arange(group_total, dtype=jnp.int32)
    block_iota = jnp.arange(block_total, dtype=jnp.int32)
    extra_pair = (jnp.mod(rank_iota[None, :] - hot_total - block_iota[:, None], cold_total) < rem_pairs).astype(jnp.int32)
    tallies = jnp.where(rank_iota[None, :] < hot_total, CAP_G, 2 * (base_pairs + extra_pair)).astype(jnp.int32)
    run_ends = jnp.cumsum(tallies, axis=1)
    starts = run_ends - tallies
    position = jnp.arange(TOP_GROUPS * per_block, dtype=jnp.int32)
    run_of = jnp.sum((position[None, :, None] >= run_ends[:, None, :]).astype(jnp.int32), axis=2)
    within = position[None, :] - jnp.take_along_axis(starts, run_of, axis=1)
    parity = within % 2
    split_kind = jax.random.randint(key_kind, (block_total, group_total), 0, 3)
    kind_of = jnp.take_along_axis(split_kind, run_of, axis=1)
    first_table = jnp.array([[0, 2], [0, 1], [0, 1]], dtype=jnp.int32)
    second_table = jnp.array([[1, 3], [2, 3], [3, 2]], dtype=jnp.int32)
    group_of = group_order[run_of]
    first_ids = group_of * GROUP_EXP + first_table[kind_of, parity]
    second_ids = group_of * GROUP_EXP + second_table[kind_of, parity]
    pair_ids = jnp.stack([first_ids, second_ids], axis=2)
    per_token = pair_ids.reshape(block_total, TOP_GROUPS, per_block, 2).transpose(0, 2, 1, 3).reshape(block_total, per_block, TOP)
    token_scores = jax.random.randint(key_tokens, (block_total, per_block), 0, 1 << 20) * per_block + jnp.arange(per_block, dtype=jnp.int32)[None, :]
    token_order = jnp.argsort(token_scores, axis=1)
    per_token = jnp.take_along_axis(per_token, token_order[:, :, None], axis=1)
    slot_scores = jax.random.randint(key_slots, (block_total, per_block, TOP), 0, 1 << 20) * TOP + jnp.arange(TOP, dtype=jnp.int32)[None, None, :]
    slot_order = jnp.argsort(slot_scores, axis=2)
    per_token = jnp.take_along_axis(per_token, slot_order, axis=2)
    return per_token.reshape(block_total * per_block, TOP).astype(jnp.int32)


def level_of(stream_key, extent, shards, least, largest):
    level = 1.0
    for axis_at, shards_of in shards:
        steps = jax.random.uniform(jax.random.fold_in(jax.random.fold_in(stream_key, 6), axis_at), (shards_of,), jnp.float32, least / len(shards), largest / len(shards))
        level = level * jnp.repeat(jnp.exp(steps), extent[axis_at] // shards_of).reshape((-1,) + (1,) * (len(extent) - 1 - axis_at))
    return level


def centred(rng, shape, spread, reach, pieces=(), kind=jnp.bfloat16):
    factor_of = level_of(rng, shape, pieces, -0.22, 0.18) if pieces else 1.0
    values = jax.random.normal(rng, shape, jnp.float32) * spread * factor_of
    return jnp.minimum(jnp.maximum(values, -reach), reach).astype(kind)


def setup_inputs(seed: int = 0, part: int = 0) -> dict:
    streams_of = jax.random.split(jax.random.key(seed), 8)
    part_splits = jax.random.split(jax.random.fold_in(streams_of[7], part), 8)
    return {
        "tokens": centred(part_splits[0], (TOKENS, D), 1.0, 6.0, ((0, 16),)),
        "cotangent": centred(part_splits[1], (TOKENS, D), 0.5, 4.0, ((0, 16),)),
        "expert_ids": draw_expert_ids(jax.random.fold_in(jax.random.fold_in(streams_of[7], part), 71), part),
        "route_weights": jnp.clip(jnp.exp(math.log(0.5) - 2.306499 * jax.random.uniform(part_splits[3], (TOKENS, TOP), jnp.float32) ** level_of(part_splits[3], (TOKENS, TOP), ((0, 16),), -0.2, 0.2)), 0.049804688, 0.5).astype(jnp.bfloat16),
        "gate_weight": centred(streams_of[4], (EXPERTS, D, FF), D ** -0.5, 0.125, ((0, 16),)),
        "up_weight": centred(streams_of[5], (EXPERTS, D, FF), D ** -0.5, 0.125, ((0, 16),)),
        "down_weight": centred(streams_of[6], (EXPERTS, FF, D), FF ** -0.5, 0.3125, ((0, 16),)),
    }


def expert_terms(token_rows, grad_rows, weight_rows, gate_matrix, up_matrix, down_matrix):
    gate_act = jnp.dot(token_rows, gate_matrix, preferred_element_type=jnp.float32)
    up_act = jnp.dot(token_rows, up_matrix, preferred_element_type=jnp.float32)
    back_grad = jnp.dot(grad_rows, down_matrix.T, preferred_element_type=jnp.float32)
    sigmoid_val = jax.nn.sigmoid(gate_act)
    silu_val = gate_act * sigmoid_val
    route_grad = jnp.sum(back_grad * silu_val * up_act, axis=1)
    hidden_grad = weight_rows[:, None] * back_grad
    gate_grad = (hidden_grad * up_act * sigmoid_val * (1.0 + gate_act * (1.0 - sigmoid_val))).astype(jnp.bfloat16)
    up_grad = (hidden_grad * silu_val).astype(jnp.bfloat16)
    input_grad = jnp.dot(gate_grad, gate_matrix.T, preferred_element_type=jnp.float32)
    input_grad = input_grad + jnp.dot(up_grad, up_matrix.T, preferred_element_type=jnp.float32)
    return input_grad, route_grad


def reference(tokens, cotangent, expert_ids, route_weights, gate_weight, up_weight, down_weight):
    slot_total = TOKENS * TOP
    flat_ids = expert_ids.reshape(slot_total)
    flat_weight = jnp.concatenate([route_weights.reshape(slot_total).astype(jnp.float32), jnp.zeros((1,), jnp.float32)])
    pad_tokens = jnp.concatenate([tokens, jnp.zeros((1, D), tokens.dtype)])
    pad_cotangent = jnp.concatenate([cotangent, jnp.zeros((1, D), cotangent.dtype)])

    def group_step(carried, group_idx):
        running, route_acc = carried
        group_sum = jnp.zeros((TOKENS, D), jnp.float32)
        for local_idx in range(GROUP_EXP):
            expert_idx = group_idx * GROUP_EXP + local_idx
            slot_idx = jnp.nonzero(flat_ids == expert_idx, size=CAP_E, fill_value=slot_total)[0].astype(jnp.int32)
            token_idx = (slot_idx // TOP).astype(jnp.int32)
            input_grad, route_grad = expert_terms(pad_tokens[token_idx], pad_cotangent[token_idx], flat_weight[slot_idx], gate_weight[expert_idx], up_weight[expert_idx], down_weight[expert_idx])
            group_sum = group_sum.at[token_idx].add(input_grad, mode="drop")
            route_acc = route_acc.at[slot_idx].add(route_grad, mode="drop")
        rounded = lax.optimization_barrier(group_sum.astype(jnp.bfloat16))
        return (running + rounded.astype(jnp.float32), route_acc), None

    start_state = (jnp.zeros((TOKENS, D), jnp.float32), jnp.zeros((slot_total,), jnp.float32))
    final_state, unused = lax.scan(group_step, start_state, jnp.arange(GROUPS, dtype=jnp.int32))
    running, route_acc = final_state
    return running.astype(jnp.bfloat16), route_acc.reshape(TOKENS, TOP).astype(jnp.bfloat16)
```

```python
import functools

import jax
import jax.numpy as jnp
from jax import lax
from jax.experimental import pallas as pl
from jax.experimental.pallas import tpu as pltpu
from jax.sharding import PartitionSpec as P

TOP = 8
TOP_GROUPS = 4


def shortened(shard):
    return jax.tree.map(lambda a: a.astype(jnp.bfloat16) if a.dtype == jnp.float32 else a, shard)


def take_rows(values, indices, filler):
    return jnp.take(values, indices, axis=0, mode="fill", fill_value=filler)


def route_table(targets, dest_total, capacity):
    token_total = targets.shape[0]
    dest_iota = jnp.arange(dest_total, dtype=jnp.int32)
    reached = jnp.any(targets[:, :, None] == dest_iota[None, None, :], axis=1)
    ranked = jnp.cumsum(reached.astype(jnp.int32), axis=0) - 1
    slot_of = jnp.where(reached, ranked, capacity)
    dest_grid = jnp.broadcast_to(dest_iota[None, :], slot_of.shape)
    token_grid = jnp.broadcast_to(jnp.arange(token_total, dtype=jnp.int32)[:, None], slot_of.shape)
    sources = jnp.full((dest_total, capacity), token_total, jnp.int32)
    sources = sources.at[dest_grid, slot_of].set(token_grid, mode="drop")
    return (slot_of, sources)


def token_groups(group_ids, group_total):
    token_total = group_ids.shape[0]
    group_iota = jnp.arange(group_total, dtype=jnp.int32)
    reached = jnp.any(group_ids[:, :, None] == group_iota[None, None, :], axis=1)
    ranked = jnp.cumsum(reached.astype(jnp.int32), axis=1) - 1
    column = jnp.where(reached, ranked, TOP_GROUPS)
    token_grid = jnp.broadcast_to(jnp.arange(token_total, dtype=jnp.int32)[:, None], column.shape)
    listed = jnp.full((token_total, TOP_GROUPS), group_total, jnp.int32)
    return listed.at[token_grid, column].set(
        jnp.broadcast_to(group_iota[None, :], column.shape), mode="drop"
    )


def expert_pass(
    token_rows,
    grad_rows,
    id_rows,
    weight_rows,
    gate_weight,
    up_weight,
    down_weight,
    first_expert,
    capacity,
):
    row_total = token_rows.shape[0]
    local_total = gate_weight.shape[0]
    model_width = token_rows.shape[1]
    experts_here = first_expert + jnp.arange(local_total, dtype=jnp.int32)
    matched = id_rows[None, :, :] == experts_here[:, None, None]
    chosen = jnp.any(matched, axis=2)
    weight_of = jnp.sum(
        jnp.where(matched, weight_rows.astype(jnp.float32)[None, :, :], 0.0), axis=2
    )
    ranked = jnp.cumsum(chosen.astype(jnp.int32), axis=1) - 1
    slot_of = jnp.where(chosen, ranked, capacity)
    expert_grid = jnp.broadcast_to(jnp.arange(local_total, dtype=jnp.int32)[:, None], slot_of.shape)
    row_grid = jnp.broadcast_to(jnp.arange(row_total, dtype=jnp.int32)[None, :], slot_of.shape)
    picks = (
        jnp.full((local_total, capacity), row_total, jnp.int32)
        .at[expert_grid, slot_of]
        .set(row_grid, mode="drop")
    )
    buffer_x = take_rows(token_rows, picks, 0)
    buffer_g = take_rows(grad_rows, picks, 0)
    buffer_w = jnp.take_along_axis(weight_of, picks, axis=1, mode="fill", fill_value=0.0)
    gate_act = jnp.einsum("ecd,edf->ecf", buffer_x, gate_weight, preferred_element_type=jnp.float32)
    up_act = jnp.einsum("ecd,edf->ecf", buffer_x, up_weight, preferred_element_type=jnp.float32)
    back_grad = jnp.einsum(
        "ecd,efd->ecf", buffer_g, down_weight, preferred_element_type=jnp.float32
    )
    sigmoid_val = jax.nn.sigmoid(gate_act)
    silu_val = gate_act * sigmoid_val
    route_grad = jnp.sum(back_grad * silu_val * up_act, axis=2)
    hidden_grad = buffer_w[:, :, None] * back_grad
    gate_grad = (
        hidden_grad * up_act * sigmoid_val * (1.0 + gate_act * (1.0 - sigmoid_val))
    ).astype(jnp.bfloat16)
    up_grad = (hidden_grad * silu_val).astype(jnp.bfloat16)
    input_grad = jnp.einsum(
        "ecf,edf->ecd", gate_grad, gate_weight, preferred_element_type=jnp.float32
    )
    input_grad = input_grad + jnp.einsum(
        "ecf,edf->ecd", up_grad, up_weight, preferred_element_type=jnp.float32
    )
    partial_value = jnp.zeros((row_total, model_width), jnp.float32)
    partial_value = partial_value.at[picks.reshape(-1)].add(
        input_grad.reshape(-1, model_width), mode="drop"
    )
    cap_grid = jnp.broadcast_to(jnp.arange(local_total, dtype=jnp.int32)[:, None], picks.shape)
    route_per = (
        jnp.zeros((local_total, row_total), jnp.float32)
        .at[cap_grid, picks]
        .add(route_grad, mode="drop")
    )
    route_rows = jnp.sum(jnp.where(matched, route_per[:, :, None], 0.0), axis=0)
    return (partial_value, route_rows)


def routed_body(tokens, cotangent, expert_ids, route_weights, gate_weight, up_weight, down_weight):
    group_total = lax.axis_size("grp")
    loc_total = lax.axis_size("loc")
    token_total = tokens.shape[0]
    model_width = tokens.shape[1]
    per_device = gate_weight.shape[0]
    per_group = per_device * loc_total
    group_cap = 6 * token_total // group_total
    expert_cap = 3 * token_total * loc_total
    device_rank = lax.axis_index("grp") * loc_total + lax.axis_index("loc")
    first_expert = device_rank * per_device
    group_ids = expert_ids // per_group
    listed = token_groups(group_ids, group_total)
    slot_range = jnp.arange(TOP, dtype=jnp.int32)[None, :]
    slot_of, sources = route_table(group_ids, group_total, group_cap)
    send_x = take_rows(tokens, sources, 0)
    send_g = take_rows(cotangent, sources, 0)
    send_ids = take_rows(expert_ids, sources, -1)
    send_w = take_rows(route_weights, sources, 0)
    recv_x, recv_g, recv_ids, recv_w = (
        lax.all_to_all(send_x, "grp", split_axis=0, concat_axis=0, tiled=True),
        lax.all_to_all(send_g, "grp", split_axis=0, concat_axis=0, tiled=True),
        lax.all_to_all(send_ids, "grp", split_axis=0, concat_axis=0, tiled=True),
        lax.all_to_all(send_w, "grp", split_axis=0, concat_axis=0, tiled=True),
    )
    row_total = group_total * group_cap
    shared_x, shared_g, shared_ids, shared_w = (
        lax.all_gather(recv_x.reshape(row_total, model_width), "loc", axis=0, tiled=True),
        lax.all_gather(recv_g.reshape(row_total, model_width), "loc", axis=0, tiled=True),
        lax.all_gather(shortened(recv_ids.reshape(row_total, TOP)), "loc", axis=0, tiled=True),
        lax.all_gather(recv_w.reshape(row_total, TOP), "loc", axis=0, tiled=True),
    )
    partial_value, route_rows = expert_pass(
        shared_x,
        shared_g,
        shared_ids,
        shared_w,
        gate_weight,
        up_weight,
        down_weight,
        first_expert,
        expert_cap,
    )
    summed, route_sum = (
        lax.psum_scatter(partial_value, "loc", scatter_dimension=0, tiled=True),
        lax.psum_scatter(route_rows, "loc", scatter_dimension=0, tiled=True),
    )
    group_part = summed.astype(jnp.bfloat16).reshape(group_total, group_cap, model_width)
    route_part = route_sum.astype(jnp.bfloat16).reshape(group_total, group_cap, TOP)
    back_terms, back_route = (
        lax.all_to_all(group_part, "grp", split_axis=0, concat_axis=0, tiled=True),
        lax.all_to_all(route_part, "grp", split_axis=0, concat_axis=0, tiled=True),
    )
    slot_pad = jnp.concatenate([slot_of, jnp.full((token_total, 1), group_cap, jnp.int32)], axis=1)
    found = jnp.take_along_axis(slot_pad, listed, axis=1)
    position = jnp.where(found < group_cap, listed * group_cap + found, row_total)
    pieces = take_rows(back_terms.reshape(row_total, model_width), position, 0)
    grad_tokens = jnp.sum(pieces.astype(jnp.float32), axis=1).astype(jnp.bfloat16)
    slot_found = jnp.take_along_axis(slot_of, group_ids, axis=1)
    route_index = (group_ids * group_cap + slot_found) * TOP + slot_range
    grad_weights = back_route.reshape(row_total * TOP)[route_index]
    return (grad_tokens, grad_weights)


LANES = 128
NT = (((1,), (1,)), ((), ()))


def experts_kernel(piece_rows, per_device, place, *refs):
    pieces = len(piece_rows)
    x_in, g_in = refs[:pieces], refs[pieces : 2 * pieces]
    (w_in, gate_own, up_own, down_own, gate_other, up_other, down_other, out, x, g, gate_up, down, total, sems, row_sems) = refs[
        2 * pieces :
    ]
    width = x.shape[1]
    hidden = down.shape[1]
    copies = []
    start = 0
    for i, rows in enumerate(piece_rows):
        copies.append(pltpu.make_async_copy(x_in[i], x.at[pl.ds(start, rows)], row_sems.at[0, i]))
        copies.append(pltpu.make_async_copy(g_in[i], g.at[pl.ds(start, rows)], row_sems.at[1, i]))
        start += rows
    for copy in copies:
        copy.start()

    def weight_copies(e, gate, up, down_weight, source):
        return (
            pltpu.make_async_copy(gate.at[source], gate_up.at[e, :, pl.ds(0, hidden)], sems.at[0, e]),
            pltpu.make_async_copy(up.at[source], gate_up.at[e, :, pl.ds(hidden, hidden)], sems.at[1, e]),
            pltpu.make_async_copy(down_weight.at[source], down.at[e], sems.at[2, e]),
        )

    for e in range(2 * per_device):
        mine = (gate_own, up_own, down_own) if e < per_device else (gate_other, up_other, down_other)
        for copy in weight_copies(e, *mine, e % per_device):
            copy.start()
    for copy in copies:
        copy.wait()
    weight_rows = jnp.concatenate(
        [w_in[pl.ds(pl.multiple_of(place[2 + i], 16), rows), :] for i, rows in enumerate(piece_rows)], axis=0
    ).astype(jnp.float32)
    lane = lax.broadcasted_iota(jnp.int32, weight_rows.shape, 1)

    def step(e, route):
        for copy in weight_copies(e, gate_own, up_own, down_own, 0):
            copy.wait()
        column = place[0] + lax.rem(place[1] + e, 2 * per_device)
        weight = jnp.sum(jnp.where(lane == column, weight_rows, 0.0), axis=1, keepdims=True)
        both = jnp.dot(x[...], gate_up[e], preferred_element_type=jnp.float32)
        gate_act, up_act = both[:, :hidden], both[:, hidden:]
        back = lax.dot_general(g[...], down[e], NT, preferred_element_type=jnp.float32)
        sig = jax.nn.sigmoid(gate_act)
        silu = gate_act * sig
        route_grad = jnp.sum(back * silu * up_act, axis=1, keepdims=True)
        hidden_grad = weight * back
        gate_grad = (hidden_grad * up_act * sig * (1.0 + gate_act * (1.0 - sig))).astype(jnp.bfloat16)
        up_grad = (hidden_grad * silu).astype(jnp.bfloat16)
        grads = jnp.concatenate([gate_grad, up_grad], axis=1)
        term = lax.dot_general(grads, gate_up[e], NT, preferred_element_type=jnp.float32)

        @pl.when(e == 0)
        def _():
            total[...] = term

        @pl.when(e > 0)
        def _():
            total[...] += term

        return route + jnp.where(lane == column, route_grad, 0.0)

    route = lax.fori_loop(0, 2 * per_device, step, jnp.zeros(weight_rows.shape, jnp.float32))
    out[:, :width] = total[...].astype(out.dtype)
    out[:, width:] = route.astype(out.dtype)


def experts_call(place, xs, gs, weight_table, own, other):
    piece_rows = tuple(a.shape[0] for a in xs)
    rows = sum(piece_rows)
    per_device, width, hidden = own[0].shape
    anywhere = pl.BlockSpec(memory_space=pl.ANY)
    return pl.pallas_call(
        functools.partial(experts_kernel, piece_rows, per_device),
        out_shape=jax.ShapeDtypeStruct((rows, width + LANES), jnp.bfloat16),
        in_specs=[pl.BlockSpec(memory_space=pltpu.SMEM)]
        + [anywhere] * (2 * len(xs))
        + [pl.BlockSpec(memory_space=pltpu.VMEM)]
        + [anywhere] * 6,
        out_specs=pl.BlockSpec(memory_space=pltpu.VMEM),
        scratch_shapes=[
            pltpu.VMEM((rows, width), jnp.bfloat16),
            pltpu.VMEM((rows, width), jnp.bfloat16),
            pltpu.VMEM((2 * per_device, width, 2 * hidden), jnp.bfloat16),
            pltpu.VMEM((2 * per_device, hidden, width), jnp.bfloat16),
            pltpu.VMEM((rows, width), jnp.float32),
            pltpu.SemaphoreType.DMA((3, 2 * per_device)),
            pltpu.SemaphoreType.DMA((2, len(xs))),
        ],
        compiler_params=pltpu.CompilerParams(vmem_limit_bytes=44 * 1024 * 1024),
        cost_estimate=pl.CostEstimate(
            flops=2 * per_device * rows * 10 * width * hidden,
            bytes_accessed=2 * per_device * 6 * width * hidden + rows * width * 6,
            transcendentals=2 * per_device * rows * hidden,
        ),
    )(place, *xs, *gs, weight_table, *own, *other)


def added(a, b):
    return (a.astype(jnp.float32) + b.astype(jnp.float32)).astype(jnp.bfloat16)


def ring_body(tokens, cotangent, expert_ids, route_weights, gate_weight, up_weight, down_weight):
    ring_total = lax.axis_size("grp")
    loc_total = lax.axis_size("loc")
    block, width = tokens.shape
    per_device = gate_weight.shape[0]
    expert_total = ring_total * loc_total * per_device
    order = list(range(0, ring_total, 2)) + list(range(ring_total - 1, 0, -2))
    ahead = [(order[i], order[(i + 1) % ring_total]) for i in range(ring_total)]
    behind = [(b, a) for a, b in ahead]
    rank, loc = lax.axis_index("grp"), lax.axis_index("loc")
    order_array = jnp.array(order, jnp.int32)
    position = jnp.argmax(order_array == rank).astype(jnp.int32)

    def send(a, way):
        return lax.ppermute(a, "grp", way)

    own = (gate_weight, up_weight, down_weight)
    swap = [(i, loc_total - 1 - i) for i in range(loc_total)]
    other = tuple(lax.ppermute(a, "loc", swap) for a in own)
    expert_iota = jnp.arange(LANES, dtype=jnp.int32)
    named = expert_ids[:, :, None] == expert_iota[None, None, :]
    table = jnp.sum(jnp.where(named, route_weights.astype(jnp.float32)[:, :, None], 0.0), axis=1)
    weight_table = lax.all_gather(table.astype(jnp.bfloat16), "grp", axis=0, tiled=True)
    lane_base = rank * (loc_total * per_device)

    def call(xs, gs, starts):
        place = jnp.stack([lane_base, loc * per_device] + starts).astype(jnp.int32)
        return experts_call(place, xs, gs, weight_table, own, other)

    def row_of(distance):
        return order_array[(position + distance) % ring_total] * block

    half = ring_total // 2
    cut = block // 2
    x_up, g_up, x_down, g_down = tokens, cotangent, tokens, cotangent
    partial_up, partial_down = [None], [None]
    own_part = call([tokens], [cotangent], [row_of(0)])
    for s in range(1, half):
        x_up, x_down = send(x_up, ahead), send(x_down, behind)
        g_up, g_down = send(g_up, ahead), send(g_down, behind)
        part = call([x_up, x_down], [g_up, g_down], [row_of(-s), row_of(s)])
        partial_up.append(part[:block])
        partial_down.append(part[block:])
    x_up, x_down = send(x_up[:cut], ahead), send(x_down[cut:], behind)
    g_up, g_down = send(g_up[:cut], ahead), send(g_down[cut:], behind)
    part = call([x_up, x_down], [g_up, g_down], [row_of(half), row_of(half) + cut])
    back_up, back_down = send(part[:cut], behind), send(part[cut:], ahead)
    for s in range(half - 1, 0, -1):
        if s == half - 1:
            mine = partial_up[s]
            sum_up = jnp.concatenate([added(mine[:cut], back_up), mine[cut:]], axis=0)
            mine = partial_down[s]
            sum_down = jnp.concatenate([mine[:cut], added(mine[cut:], back_down)], axis=0)
        else:
            sum_up, sum_down = added(partial_up[s], back_up), added(partial_down[s], back_down)
        back_up, back_down = send(sum_up, behind), send(sum_down, ahead)
    summed = own_part.astype(jnp.float32) + back_up.astype(jnp.float32) + back_down.astype(jnp.float32)
    grad_tokens = summed[:, :width].astype(jnp.bfloat16)
    route = summed[:, width:]
    grad_weights = jnp.sum(jnp.where(named, route[:, None, :], 0.0), axis=2).astype(jnp.bfloat16)
    return (grad_tokens, grad_weights)


def body(tokens, cotangent, expert_ids, route_weights, gate_weight, up_weight, down_weight):
    args = (tokens, cotangent, expert_ids, route_weights, gate_weight, up_weight, down_weight)
    ring_total, loc_total = lax.axis_size("grp"), lax.axis_size("loc")
    experts = ring_total * loc_total * gate_weight.shape[0]
    if loc_total == 2 and ring_total % 2 == 0 and 4 <= ring_total <= 8 and experts <= LANES and tokens.shape[0] % 32 == 0:
        return ring_body(*args)
    return routed_body(*args)


def solution(mesh):
    placed = (
        P(("rep", "grp", "loc"), None),
        P(("rep", "grp", "loc"), None),
        P(("rep", "grp", "loc"), None),
        P(("rep", "grp", "loc"), None),
        P(("grp", "loc"), None, None),
        P(("grp", "loc"), None, None),
        P(("grp", "loc"), None, None),
    )
    return jax.shard_map(
        body,
        mesh=mesh,
        in_specs=placed,
        out_specs=(P(("rep", "grp", "loc"), None), P(("rep", "grp", "loc"), None)),
        check_vma=False,
    )
```

```python
import functools

import jax
import jax.numpy as jnp
from jax import lax
from jax.experimental import pallas as pl
from jax.experimental.pallas import tpu as pltpu
from jax.sharding import PartitionSpec as P

TOP = 8
TOP_GROUPS = 4


def shortened(shard):
    return jax.tree.map(lambda a: a.astype(jnp.bfloat16) if a.dtype == jnp.float32 else a, shard)


def take_rows(values, indices, filler):
    return jnp.take(values, indices, axis=0, mode="fill", fill_value=filler)


def route_table(targets, dest_total, capacity):
    token_total = targets.shape[0]
    dest_iota = jnp.arange(dest_total, dtype=jnp.int32)
    reached = jnp.any(targets[:, :, None] == dest_iota[None, None, :], axis=1)
    ranked = jnp.cumsum(reached.astype(jnp.int32), axis=0) - 1
    slot_of = jnp.where(reached, ranked, capacity)
    dest_grid = jnp.broadcast_to(dest_iota[None, :], slot_of.shape)
    token_grid = jnp.broadcast_to(jnp.arange(token_total, dtype=jnp.int32)[:, None], slot_of.shape)
    sources = jnp.full((dest_total, capacity), token_total, jnp.int32)
    sources = sources.at[dest_grid, slot_of].set(token_grid, mode="drop")
    return (slot_of, sources)


def token_groups(group_ids, group_total):
    token_total = group_ids.shape[0]
    group_iota = jnp.arange(group_total, dtype=jnp.int32)
    reached = jnp.any(group_ids[:, :, None] == group_iota[None, None, :], axis=1)
    ranked = jnp.cumsum(reached.astype(jnp.int32), axis=1) - 1
    column = jnp.where(reached, ranked, TOP_GROUPS)
    token_grid = jnp.broadcast_to(jnp.arange(token_total, dtype=jnp.int32)[:, None], column.shape)
    listed = jnp.full((token_total, TOP_GROUPS), group_total, jnp.int32)
    return listed.at[token_grid, column].set(
        jnp.broadcast_to(group_iota[None, :], column.shape), mode="drop"
    )


def expert_pass(
    token_rows,
    grad_rows,
    id_rows,
    weight_rows,
    gate_weight,
    up_weight,
    down_weight,
    first_expert,
    capacity,
):
    row_total = token_rows.shape[0]
    local_total = gate_weight.shape[0]
    model_width = token_rows.shape[1]
    experts_here = first_expert + jnp.arange(local_total, dtype=jnp.int32)
    matched = id_rows[None, :, :] == experts_here[:, None, None]
    chosen = jnp.any(matched, axis=2)
    weight_of = jnp.sum(
        jnp.where(matched, weight_rows.astype(jnp.float32)[None, :, :], 0.0), axis=2
    )
    ranked = jnp.cumsum(chosen.astype(jnp.int32), axis=1) - 1
    slot_of = jnp.where(chosen, ranked, capacity)
    expert_grid = jnp.broadcast_to(jnp.arange(local_total, dtype=jnp.int32)[:, None], slot_of.shape)
    row_grid = jnp.broadcast_to(jnp.arange(row_total, dtype=jnp.int32)[None, :], slot_of.shape)
    picks = (
        jnp.full((local_total, capacity), row_total, jnp.int32)
        .at[expert_grid, slot_of]
        .set(row_grid, mode="drop")
    )
    buffer_x = take_rows(token_rows, picks, 0)
    buffer_g = take_rows(grad_rows, picks, 0)
    buffer_w = jnp.take_along_axis(weight_of, picks, axis=1, mode="fill", fill_value=0.0)
    gate_act = jnp.einsum("ecd,edf->ecf", buffer_x, gate_weight, preferred_element_type=jnp.float32)
    up_act = jnp.einsum("ecd,edf->ecf", buffer_x, up_weight, preferred_element_type=jnp.float32)
    back_grad = jnp.einsum(
        "ecd,efd->ecf", buffer_g, down_weight, preferred_element_type=jnp.float32
    )
    sigmoid_val = jax.nn.sigmoid(gate_act)
    silu_val = gate_act * sigmoid_val
    route_grad = jnp.sum(back_grad * silu_val * up_act, axis=2)
    hidden_grad = buffer_w[:, :, None] * back_grad
    gate_grad = (
        hidden_grad * up_act * sigmoid_val * (1.0 + gate_act * (1.0 - sigmoid_val))
    ).astype(jnp.bfloat16)
    up_grad = (hidden_grad * silu_val).astype(jnp.bfloat16)
    input_grad = jnp.einsum(
        "ecf,edf->ecd", gate_grad, gate_weight, preferred_element_type=jnp.float32
    )
    input_grad = input_grad + jnp.einsum(
        "ecf,edf->ecd", up_grad, up_weight, preferred_element_type=jnp.float32
    )
    partial_value = jnp.zeros((row_total, model_width), jnp.float32)
    partial_value = partial_value.at[picks.reshape(-1)].add(
        input_grad.reshape(-1, model_width), mode="drop"
    )
    cap_grid = jnp.broadcast_to(jnp.arange(local_total, dtype=jnp.int32)[:, None], picks.shape)
    route_per = (
        jnp.zeros((local_total, row_total), jnp.float32)
        .at[cap_grid, picks]
        .add(route_grad, mode="drop")
    )
    route_rows = jnp.sum(jnp.where(matched, route_per[:, :, None], 0.0), axis=0)
    return (partial_value, route_rows)


def routed_body(tokens, cotangent, expert_ids, route_weights, gate_weight, up_weight, down_weight):
    group_total = lax.axis_size("grp")
    loc_total = lax.axis_size("loc")
    token_total = tokens.shape[0]
    model_width = tokens.shape[1]
    per_device = gate_weight.shape[0]
    per_group = per_device * loc_total
    group_cap = 6 * token_total // group_total
    expert_cap = 3 * token_total * loc_total
    device_rank = lax.axis_index("grp") * loc_total + lax.axis_index("loc")
    first_expert = device_rank * per_device
    group_ids = expert_ids // per_group
    listed = token_groups(group_ids, group_total)
    slot_range = jnp.arange(TOP, dtype=jnp.int32)[None, :]
    slot_of, sources = route_table(group_ids, group_total, group_cap)
    send_x = take_rows(tokens, sources, 0)
    send_g = take_rows(cotangent, sources, 0)
    send_ids = take_rows(expert_ids, sources, -1)
    send_w = take_rows(route_weights, sources, 0)
    recv_x, recv_g, recv_ids, recv_w = (
        lax.all_to_all(send_x, "grp", split_axis=0, concat_axis=0, tiled=True),
        lax.all_to_all(send_g, "grp", split_axis=0, concat_axis=0, tiled=True),
        lax.all_to_all(send_ids, "grp", split_axis=0, concat_axis=0, tiled=True),
        lax.all_to_all(send_w, "grp", split_axis=0, concat_axis=0, tiled=True),
    )
    row_total = group_total * group_cap
    shared_x, shared_g, shared_ids, shared_w = (
        lax.all_gather(recv_x.reshape(row_total, model_width), "loc", axis=0, tiled=True),
        lax.all_gather(recv_g.reshape(row_total, model_width), "loc", axis=0, tiled=True),
        lax.all_gather(shortened(recv_ids.reshape(row_total, TOP)), "loc", axis=0, tiled=True),
        lax.all_gather(recv_w.reshape(row_total, TOP), "loc", axis=0, tiled=True),
    )
    partial_value, route_rows = expert_pass(
        shared_x,
        shared_g,
        shared_ids,
        shared_w,
        gate_weight,
        up_weight,
        down_weight,
        first_expert,
        expert_cap,
    )
    summed, route_sum = (
        lax.psum_scatter(partial_value, "loc", scatter_dimension=0, tiled=True),
        lax.psum_scatter(route_rows, "loc", scatter_dimension=0, tiled=True),
    )
    group_part = summed.astype(jnp.bfloat16).reshape(group_total, group_cap, model_width)
    route_part = route_sum.astype(jnp.bfloat16).reshape(group_total, group_cap, TOP)
    back_terms, back_route = (
        lax.all_to_all(group_part, "grp", split_axis=0, concat_axis=0, tiled=True),
        lax.all_to_all(route_part, "grp", split_axis=0, concat_axis=0, tiled=True),
    )
    slot_pad = jnp.concatenate([slot_of, jnp.full((token_total, 1), group_cap, jnp.int32)], axis=1)
    found = jnp.take_along_axis(slot_pad, listed, axis=1)
    position = jnp.where(found < group_cap, listed * group_cap + found, row_total)
    pieces = take_rows(back_terms.reshape(row_total, model_width), position, 0)
    grad_tokens = jnp.sum(pieces.astype(jnp.float32), axis=1).astype(jnp.bfloat16)
    slot_found = jnp.take_along_axis(slot_of, group_ids, axis=1)
    route_index = (group_ids * group_cap + slot_found) * TOP + slot_range
    grad_weights = back_route.reshape(row_total * TOP)[route_index]
    return (grad_tokens, grad_weights)


LANES = 128
NT = (((1,), (1,)), ((), ()))
ANYWHERE = pl.BlockSpec(memory_space=pl.ANY)
IN_VMEM = pl.BlockSpec(memory_space=pltpu.VMEM)
IN_SMEM = pl.BlockSpec(memory_space=pltpu.SMEM)
MIB = 1024 * 1024


def pack_kernel(tokens, cotangent, ids, weights, *outs):
    rows, width = tokens.shape
    lane = lax.broadcasted_iota(jnp.int32, (rows, LANES), 1)
    table = jnp.zeros((rows, LANES), jnp.float32)
    for k in range(ids.shape[1]):
        table += jnp.where(lane == ids[:, k : k + 1], weights[:, k : k + 1].astype(jnp.float32), 0.0)
    table = table.astype(jnp.bfloat16)
    cut = rows // len(outs)
    for i, out in enumerate(outs):
        part = slice(i * cut, (i + 1) * cut)
        out[:, :width] = tokens[part, :]
        out[:, width : 2 * width] = cotangent[part, :]
        out[:, 2 * width :] = table[part, :]


def pack(tokens, cotangent, ids, weights):
    rows, width = tokens.shape
    shape = jax.ShapeDtypeStruct((rows // 2, 2 * width + LANES), jnp.bfloat16)
    return pl.pallas_call(
        pack_kernel,
        out_shape=(shape, shape),
        in_specs=[IN_VMEM] * 4,
        out_specs=(IN_VMEM, IN_VMEM),
        compiler_params=pltpu.CompilerParams(vmem_limit_bytes=12 * MIB),
    )(tokens, cotangent, ids, weights)


def experts_kernel(pieces, per_device, place, *refs):
    packed = refs[:pieces]
    gate_own, up_own, down_own, gate_other, up_other, down_other = refs[pieces : pieces + 6]
    outs = refs[pieces + 6 : 2 * pieces + 6]
    gate_up, down, total, sems = refs[2 * pieces + 6 :]
    expert_total = 2 * per_device
    hidden, width = down.shape[1] // per_device, down.shape[2]
    copies = []
    for e in range(expert_total):
        mine = (gate_own, up_own, down_own) if e < per_device else (gate_other, up_other, down_other)
        pair, at = e // per_device, e % per_device
        copies.append(
            (
                pltpu.make_async_copy(mine[0].at[at], gate_up.at[e, :, pl.ds(0, hidden)], sems.at[0, e]),
                pltpu.make_async_copy(mine[1].at[at], gate_up.at[e, :, pl.ds(hidden, hidden)], sems.at[1, e]),
                pltpu.make_async_copy(mine[2].at[at], down.at[pair, pl.ds(at * hidden, hidden), :], sems.at[2, e]),
            )
        )
    for pair in range(2):
        mine = copies[pair * per_device : (pair + 1) * per_device]
        for kind in (2, 0, 1):
            for copy in mine:
                copy[kind].start()
    x = jnp.concatenate([a[:, :width] for a in packed], axis=0)
    g = jnp.concatenate([a[:, width : 2 * width] for a in packed], axis=0)
    table = jnp.concatenate([a[:, 2 * width :] for a in packed], axis=0).astype(jnp.float32)
    lane = lax.broadcasted_iota(jnp.int32, table.shape, 1)
    route = jnp.zeros(table.shape, jnp.float32)
    for pair in range(2):
        for e in range(pair * per_device, (pair + 1) * per_device):
            copies[e][2].wait()
        backs = lax.dot_general(g, down[pair], NT, preferred_element_type=jnp.float32)
        for e in range(pair * per_device, (pair + 1) * per_device):
            copies[e][0].wait()
            copies[e][1].wait()
            at = e % per_device
            back = backs[:, at * hidden : (at + 1) * hidden]
            column = place[0] + lax.rem(place[1] + e, expert_total)
            weight = jnp.sum(jnp.where(lane == column, table, 0.0), axis=1, keepdims=True)
            both = jnp.dot(x, gate_up[e], preferred_element_type=jnp.float32)
            gate_act, up_act = both[:, :hidden], both[:, hidden:]
            sig = jax.nn.sigmoid(gate_act)
            silu = gate_act * sig
            back_up = back * up_act
            route_grad = jnp.sum(back_up * silu, axis=1, keepdims=True)
            gate_grad = (weight * back_up * sig * (1.0 + gate_act * (1.0 - sig))).astype(jnp.bfloat16)
            up_grad = (weight * back * silu).astype(jnp.bfloat16)
            grads = jnp.concatenate([gate_grad, up_grad], axis=1)
            term = lax.dot_general(grads, gate_up[e], NT, preferred_element_type=jnp.float32)
            if e == 0:
                total[...] = term
            else:
                total[...] += term
            route += jnp.where(lane == column, route_grad, 0.0)
    start = 0
    for out in outs:
        rows = out.shape[0]
        out[:, :width] = total[start : start + rows, :].astype(out.dtype)
        out[:, width:] = route[start : start + rows, :].astype(out.dtype)
        start += rows


def experts_call(place, packed, own, other):
    rows = sum(a.shape[0] for a in packed)
    per_device, width, hidden = own[0].shape
    return pl.pallas_call(
        functools.partial(experts_kernel, len(packed), per_device),
        out_shape=[jax.ShapeDtypeStruct((a.shape[0], width + LANES), jnp.bfloat16) for a in packed],
        in_specs=[IN_SMEM] + [IN_VMEM] * len(packed) + [ANYWHERE] * 6,
        out_specs=[IN_VMEM] * len(packed),
        scratch_shapes=[
            pltpu.VMEM((2 * per_device, width, 2 * hidden), jnp.bfloat16),
            pltpu.VMEM((2, per_device * hidden, width), jnp.bfloat16),
            pltpu.VMEM((rows, width), jnp.float32),
            pltpu.SemaphoreType.DMA((3, 2 * per_device)),
        ],
        compiler_params=pltpu.CompilerParams(vmem_limit_bytes=36 * MIB),
        cost_estimate=pl.CostEstimate(
            flops=2 * per_device * max(rows, 200) * 10 * width * hidden,
            bytes_accessed=2 * per_device * 6 * width * hidden,
            transcendentals=2 * per_device * rows * hidden,
        ),
    )(place, *packed, *own, *other)


def finish_kernel(ids, top0, top1, top2, low0, low1, low2, grad_tokens, grad_weights):
    rows, width = grad_tokens.shape
    cut = rows // 2
    lane = lax.broadcasted_iota(jnp.int32, (cut, LANES), 1)
    for start, terms in ((0, (top0, top1, top2)), (cut, (low0, low1, low2))):
        part = slice(start, start + cut)
        summed = sum(t[...].astype(jnp.float32) for t in terms)
        grad_tokens[part, :] = summed[:, :width].astype(grad_tokens.dtype)
        route = summed[:, width:]
        found = [
            jnp.sum(jnp.where(lane == ids[part, k : k + 1], route, 0.0), axis=1, keepdims=True)
            for k in range(ids.shape[1])
        ]
        grad_weights[part, :] = jnp.concatenate(found, axis=1).astype(grad_weights.dtype)


def finish(ids, terms, width):
    rows, top = ids.shape
    return pl.pallas_call(
        finish_kernel,
        out_shape=(
            jax.ShapeDtypeStruct((rows, width), jnp.bfloat16),
            jax.ShapeDtypeStruct((rows, top), jnp.bfloat16),
        ),
        in_specs=[IN_VMEM] * 7,
        out_specs=(IN_VMEM, IN_VMEM),
        compiler_params=pltpu.CompilerParams(vmem_limit_bytes=12 * MIB),
    )(ids, *terms)


def added(a, b):
    return (a.astype(jnp.float32) + b.astype(jnp.float32)).astype(jnp.bfloat16)


def after(a, *others):
    return lax.optimization_barrier((a,) + others)[0]


def ring_body(tokens, cotangent, expert_ids, route_weights, gate_weight, up_weight, down_weight):
    ring_total = lax.axis_size("grp")
    loc_total = lax.axis_size("loc")
    width = tokens.shape[1]
    per_device = gate_weight.shape[0]
    order = list(range(0, ring_total, 2)) + list(range(ring_total - 1, 0, -2))
    ahead = [(order[i], order[(i + 1) % ring_total]) for i in range(ring_total)]
    behind = [(b, a) for a, b in ahead]
    rank, loc = lax.axis_index("grp"), lax.axis_index("loc")

    def send(pair):
        return lax.ppermute(pair[0], "grp", ahead), lax.ppermute(pair[1], "grp", behind)

    def send_back(pair):
        return lax.ppermute(pair[0], "grp", behind), lax.ppermute(pair[1], "grp", ahead)

    def tie(pair, *others):
        return lax.optimization_barrier((pair[0], pair[1]) + others)[:2]

    own = (gate_weight, up_weight, down_weight)
    swap = [(i, loc_total - 1 - i) for i in range(loc_total)]
    other = tuple(lax.ppermute(a, "loc", swap) for a in own)
    place = jnp.stack([rank * (loc_total * per_device), loc * per_device]).astype(jnp.int32)

    def call(packed, *others):
        return experts_call(after(place, *others) if others else place, packed, own, other)

    top, low = pack(tokens, cotangent, expert_ids, route_weights)
    half = ring_total // 2
    long, short = send((top, low)), send((low, top))
    mine = call([top, low])
    last = mine[0]
    long_terms, short_terms = [None], [None]
    for s in range(1, half):
        long_next = send(tie(long, last) if s > 1 else long)
        if s + 1 < half:
            short_next = send(tie(short, last))
        part = call([long[0], short[0], long[1], short[1]], last)
        long_terms.append((part[0], part[2]))
        short_terms.append((part[1], part[3]))
        last = part[0]
        long, short = long_next, short_next
    short_back = send_back(short_terms[half - 1])
    part = call([long[0], long[1]], last)
    long_back = send_back((part[0], part[1]))
    for s in range(half - 1, 0, -1):
        if s < half - 1:
            short_back = send_back(tuple(added(a, b) for a, b in zip(short_terms[s], short_back)))
        long_back = send_back(tuple(added(a, b) for a, b in zip(long_terms[s], long_back)))
    terms = (mine[0], long_back[0], short_back[1], mine[1], short_back[0], long_back[1])
    return finish(expert_ids, terms, width)


def body(tokens, cotangent, expert_ids, route_weights, gate_weight, up_weight, down_weight):
    args = (tokens, cotangent, expert_ids, route_weights, gate_weight, up_weight, down_weight)
    ring_total, loc_total = lax.axis_size("grp"), lax.axis_size("loc")
    experts = ring_total * loc_total * gate_weight.shape[0]
    if loc_total == 2 and ring_total % 2 == 0 and 4 <= ring_total <= 8 and experts <= LANES and tokens.shape[0] % 32 == 0:
        return ring_body(*args)
    return routed_body(*args)


def solution(mesh):
    placed = (
        P(("rep", "grp", "loc"), None),
        P(("rep", "grp", "loc"), None),
        P(("rep", "grp", "loc"), None),
        P(("rep", "grp", "loc"), None),
        P(("grp", "loc"), None, None),
        P(("grp", "loc"), None, None),
        P(("grp", "loc"), None, None),
    )
    return jax.shard_map(
        body,
        mesh=mesh,
        in_specs=placed,
        out_specs=(P(("rep", "grp", "loc"), None), P(("rep", "grp", "loc"), None)),
        check_vma=False,
    )
```

```python
import functools

import jax
import jax.numpy as jnp
from jax import lax
from jax.experimental import pallas as pl
from jax.experimental.pallas import tpu as pltpu
from jax.sharding import PartitionSpec as P

TOP = 8
TOP_GROUPS = 4


def shortened(shard):
    return jax.tree.map(lambda a: a.astype(jnp.bfloat16) if a.dtype == jnp.float32 else a, shard)


def take_rows(values, indices, filler):
    return jnp.take(values, indices, axis=0, mode="fill", fill_value=filler)


def route_table(targets, dest_total, capacity):
    token_total = targets.shape[0]
    dest_iota = jnp.arange(dest_total, dtype=jnp.int32)
    reached = jnp.any(targets[:, :, None] == dest_iota[None, None, :], axis=1)
    ranked = jnp.cumsum(reached.astype(jnp.int32), axis=0) - 1
    slot_of = jnp.where(reached, ranked, capacity)
    dest_grid = jnp.broadcast_to(dest_iota[None, :], slot_of.shape)
    token_grid = jnp.broadcast_to(jnp.arange(token_total, dtype=jnp.int32)[:, None], slot_of.shape)
    sources = jnp.full((dest_total, capacity), token_total, jnp.int32)
    sources = sources.at[dest_grid, slot_of].set(token_grid, mode="drop")
    return (slot_of, sources)


def token_groups(group_ids, group_total):
    token_total = group_ids.shape[0]
    group_iota = jnp.arange(group_total, dtype=jnp.int32)
    reached = jnp.any(group_ids[:, :, None] == group_iota[None, None, :], axis=1)
    ranked = jnp.cumsum(reached.astype(jnp.int32), axis=1) - 1
    column = jnp.where(reached, ranked, TOP_GROUPS)
    token_grid = jnp.broadcast_to(jnp.arange(token_total, dtype=jnp.int32)[:, None], column.shape)
    listed = jnp.full((token_total, TOP_GROUPS), group_total, jnp.int32)
    return listed.at[token_grid, column].set(
        jnp.broadcast_to(group_iota[None, :], column.shape), mode="drop"
    )


def expert_pass(
    token_rows,
    grad_rows,
    id_rows,
    weight_rows,
    gate_weight,
    up_weight,
    down_weight,
    first_expert,
    capacity,
):
    row_total = token_rows.shape[0]
    local_total = gate_weight.shape[0]
    model_width = token_rows.shape[1]
    experts_here = first_expert + jnp.arange(local_total, dtype=jnp.int32)
    matched = id_rows[None, :, :] == experts_here[:, None, None]
    chosen = jnp.any(matched, axis=2)
    weight_of = jnp.sum(
        jnp.where(matched, weight_rows.astype(jnp.float32)[None, :, :], 0.0), axis=2
    )
    ranked = jnp.cumsum(chosen.astype(jnp.int32), axis=1) - 1
    slot_of = jnp.where(chosen, ranked, capacity)
    expert_grid = jnp.broadcast_to(jnp.arange(local_total, dtype=jnp.int32)[:, None], slot_of.shape)
    row_grid = jnp.broadcast_to(jnp.arange(row_total, dtype=jnp.int32)[None, :], slot_of.shape)
    picks = (
        jnp.full((local_total, capacity), row_total, jnp.int32)
        .at[expert_grid, slot_of]
        .set(row_grid, mode="drop")
    )
    buffer_x = take_rows(token_rows, picks, 0)
    buffer_g = take_rows(grad_rows, picks, 0)
    buffer_w = jnp.take_along_axis(weight_of, picks, axis=1, mode="fill", fill_value=0.0)
    gate_act = jnp.einsum("ecd,edf->ecf", buffer_x, gate_weight, preferred_element_type=jnp.float32)
    up_act = jnp.einsum("ecd,edf->ecf", buffer_x, up_weight, preferred_element_type=jnp.float32)
    back_grad = jnp.einsum(
        "ecd,efd->ecf", buffer_g, down_weight, preferred_element_type=jnp.float32
    )
    sigmoid_val = jax.nn.sigmoid(gate_act)
    silu_val = gate_act * sigmoid_val
    route_grad = jnp.sum(back_grad * silu_val * up_act, axis=2)
    hidden_grad = buffer_w[:, :, None] * back_grad
    gate_grad = (
        hidden_grad * up_act * sigmoid_val * (1.0 + gate_act * (1.0 - sigmoid_val))
    ).astype(jnp.bfloat16)
    up_grad = (hidden_grad * silu_val).astype(jnp.bfloat16)
    input_grad = jnp.einsum(
        "ecf,edf->ecd", gate_grad, gate_weight, preferred_element_type=jnp.float32
    )
    input_grad = input_grad + jnp.einsum(
        "ecf,edf->ecd", up_grad, up_weight, preferred_element_type=jnp.float32
    )
    partial_value = jnp.zeros((row_total, model_width), jnp.float32)
    partial_value = partial_value.at[picks.reshape(-1)].add(
        input_grad.reshape(-1, model_width), mode="drop"
    )
    cap_grid = jnp.broadcast_to(jnp.arange(local_total, dtype=jnp.int32)[:, None], picks.shape)
    route_per = (
        jnp.zeros((local_total, row_total), jnp.float32)
        .at[cap_grid, picks]
        .add(route_grad, mode="drop")
    )
    route_rows = jnp.sum(jnp.where(matched, route_per[:, :, None], 0.0), axis=0)
    return (partial_value, route_rows)


def routed_body(tokens, cotangent, expert_ids, route_weights, gate_weight, up_weight, down_weight):
    group_total = lax.axis_size("grp")
    loc_total = lax.axis_size("loc")
    token_total = tokens.shape[0]
    model_width = tokens.shape[1]
    per_device = gate_weight.shape[0]
    per_group = per_device * loc_total
    group_cap = 6 * token_total // group_total
    expert_cap = 3 * token_total * loc_total
    device_rank = lax.axis_index("grp") * loc_total + lax.axis_index("loc")
    first_expert = device_rank * per_device
    group_ids = expert_ids // per_group
    listed = token_groups(group_ids, group_total)
    slot_range = jnp.arange(TOP, dtype=jnp.int32)[None, :]
    slot_of, sources = route_table(group_ids, group_total, group_cap)
    send_x = take_rows(tokens, sources, 0)
    send_g = take_rows(cotangent, sources, 0)
    send_ids = take_rows(expert_ids, sources, -1)
    send_w = take_rows(route_weights, sources, 0)
    recv_x, recv_g, recv_ids, recv_w = (
        lax.all_to_all(send_x, "grp", split_axis=0, concat_axis=0, tiled=True),
        lax.all_to_all(send_g, "grp", split_axis=0, concat_axis=0, tiled=True),
        lax.all_to_all(send_ids, "grp", split_axis=0, concat_axis=0, tiled=True),
        lax.all_to_all(send_w, "grp", split_axis=0, concat_axis=0, tiled=True),
    )
    row_total = group_total * group_cap
    shared_x, shared_g, shared_ids, shared_w = (
        lax.all_gather(recv_x.reshape(row_total, model_width), "loc", axis=0, tiled=True),
        lax.all_gather(recv_g.reshape(row_total, model_width), "loc", axis=0, tiled=True),
        lax.all_gather(shortened(recv_ids.reshape(row_total, TOP)), "loc", axis=0, tiled=True),
        lax.all_gather(recv_w.reshape(row_total, TOP), "loc", axis=0, tiled=True),
    )
    partial_value, route_rows = expert_pass(
        shared_x,
        shared_g,
        shared_ids,
        shared_w,
        gate_weight,
        up_weight,
        down_weight,
        first_expert,
        expert_cap,
    )
    summed, route_sum = (
        lax.psum_scatter(partial_value, "loc", scatter_dimension=0, tiled=True),
        lax.psum_scatter(route_rows, "loc", scatter_dimension=0, tiled=True),
    )
    group_part = summed.astype(jnp.bfloat16).reshape(group_total, group_cap, model_width)
    route_part = route_sum.astype(jnp.bfloat16).reshape(group_total, group_cap, TOP)
    back_terms, back_route = (
        lax.all_to_all(group_part, "grp", split_axis=0, concat_axis=0, tiled=True),
        lax.all_to_all(route_part, "grp", split_axis=0, concat_axis=0, tiled=True),
    )
    slot_pad = jnp.concatenate([slot_of, jnp.full((token_total, 1), group_cap, jnp.int32)], axis=1)
    found = jnp.take_along_axis(slot_pad, listed, axis=1)
    position = jnp.where(found < group_cap, listed * group_cap + found, row_total)
    pieces = take_rows(back_terms.reshape(row_total, model_width), position, 0)
    grad_tokens = jnp.sum(pieces.astype(jnp.float32), axis=1).astype(jnp.bfloat16)
    slot_found = jnp.take_along_axis(slot_of, group_ids, axis=1)
    route_index = (group_ids * group_cap + slot_found) * TOP + slot_range
    grad_weights = back_route.reshape(row_total * TOP)[route_index]
    return (grad_tokens, grad_weights)


LANES = 128
NT = (((1,), (1,)), ((), ()))
ANYWHERE = pl.BlockSpec(memory_space=pl.ANY)
IN_VMEM = pl.BlockSpec(memory_space=pltpu.VMEM)
IN_SMEM = pl.BlockSpec(memory_space=pltpu.SMEM)
MIB = 1024 * 1024
TOKEN = jax.ShapeDtypeStruct((8, LANES), jnp.float32)


def pack_kernel(tokens, cotangent, ids, weights, block, ids_here, weights_here, sems):
    rows, width = tokens.shape
    small = (
        pltpu.make_async_copy(ids, ids_here, sems.at[0]),
        pltpu.make_async_copy(weights, weights_here, sems.at[1]),
    )
    large = (
        pltpu.make_async_copy(tokens, block.at[:, pl.ds(0, width)], sems.at[2]),
        pltpu.make_async_copy(cotangent, block.at[:, pl.ds(width, width)], sems.at[3]),
    )
    for copy in small + large:
        copy.start()
    for copy in small:
        copy.wait()
    expert = lax.broadcasted_iota(jnp.int32, (LANES, rows), 0)
    table = jnp.zeros((LANES, rows), jnp.float32)
    for k in range(ids.shape[0]):
        chosen = expert == ids_here[k : k + 1, :]
        table += jnp.where(chosen, weights_here[k : k + 1, :].astype(jnp.float32), 0.0)
    block[:, 2 * width :] = table.T.astype(jnp.bfloat16)
    for copy in large:
        copy.wait()


def pack(tokens, cotangent, ids, weights):
    rows, width = tokens.shape
    return pl.pallas_call(
        pack_kernel,
        out_shape=pltpu.VMEM((rows, 2 * width + LANES), jnp.bfloat16),
        in_specs=[ANYWHERE] * 4,
        out_specs=IN_VMEM,
        scratch_shapes=[
            pltpu.VMEM((ids.shape[1], rows), jnp.int32),
            pltpu.VMEM((ids.shape[1], rows), jnp.bfloat16),
            pltpu.SemaphoreType.DMA((4,)),
        ],
        compiler_params=pltpu.CompilerParams(vmem_limit_bytes=8 * MIB),
    )(*(in_hbm(a) for a in (tokens, cotangent, ids.T, weights.T)))


def in_hbm(a):
    return pltpu.with_memory_space_constraint(a, pltpu.HBM)


def in_vmem(a):
    return pltpu.with_memory_space_constraint(a, pltpu.VMEM)


def load_kernel(after_this, gate, up, down, gate_up, back, down_back, token, down_here, sems):
    del after_this
    token[...] = jnp.zeros_like(token)
    per_device, hidden = gate.shape[0], gate.shape[2]
    copies = []
    for e in range(per_device):
        copies.append(
            (
                pltpu.make_async_copy(down.at[e], down_here.at[e], sems.at[2, e]),
                pltpu.make_async_copy(gate.at[e], gate_up.at[e, :, pl.ds(0, hidden)], sems.at[0, e]),
                pltpu.make_async_copy(up.at[e], gate_up.at[e, :, pl.ds(hidden, hidden)], sems.at[1, e]),
            )
        )
    for three in copies:
        for copy in three:
            copy.start()
    for e, (first, second, third) in enumerate(copies):
        first.wait()
        down_back[:, e * hidden : (e + 1) * hidden] = down_here[e].T
        second.wait()
        third.wait()
        back[2 * e * hidden : 2 * (e + 1) * hidden, :] = gate_up[e].T


def load(after_this, gate, up, down):
    per_device, width, hidden = gate.shape
    return pl.pallas_call(
        load_kernel,
        out_shape=(
            pltpu.VMEM((per_device, width, 2 * hidden), jnp.bfloat16),
            pltpu.VMEM((2 * per_device * hidden, width), jnp.bfloat16),
            pltpu.VMEM((width, per_device * hidden), jnp.bfloat16),
            TOKEN,
        ),
        in_specs=[ANYWHERE] * 4,
        out_specs=(IN_VMEM,) * 4,
        scratch_shapes=[pltpu.VMEM(down.shape, jnp.bfloat16), pltpu.SemaphoreType.DMA((3, per_device))],
        compiler_params=pltpu.CompilerParams(vmem_limit_bytes=8 * MIB),
        cost_estimate=pl.CostEstimate(flops=1, bytes_accessed=24 * MIB, transcendentals=0),
    )(after_this, gate, up, down)


def experts_kernel(pieces, place, after_this, *refs):
    del after_this
    packed, refs = refs[:pieces], refs[pieces:]
    loaded, refs = (refs[:3], refs[3:6]), refs[6:]
    outs, token = refs[:pieces], refs[pieces]
    token[...] = jnp.zeros_like(token)
    per_device, width, both_hidden = loaded[0][0].shape
    hidden = both_hidden // 2
    x = jnp.concatenate([a[:, :width] for a in packed], axis=0)
    g = jnp.concatenate([a[:, width : 2 * width] for a in packed], axis=0)
    table = jnp.concatenate([a[:, 2 * width :] for a in packed], axis=0).astype(jnp.float32)
    lane = lax.broadcasted_iota(jnp.int32, table.shape, 1)
    route = jnp.zeros(table.shape, jnp.float32)
    grads = []
    for pair, (gate_up, _, down_back) in enumerate(loaded):
        backs = jnp.dot(g, down_back[...], preferred_element_type=jnp.float32)
        mine = []
        for at in range(per_device):
            back = backs[:, at * hidden : (at + 1) * hidden]
            column = place[0] + lax.rem(place[1] + pair * per_device + at, 2 * per_device)
            weight = jnp.sum(jnp.where(lane == column, table, 0.0), axis=1, keepdims=True)
            both = jnp.dot(x, gate_up[at], preferred_element_type=jnp.float32)
            gate_act, up_act = both[:, :hidden], both[:, hidden:]
            sig = jax.nn.sigmoid(gate_act)
            silu = gate_act * sig
            back_up = back * up_act
            route_grad = jnp.sum(back_up * silu, axis=1, keepdims=True)
            mine.append((weight * back_up * sig * (1.0 + gate_act * (1.0 - sig))).astype(jnp.bfloat16))
            mine.append((weight * back * silu).astype(jnp.bfloat16))
            route += jnp.where(lane == column, route_grad, 0.0)
        grads.append(jnp.concatenate(mine, axis=1))
    step = 4 * LANES
    for lanes in range(0, width, step):
        part = slice(lanes, lanes + step)
        total = sum(
            jnp.dot(a, back[:, part], preferred_element_type=jnp.float32) for a, (_, back, _) in zip(grads, loaded)
        ).astype(jnp.bfloat16)
        start = 0
        for out in outs:
            out[:, part] = total[start : start + out.shape[0]]
            start += out.shape[0]
    start = 0
    for out in outs:
        out[:, width:] = route[start : start + out.shape[0]].astype(out.dtype)
        start += out.shape[0]


def experts_call(place, after_this, packed, loaded):
    width = loaded[0].shape[1]
    return pl.pallas_call(
        functools.partial(experts_kernel, len(packed)),
        out_shape=[jax.ShapeDtypeStruct((a.shape[0], width + LANES), jnp.bfloat16) for a in packed] + [TOKEN],
        in_specs=[IN_SMEM, ANYWHERE] + [IN_VMEM] * (len(packed) + 6),
        out_specs=[IN_VMEM] * (len(packed) + 1),
        compiler_params=pltpu.CompilerParams(vmem_limit_bytes=12 * MIB),
        cost_estimate=pl.CostEstimate(flops=1, bytes_accessed=1, transcendentals=0),
    )(place, after_this, *(in_vmem(a) for a in packed), *loaded)


def finish_kernel(ids, mine, top0, top1, low0, low1, grad_tokens, grad_weights):
    rows, width = grad_tokens.shape
    cut = rows // 2
    routes = []
    for start, terms in ((0, (top0, top1)), (cut, (low0, low1))):
        summed = mine[start : start + cut, :].astype(jnp.float32)
        for term in terms:
            summed += term[...].astype(jnp.float32)
        grad_tokens[start : start + cut, :] = summed[:, :width].astype(grad_tokens.dtype)
        routes.append(summed[:, width:])
    route = jnp.concatenate(routes, axis=0).T
    expert = lax.broadcasted_iota(jnp.int32, route.shape, 0)
    found = [
        jnp.sum(jnp.where(expert == ids[k : k + 1, :], route, 0.0), axis=0, keepdims=True) for k in range(ids.shape[0])
    ]
    grad_weights[...] = jnp.concatenate(found, axis=0).astype(grad_weights.dtype)


def finish(ids, terms, width):
    rows, top = ids.shape
    grad_tokens, grad_weights = pl.pallas_call(
        finish_kernel,
        out_shape=(
            jax.ShapeDtypeStruct((rows, width), jnp.bfloat16),
            jax.ShapeDtypeStruct((top, rows), jnp.bfloat16),
        ),
        in_specs=[IN_VMEM] * 6,
        out_specs=(IN_VMEM, IN_VMEM),
        compiler_params=pltpu.CompilerParams(vmem_limit_bytes=12 * MIB),
    )(ids.T, *terms)
    return grad_tokens, grad_weights.T


def add_kernel(a, b, c, d, ab, cd):
    ab[...] = (a[...].astype(jnp.float32) + b[...].astype(jnp.float32)).astype(ab.dtype)
    cd[...] = (c[...].astype(jnp.float32) + d[...].astype(jnp.float32)).astype(cd.dtype)


def added(pair, came):
    a, c = pair
    b, d = came
    return pl.pallas_call(
        add_kernel,
        out_shape=(jax.ShapeDtypeStruct(a.shape, a.dtype), jax.ShapeDtypeStruct(c.shape, c.dtype)),
        in_specs=[IN_VMEM] * 4,
        out_specs=(IN_VMEM, IN_VMEM),
        compiler_params=pltpu.CompilerParams(vmem_limit_bytes=8 * MIB),
        cost_estimate=pl.CostEstimate(flops=1, bytes_accessed=1, transcendentals=0),
    )(a, b, c, d)


def ring_body(tokens, cotangent, expert_ids, route_weights, gate_weight, up_weight, down_weight):
    ring_total = lax.axis_size("grp")
    loc_total = lax.axis_size("loc")
    width = tokens.shape[1]
    per_device = gate_weight.shape[0]
    order = list(range(0, ring_total, 2)) + list(range(ring_total - 1, 0, -2))
    ahead = [(order[i], order[(i + 1) % ring_total]) for i in range(ring_total)]
    behind = [(b, a) for a, b in ahead]
    rank, loc = lax.axis_index("grp"), lax.axis_index("loc")

    def send(pair):
        return lax.ppermute(pair[0], "grp", ahead), lax.ppermute(pair[1], "grp", behind)

    def send_back(pair):
        return lax.ppermute(pair[0], "grp", behind), lax.ppermute(pair[1], "grp", ahead)

    def tie(pair, *others):
        return lax.optimization_barrier((pair[0], pair[1]) + others)[:2]

    own = (gate_weight, up_weight, down_weight)
    other = [lax.ppermute(a, "loc", [(i, loc_total - 1 - i) for i in range(loc_total)]) for a in own]
    block = pack(tokens, cotangent, expert_ids, route_weights)
    came = send((block, block))
    place = jnp.stack([rank * (loc_total * per_device), loc * per_device]).astype(jnp.int32)
    *loaded, loaded_own = load(place, *(in_hbm(a) for a in own))
    *others, last = load(loaded_own, *tie(other[:2], *came), other[2])
    loaded += others

    def call(after_this, *packed):
        *parts, token = experts_call(place, after_this, packed, loaded)
        return parts, token

    half, cut = ring_total // 2, block.shape[0] // 2

    def split(pair):
        return (pair[0][:cut], pair[1][cut:]), (pair[0][cut:], pair[1][:cut])

    long, short = split(came)
    long_next, short_next = send(tie(long, loaded_own, *other)), send(tie(short, loaded_own, *other))
    (mine,), last = call(last, block)
    parts, last = call(last, *came)
    ahead_terms, behind_terms = split(parts)
    long_terms, short_terms = [None, ahead_terms], [None, behind_terms]
    for s in range(2, half - 1):
        long, short = long_next, short_next
        long_next = send(long)
        short_next = send(tie(short, last))
        parts, last = call(last, long[0], short[0], long[1], short[1])
        long_terms.append((parts[0], parts[2]))
        short_terms.append((parts[1], parts[3]))
    long, short = long_next, short_next
    long_last = send(tie(long, last))
    parts, last = call(last, *long)
    long_terms.append(tuple(parts))
    parts, last = call(last, *short)
    short_back = send_back(parts)
    parts, last = call(last, *long_last)
    long_back = send_back(tie(parts, *short_back))
    for s in range(half - 1, 0, -1):
        if s < half - 1:
            short_back = send_back(added(short_terms[s], short_back))
        long_back = send_back(added(long_terms[s], long_back))
    return finish(expert_ids, (mine, long_back[0], short_back[1], short_back[0], long_back[1]), width)


def body(tokens, cotangent, expert_ids, route_weights, gate_weight, up_weight, down_weight):
    args = (tokens, cotangent, expert_ids, route_weights, gate_weight, up_weight, down_weight)
    ring_total, loc_total = lax.axis_size("grp"), lax.axis_size("loc")
    experts = ring_total * loc_total * gate_weight.shape[0]
    if loc_total == 2 and ring_total in (6, 8) and experts <= LANES and tokens.shape[0] % 32 == 0:
        return ring_body(*args)
    return routed_body(*args)


def solution(mesh):
    placed = (
        P(("rep", "grp", "loc"), None),
        P(("rep", "grp", "loc"), None),
        P(("rep", "grp", "loc"), None),
        P(("rep", "grp", "loc"), None),
        P(("grp", "loc"), None, None),
        P(("grp", "loc"), None, None),
        P(("grp", "loc"), None, None),
    )
    return jax.shard_map(
        body,
        mesh=mesh,
        in_specs=placed,
        out_specs=(P(("rep", "grp", "loc"), None), P(("rep", "grp", "loc"), None)),
        check_vma=False,
    )
```

```python
import functools

import jax
import jax.numpy as jnp
from jax import lax
from jax.experimental import pallas as pl
from jax.experimental.pallas import tpu as pltpu
from jax.sharding import PartitionSpec as P

TOP = 8
TOP_GROUPS = 4


def shortened(shard):
    return jax.tree.map(lambda a: a.astype(jnp.bfloat16) if a.dtype == jnp.float32 else a, shard)


def take_rows(values, indices, filler):
    return jnp.take(values, indices, axis=0, mode="fill", fill_value=filler)


def route_table(targets, dest_total, capacity):
    token_total = targets.shape[0]
    dest_iota = jnp.arange(dest_total, dtype=jnp.int32)
    reached = jnp.any(targets[:, :, None] == dest_iota[None, None, :], axis=1)
    ranked = jnp.cumsum(reached.astype(jnp.int32), axis=0) - 1
    slot_of = jnp.where(reached, ranked, capacity)
    dest_grid = jnp.broadcast_to(dest_iota[None, :], slot_of.shape)
    token_grid = jnp.broadcast_to(jnp.arange(token_total, dtype=jnp.int32)[:, None], slot_of.shape)
    sources = jnp.full((dest_total, capacity), token_total, jnp.int32)
    sources = sources.at[dest_grid, slot_of].set(token_grid, mode="drop")
    return (slot_of, sources)


def token_groups(group_ids, group_total):
    token_total = group_ids.shape[0]
    group_iota = jnp.arange(group_total, dtype=jnp.int32)
    reached = jnp.any(group_ids[:, :, None] == group_iota[None, None, :], axis=1)
    ranked = jnp.cumsum(reached.astype(jnp.int32), axis=1) - 1
    column = jnp.where(reached, ranked, TOP_GROUPS)
    token_grid = jnp.broadcast_to(jnp.arange(token_total, dtype=jnp.int32)[:, None], column.shape)
    listed = jnp.full((token_total, TOP_GROUPS), group_total, jnp.int32)
    return listed.at[token_grid, column].set(
        jnp.broadcast_to(group_iota[None, :], column.shape), mode="drop"
    )


def expert_pass(
    token_rows,
    grad_rows,
    id_rows,
    weight_rows,
    gate_weight,
    up_weight,
    down_weight,
    first_expert,
    capacity,
):
    row_total = token_rows.shape[0]
    local_total = gate_weight.shape[0]
    model_width = token_rows.shape[1]
    experts_here = first_expert + jnp.arange(local_total, dtype=jnp.int32)
    matched = id_rows[None, :, :] == experts_here[:, None, None]
    chosen = jnp.any(matched, axis=2)
    weight_of = jnp.sum(
        jnp.where(matched, weight_rows.astype(jnp.float32)[None, :, :], 0.0), axis=2
    )
    ranked = jnp.cumsum(chosen.astype(jnp.int32), axis=1) - 1
    slot_of = jnp.where(chosen, ranked, capacity)
    expert_grid = jnp.broadcast_to(jnp.arange(local_total, dtype=jnp.int32)[:, None], slot_of.shape)
    row_grid = jnp.broadcast_to(jnp.arange(row_total, dtype=jnp.int32)[None, :], slot_of.shape)
    picks = (
        jnp.full((local_total, capacity), row_total, jnp.int32)
        .at[expert_grid, slot_of]
        .set(row_grid, mode="drop")
    )
    buffer_x = take_rows(token_rows, picks, 0)
    buffer_g = take_rows(grad_rows, picks, 0)
    buffer_w = jnp.take_along_axis(weight_of, picks, axis=1, mode="fill", fill_value=0.0)
    gate_act = jnp.einsum("ecd,edf->ecf", buffer_x, gate_weight, preferred_element_type=jnp.float32)
    up_act = jnp.einsum("ecd,edf->ecf", buffer_x, up_weight, preferred_element_type=jnp.float32)
    back_grad = jnp.einsum(
        "ecd,efd->ecf", buffer_g, down_weight, preferred_element_type=jnp.float32
    )
    sigmoid_val = jax.nn.sigmoid(gate_act)
    silu_val = gate_act * sigmoid_val
    route_grad = jnp.sum(back_grad * silu_val * up_act, axis=2)
    hidden_grad = buffer_w[:, :, None] * back_grad
    gate_grad = (
        hidden_grad * up_act * sigmoid_val * (1.0 + gate_act * (1.0 - sigmoid_val))
    ).astype(jnp.bfloat16)
    up_grad = (hidden_grad * silu_val).astype(jnp.bfloat16)
    input_grad = jnp.einsum(
        "ecf,edf->ecd", gate_grad, gate_weight, preferred_element_type=jnp.float32
    )
    input_grad = input_grad + jnp.einsum(
        "ecf,edf->ecd", up_grad, up_weight, preferred_element_type=jnp.float32
    )
    partial_value = jnp.zeros((row_total, model_width), jnp.float32)
    partial_value = partial_value.at[picks.reshape(-1)].add(
        input_grad.reshape(-1, model_width), mode="drop"
    )
    cap_grid = jnp.broadcast_to(jnp.arange(local_total, dtype=jnp.int32)[:, None], picks.shape)
    route_per = (
        jnp.zeros((local_total, row_total), jnp.float32)
        .at[cap_grid, picks]
        .add(route_grad, mode="drop")
    )
    route_rows = jnp.sum(jnp.where(matched, route_per[:, :, None], 0.0), axis=0)
    return (partial_value, route_rows)


def routed_body(tokens, cotangent, expert_ids, route_weights, gate_weight, up_weight, down_weight):
    group_total = lax.axis_size("grp")
    loc_total = lax.axis_size("loc")
    token_total = tokens.shape[0]
    model_width = tokens.shape[1]
    per_device = gate_weight.shape[0]
    per_group = per_device * loc_total
    group_cap = 6 * token_total // group_total
    expert_cap = 3 * token_total * loc_total
    device_rank = lax.axis_index("grp") * loc_total + lax.axis_index("loc")
    first_expert = device_rank * per_device
    group_ids = expert_ids // per_group
    listed = token_groups(group_ids, group_total)
    slot_range = jnp.arange(TOP, dtype=jnp.int32)[None, :]
    slot_of, sources = route_table(group_ids, group_total, group_cap)
    send_x = take_rows(tokens, sources, 0)
    send_g = take_rows(cotangent, sources, 0)
    send_ids = take_rows(expert_ids, sources, -1)
    send_w = take_rows(route_weights, sources, 0)
    recv_x, recv_g, recv_ids, recv_w = (
        lax.all_to_all(send_x, "grp", split_axis=0, concat_axis=0, tiled=True),
        lax.all_to_all(send_g, "grp", split_axis=0, concat_axis=0, tiled=True),
        lax.all_to_all(send_ids, "grp", split_axis=0, concat_axis=0, tiled=True),
        lax.all_to_all(send_w, "grp", split_axis=0, concat_axis=0, tiled=True),
    )
    row_total = group_total * group_cap
    shared_x, shared_g, shared_ids, shared_w = (
        lax.all_gather(recv_x.reshape(row_total, model_width), "loc", axis=0, tiled=True),
        lax.all_gather(recv_g.reshape(row_total, model_width), "loc", axis=0, tiled=True),
        lax.all_gather(shortened(recv_ids.reshape(row_total, TOP)), "loc", axis=0, tiled=True),
        lax.all_gather(recv_w.reshape(row_total, TOP), "loc", axis=0, tiled=True),
    )
    partial_value, route_rows = expert_pass(
        shared_x,
        shared_g,
        shared_ids,
        shared_w,
        gate_weight,
        up_weight,
        down_weight,
        first_expert,
        expert_cap,
    )
    summed, route_sum = (
        lax.psum_scatter(partial_value, "loc", scatter_dimension=0, tiled=True),
        lax.psum_scatter(route_rows, "loc", scatter_dimension=0, tiled=True),
    )
    group_part = summed.astype(jnp.bfloat16).reshape(group_total, group_cap, model_width)
    route_part = route_sum.astype(jnp.bfloat16).reshape(group_total, group_cap, TOP)
    back_terms, back_route = (
        lax.all_to_all(group_part, "grp", split_axis=0, concat_axis=0, tiled=True),
        lax.all_to_all(route_part, "grp", split_axis=0, concat_axis=0, tiled=True),
    )
    slot_pad = jnp.concatenate([slot_of, jnp.full((token_total, 1), group_cap, jnp.int32)], axis=1)
    found = jnp.take_along_axis(slot_pad, listed, axis=1)
    position = jnp.where(found < group_cap, listed * group_cap + found, row_total)
    pieces = take_rows(back_terms.reshape(row_total, model_width), position, 0)
    grad_tokens = jnp.sum(pieces.astype(jnp.float32), axis=1).astype(jnp.bfloat16)
    slot_found = jnp.take_along_axis(slot_of, group_ids, axis=1)
    route_index = (group_ids * group_cap + slot_found) * TOP + slot_range
    grad_weights = back_route.reshape(row_total * TOP)[route_index]
    return (grad_tokens, grad_weights)


LANES = 128
NT = (((1,), (1,)), ((), ()))
ANYWHERE = pl.BlockSpec(memory_space=pl.ANY)
IN_VMEM = pl.BlockSpec(memory_space=pltpu.VMEM)
IN_SMEM = pl.BlockSpec(memory_space=pltpu.SMEM)
MIB = 1024 * 1024
TOKEN = jax.ShapeDtypeStruct((8, LANES), jnp.float32)


def pack_kernel(tokens, cotangent, ids, weights, block, ids_here, weights_here, sems):
    rows, width = tokens.shape
    small = (
        pltpu.make_async_copy(ids, ids_here, sems.at[0]),
        pltpu.make_async_copy(weights, weights_here, sems.at[1]),
    )
    large = (
        pltpu.make_async_copy(tokens, block.at[:, pl.ds(0, width)], sems.at[2]),
        pltpu.make_async_copy(cotangent, block.at[:, pl.ds(width, width)], sems.at[3]),
    )
    for copy in small + large:
        copy.start()
    for copy in small:
        copy.wait()
    expert = lax.broadcasted_iota(jnp.int32, (LANES, rows), 0)
    table = jnp.zeros((LANES, rows), jnp.float32)
    for k in range(ids.shape[0]):
        chosen = expert == ids_here[k : k + 1, :]
        table += jnp.where(chosen, weights_here[k : k + 1, :].astype(jnp.float32), 0.0)
    block[:, 2 * width :] = table.T.astype(jnp.bfloat16)
    for copy in large:
        copy.wait()


def pack(tokens, cotangent, ids, weights):
    rows, width = tokens.shape
    return pl.pallas_call(
        pack_kernel,
        out_shape=pltpu.VMEM((rows, 2 * width + LANES), jnp.bfloat16),
        in_specs=[ANYWHERE] * 4,
        out_specs=IN_VMEM,
        scratch_shapes=[
            pltpu.VMEM((ids.shape[1], rows), jnp.int32),
            pltpu.VMEM((ids.shape[1], rows), jnp.bfloat16),
            pltpu.SemaphoreType.DMA((4,)),
        ],
        compiler_params=pltpu.CompilerParams(vmem_limit_bytes=8 * MIB),
    )(*(in_hbm(a) for a in (tokens, cotangent, ids.T, weights.T)))


def in_hbm(a):
    return pltpu.with_memory_space_constraint(a, pltpu.HBM)


def in_vmem(a):
    return pltpu.with_memory_space_constraint(a, pltpu.VMEM)


def load_kernel(after_this, gate, up, down, gate_up, back, down_back, token, down_here, sems):
    del after_this
    token[...] = jnp.zeros_like(token)
    per_device, hidden = gate.shape[0], gate.shape[2]
    copies = []
    for e in range(per_device):
        copies.append(
            (
                pltpu.make_async_copy(down.at[e], down_here.at[e], sems.at[2, e]),
                pltpu.make_async_copy(gate.at[e], gate_up.at[e, :, pl.ds(0, hidden)], sems.at[0, e]),
                pltpu.make_async_copy(up.at[e], gate_up.at[e, :, pl.ds(hidden, hidden)], sems.at[1, e]),
            )
        )
    for three in copies:
        for copy in three:
            copy.start()
    for e, (first, second, third) in enumerate(copies):
        first.wait()
        down_back[:, e * hidden : (e + 1) * hidden] = down_here[e].T
        second.wait()
        third.wait()
        back[2 * e * hidden : 2 * (e + 1) * hidden, :] = gate_up[e].T


def load(after_this, gate, up, down):
    per_device, width, hidden = gate.shape
    return pl.pallas_call(
        load_kernel,
        out_shape=(
            pltpu.VMEM((per_device, width, 2 * hidden), jnp.bfloat16),
            pltpu.VMEM((2 * per_device * hidden, width), jnp.bfloat16),
            pltpu.VMEM((width, per_device * hidden), jnp.bfloat16),
            TOKEN,
        ),
        in_specs=[ANYWHERE] * 4,
        out_specs=(IN_VMEM,) * 4,
        scratch_shapes=[pltpu.VMEM(down.shape, jnp.bfloat16), pltpu.SemaphoreType.DMA((3, per_device))],
        compiler_params=pltpu.CompilerParams(vmem_limit_bytes=8 * MIB),
        cost_estimate=pl.CostEstimate(flops=1, bytes_accessed=24 * MIB, transcendentals=0),
    )(after_this, gate, up, down)


def experts_kernel(pieces, place, after_this, *refs):
    del after_this
    packed, refs = refs[:pieces], refs[pieces:]
    loaded, refs = (refs[:3], refs[3:6]), refs[6:]
    outs, token = refs[:pieces], refs[pieces]
    token[...] = jnp.zeros_like(token)
    per_device, width, both_hidden = loaded[0][0].shape
    hidden = both_hidden // 2
    x = jnp.concatenate([a[:, :width] for a in packed], axis=0)
    g = jnp.concatenate([a[:, width : 2 * width] for a in packed], axis=0)
    table = jnp.concatenate([a[:, 2 * width :] for a in packed], axis=0).astype(jnp.float32)
    lane = lax.broadcasted_iota(jnp.int32, table.shape, 1)
    route = jnp.zeros(table.shape, jnp.float32)
    grads = []
    for pair, (gate_up, _, down_back) in enumerate(loaded):
        backs = jnp.dot(g, down_back[...], preferred_element_type=jnp.float32)
        mine = []
        for at in range(per_device):
            back = backs[:, at * hidden : (at + 1) * hidden]
            column = place[0] + lax.rem(place[1] + pair * per_device + at, 2 * per_device)
            weight = jnp.sum(jnp.where(lane == column, table, 0.0), axis=1, keepdims=True)
            both = jnp.dot(x, gate_up[at], preferred_element_type=jnp.float32)
            gate_act, up_act = both[:, :hidden], both[:, hidden:]
            sig = jax.nn.sigmoid(gate_act)
            silu = gate_act * sig
            back_up = back * up_act
            route_grad = jnp.sum(back_up * silu, axis=1, keepdims=True)
            mine.append((weight * back_up * sig * (1.0 + gate_act * (1.0 - sig))).astype(jnp.bfloat16))
            mine.append((weight * back * silu).astype(jnp.bfloat16))
            route += jnp.where(lane == column, route_grad, 0.0)
        grads.append(jnp.concatenate(mine, axis=1))
    step = 4 * LANES
    for lanes in range(0, width, step):
        part = slice(lanes, lanes + step)
        total = sum(
            jnp.dot(a, back[:, part], preferred_element_type=jnp.float32) for a, (_, back, _) in zip(grads, loaded)
        ).astype(jnp.bfloat16)
        start = 0
        for out in outs:
            out[:, part] = total[start : start + out.shape[0]]
            start += out.shape[0]
    start = 0
    for out in outs:
        out[:, width:] = route[start : start + out.shape[0]].astype(out.dtype)
        start += out.shape[0]


def experts_call(place, after_this, packed, loaded):
    width = loaded[0].shape[1]
    return pl.pallas_call(
        functools.partial(experts_kernel, len(packed)),
        out_shape=[jax.ShapeDtypeStruct((a.shape[0], width + LANES), jnp.bfloat16) for a in packed] + [TOKEN],
        in_specs=[IN_SMEM, ANYWHERE] + [IN_VMEM] * (len(packed) + 6),
        out_specs=[IN_VMEM] * (len(packed) + 1),
        compiler_params=pltpu.CompilerParams(vmem_limit_bytes=12 * MIB),
        cost_estimate=pl.CostEstimate(flops=1, bytes_accessed=1, transcendentals=0),
    )(place, after_this, *(in_vmem(a) for a in packed), *loaded)


def finish_kernel(ids, mine, top0, top1, low0, low1, grad_tokens, grad_weights):
    rows, width = grad_tokens.shape
    cut = rows // 2
    routes = []
    for start, terms in ((0, (top0, top1)), (cut, (low0, low1))):
        summed = mine[start : start + cut, :].astype(jnp.float32)
        for term in terms:
            summed += term[...].astype(jnp.float32)
        grad_tokens[start : start + cut, :] = summed[:, :width].astype(grad_tokens.dtype)
        routes.append(summed[:, width:])
    route = jnp.concatenate(routes, axis=0).T
    expert = lax.broadcasted_iota(jnp.int32, route.shape, 0)
    found = [
        jnp.sum(jnp.where(expert == ids[k : k + 1, :], route, 0.0), axis=0, keepdims=True) for k in range(ids.shape[0])
    ]
    grad_weights[...] = jnp.concatenate(found, axis=0).astype(grad_weights.dtype)


def finish(ids, terms, width):
    rows, top = ids.shape
    grad_tokens, grad_weights = pl.pallas_call(
        finish_kernel,
        out_shape=(
            jax.ShapeDtypeStruct((rows, width), jnp.bfloat16),
            jax.ShapeDtypeStruct((top, rows), jnp.bfloat16),
        ),
        in_specs=[IN_VMEM] * 6,
        out_specs=(IN_VMEM, IN_VMEM),
        compiler_params=pltpu.CompilerParams(vmem_limit_bytes=12 * MIB),
    )(ids.T, *terms)
    return grad_tokens, grad_weights.T


def add_kernel(a, b, out):
    out[...] = (a[...].astype(jnp.float32) + b[...].astype(jnp.float32)).astype(out.dtype)


def added(a, b):
    return pl.pallas_call(
        add_kernel,
        out_shape=jax.ShapeDtypeStruct(a.shape, a.dtype),
        in_specs=[IN_VMEM] * 2,
        out_specs=IN_VMEM,
        compiler_params=pltpu.CompilerParams(vmem_limit_bytes=8 * MIB),
        cost_estimate=pl.CostEstimate(flops=1, bytes_accessed=1, transcendentals=0),
    )(a, b)


def ring_body(tokens, cotangent, expert_ids, route_weights, gate_weight, up_weight, down_weight):
    ring_total = lax.axis_size("grp")
    loc_total = lax.axis_size("loc")
    width = tokens.shape[1]
    per_device = gate_weight.shape[0]
    order = list(range(0, ring_total, 2)) + list(range(ring_total - 1, 0, -2))
    ahead = [(order[i], order[(i + 1) % ring_total]) for i in range(ring_total)]
    behind = [(b, a) for a, b in ahead]
    rank, loc = lax.axis_index("grp"), lax.axis_index("loc")

    def send(pair):
        return lax.ppermute(pair[0], "grp", ahead), lax.ppermute(pair[1], "grp", behind)

    def send_back(pair):
        return lax.ppermute(pair[0], "grp", behind), lax.ppermute(pair[1], "grp", ahead)

    def tie(pair, *others):
        return tuple(lax.optimization_barrier((a, *others))[0] for a in pair)

    own = (gate_weight, up_weight, down_weight)
    other = [lax.ppermute(a, "loc", [(i, loc_total - 1 - i) for i in range(loc_total)]) for a in own]
    block = pack(tokens, cotangent, expert_ids, route_weights)
    came = send((block, block))
    place = jnp.stack([rank * (loc_total * per_device), loc * per_device]).astype(jnp.int32)
    *loaded, loaded_own = load(place, *(in_hbm(a) for a in own))
    *others, last = load(loaded_own, *tie(other[:2], *came), other[2])
    loaded += others

    def call(after_this, *packed):
        *parts, token = experts_call(place, after_this, packed, loaded)
        return parts, token

    half, cut = ring_total // 2, block.shape[0] // 2

    def split(pair):
        return (pair[0][:cut], pair[1][cut:]), (pair[0][cut:], pair[1][:cut])

    long, short = split(came)
    long_next, short_next = send(tie(long, loaded_own, *other)), send(tie(short, loaded_own, *other))
    (mine,), last = call(last, block)
    filler = last
    parts, last = call(last, *came)
    ahead_terms, behind_terms = split(parts)
    long_terms, short_terms = [None, ahead_terms], [None, behind_terms]
    for s in range(2, half - 1):
        long, short = long_next, short_next
        long_next = send(tie(long, filler))
        short_next = send(tie(short, last))
        parts, last = call(last, long[0], short[0], long[1], short[1])
        long_terms.append((parts[0], parts[2]))
        short_terms.append((parts[1], parts[3]))
    long, short = long_next, short_next
    long_last = send(tie(long, last))
    parts, last = call(last, *long)
    long_terms.append(tuple(parts))
    parts, last = call(last, *short)
    short_back = send_back(parts)
    parts, last = call(last, *long_last)
    long_back = send_back(tie(parts, *short_back))
    for s in range(half - 1, 0, -1):
        if s < half - 1:
            short_back = send_back([added(a, b) for a, b in zip(short_terms[s], short_back)])
        long_back = send_back([added(a, b) for a, b in zip(long_terms[s], long_back)])
    return finish(expert_ids, (mine, long_back[0], short_back[1], short_back[0], long_back[1]), width)


def body(tokens, cotangent, expert_ids, route_weights, gate_weight, up_weight, down_weight):
    args = (tokens, cotangent, expert_ids, route_weights, gate_weight, up_weight, down_weight)
    ring_total, loc_total = lax.axis_size("grp"), lax.axis_size("loc")
    experts = ring_total * loc_total * gate_weight.shape[0]
    if loc_total == 2 and ring_total in (6, 8) and experts <= LANES and tokens.shape[0] % 32 == 0:
        return ring_body(*args)
    return routed_body(*args)


def solution(mesh):
    placed = (
        P(("rep", "grp", "loc"), None),
        P(("rep", "grp", "loc"), None),
        P(("rep", "grp", "loc"), None),
        P(("rep", "grp", "loc"), None),
        P(("grp", "loc"), None, None),
        P(("grp", "loc"), None, None),
        P(("grp", "loc"), None, None),
    )
    return jax.shard_map(
        body,
        mesh=mesh,
        in_specs=placed,
        out_specs=(P(("rep", "grp", "loc"), None), P(("rep", "grp", "loc"), None)),
        check_vma=False,
    )
```

```python
import functools

import jax
import jax.numpy as jnp
from jax import lax
from jax.experimental import pallas as pl
from jax.experimental.pallas import tpu as pltpu
from jax.sharding import PartitionSpec as P

TOP = 8
TOP_GROUPS = 4


def shortened(shard):
    return jax.tree.map(lambda a: a.astype(jnp.bfloat16) if a.dtype == jnp.float32 else a, shard)


def take_rows(values, indices, filler):
    return jnp.take(values, indices, axis=0, mode="fill", fill_value=filler)


def route_table(targets, dest_total, capacity):
    token_total = targets.shape[0]
    dest_iota = jnp.arange(dest_total, dtype=jnp.int32)
    reached = jnp.any(targets[:, :, None] == dest_iota[None, None, :], axis=1)
    ranked = jnp.cumsum(reached.astype(jnp.int32), axis=0) - 1
    slot_of = jnp.where(reached, ranked, capacity)
    dest_grid = jnp.broadcast_to(dest_iota[None, :], slot_of.shape)
    token_grid = jnp.broadcast_to(jnp.arange(token_total, dtype=jnp.int32)[:, None], slot_of.shape)
    sources = jnp.full((dest_total, capacity), token_total, jnp.int32)
    sources = sources.at[dest_grid, slot_of].set(token_grid, mode="drop")
    return (slot_of, sources)


def token_groups(group_ids, group_total):
    token_total = group_ids.shape[0]
    group_iota = jnp.arange(group_total, dtype=jnp.int32)
    reached = jnp.any(group_ids[:, :, None] == group_iota[None, None, :], axis=1)
    ranked = jnp.cumsum(reached.astype(jnp.int32), axis=1) - 1
    column = jnp.where(reached, ranked, TOP_GROUPS)
    token_grid = jnp.broadcast_to(jnp.arange(token_total, dtype=jnp.int32)[:, None], column.shape)
    listed = jnp.full((token_total, TOP_GROUPS), group_total, jnp.int32)
    return listed.at[token_grid, column].set(
        jnp.broadcast_to(group_iota[None, :], column.shape), mode="drop"
    )


def expert_pass(
    token_rows,
    grad_rows,
    id_rows,
    weight_rows,
    gate_weight,
    up_weight,
    down_weight,
    first_expert,
    capacity,
):
    row_total = token_rows.shape[0]
    local_total = gate_weight.shape[0]
    model_width = token_rows.shape[1]
    experts_here = first_expert + jnp.arange(local_total, dtype=jnp.int32)
    matched = id_rows[None, :, :] == experts_here[:, None, None]
    chosen = jnp.any(matched, axis=2)
    weight_of = jnp.sum(
        jnp.where(matched, weight_rows.astype(jnp.float32)[None, :, :], 0.0), axis=2
    )
    ranked = jnp.cumsum(chosen.astype(jnp.int32), axis=1) - 1
    slot_of = jnp.where(chosen, ranked, capacity)
    expert_grid = jnp.broadcast_to(jnp.arange(local_total, dtype=jnp.int32)[:, None], slot_of.shape)
    row_grid = jnp.broadcast_to(jnp.arange(row_total, dtype=jnp.int32)[None, :], slot_of.shape)
    picks = (
        jnp.full((local_total, capacity), row_total, jnp.int32)
        .at[expert_grid, slot_of]
        .set(row_grid, mode="drop")
    )
    buffer_x = take_rows(token_rows, picks, 0)
    buffer_g = take_rows(grad_rows, picks, 0)
    buffer_w = jnp.take_along_axis(weight_of, picks, axis=1, mode="fill", fill_value=0.0)
    gate_act = jnp.einsum("ecd,edf->ecf", buffer_x, gate_weight, preferred_element_type=jnp.float32)
    up_act = jnp.einsum("ecd,edf->ecf", buffer_x, up_weight, preferred_element_type=jnp.float32)
    back_grad = jnp.einsum(
        "ecd,efd->ecf", buffer_g, down_weight, preferred_element_type=jnp.float32
    )
    sigmoid_val = jax.nn.sigmoid(gate_act)
    silu_val = gate_act * sigmoid_val
    route_grad = jnp.sum(back_grad * silu_val * up_act, axis=2)
    hidden_grad = buffer_w[:, :, None] * back_grad
    gate_grad = (
        hidden_grad * up_act * sigmoid_val * (1.0 + gate_act * (1.0 - sigmoid_val))
    ).astype(jnp.bfloat16)
    up_grad = (hidden_grad * silu_val).astype(jnp.bfloat16)
    input_grad = jnp.einsum(
        "ecf,edf->ecd", gate_grad, gate_weight, preferred_element_type=jnp.float32
    )
    input_grad = input_grad + jnp.einsum(
        "ecf,edf->ecd", up_grad, up_weight, preferred_element_type=jnp.float32
    )
    partial_value = jnp.zeros((row_total, model_width), jnp.float32)
    partial_value = partial_value.at[picks.reshape(-1)].add(
        input_grad.reshape(-1, model_width), mode="drop"
    )
    cap_grid = jnp.broadcast_to(jnp.arange(local_total, dtype=jnp.int32)[:, None], picks.shape)
    route_per = (
        jnp.zeros((local_total, row_total), jnp.float32)
        .at[cap_grid, picks]
        .add(route_grad, mode="drop")
    )
    route_rows = jnp.sum(jnp.where(matched, route_per[:, :, None], 0.0), axis=0)
    return (partial_value, route_rows)


def routed_body(tokens, cotangent, expert_ids, route_weights, gate_weight, up_weight, down_weight):
    group_total = lax.axis_size("grp")
    loc_total = lax.axis_size("loc")
    token_total = tokens.shape[0]
    model_width = tokens.shape[1]
    per_device = gate_weight.shape[0]
    per_group = per_device * loc_total
    group_cap = 6 * token_total // group_total
    expert_cap = 3 * token_total * loc_total
    device_rank = lax.axis_index("grp") * loc_total + lax.axis_index("loc")
    first_expert = device_rank * per_device
    group_ids = expert_ids // per_group
    listed = token_groups(group_ids, group_total)
    slot_range = jnp.arange(TOP, dtype=jnp.int32)[None, :]
    slot_of, sources = route_table(group_ids, group_total, group_cap)
    send_x = take_rows(tokens, sources, 0)
    send_g = take_rows(cotangent, sources, 0)
    send_ids = take_rows(expert_ids, sources, -1)
    send_w = take_rows(route_weights, sources, 0)
    recv_x, recv_g, recv_ids, recv_w = (
        lax.all_to_all(send_x, "grp", split_axis=0, concat_axis=0, tiled=True),
        lax.all_to_all(send_g, "grp", split_axis=0, concat_axis=0, tiled=True),
        lax.all_to_all(send_ids, "grp", split_axis=0, concat_axis=0, tiled=True),
        lax.all_to_all(send_w, "grp", split_axis=0, concat_axis=0, tiled=True),
    )
    row_total = group_total * group_cap
    shared_x, shared_g, shared_ids, shared_w = (
        lax.all_gather(recv_x.reshape(row_total, model_width), "loc", axis=0, tiled=True),
        lax.all_gather(recv_g.reshape(row_total, model_width), "loc", axis=0, tiled=True),
        lax.all_gather(shortened(recv_ids.reshape(row_total, TOP)), "loc", axis=0, tiled=True),
        lax.all_gather(recv_w.reshape(row_total, TOP), "loc", axis=0, tiled=True),
    )
    partial_value, route_rows = expert_pass(
        shared_x,
        shared_g,
        shared_ids,
        shared_w,
        gate_weight,
        up_weight,
        down_weight,
        first_expert,
        expert_cap,
    )
    summed, route_sum = (
        lax.psum_scatter(partial_value, "loc", scatter_dimension=0, tiled=True),
        lax.psum_scatter(route_rows, "loc", scatter_dimension=0, tiled=True),
    )
    group_part = summed.astype(jnp.bfloat16).reshape(group_total, group_cap, model_width)
    route_part = route_sum.astype(jnp.bfloat16).reshape(group_total, group_cap, TOP)
    back_terms, back_route = (
        lax.all_to_all(group_part, "grp", split_axis=0, concat_axis=0, tiled=True),
        lax.all_to_all(route_part, "grp", split_axis=0, concat_axis=0, tiled=True),
    )
    slot_pad = jnp.concatenate([slot_of, jnp.full((token_total, 1), group_cap, jnp.int32)], axis=1)
    found = jnp.take_along_axis(slot_pad, listed, axis=1)
    position = jnp.where(found < group_cap, listed * group_cap + found, row_total)
    pieces = take_rows(back_terms.reshape(row_total, model_width), position, 0)
    grad_tokens = jnp.sum(pieces.astype(jnp.float32), axis=1).astype(jnp.bfloat16)
    slot_found = jnp.take_along_axis(slot_of, group_ids, axis=1)
    route_index = (group_ids * group_cap + slot_found) * TOP + slot_range
    grad_weights = back_route.reshape(row_total * TOP)[route_index]
    return (grad_tokens, grad_weights)


LANES = 128
NT = (((1,), (1,)), ((), ()))
ANYWHERE = pl.BlockSpec(memory_space=pl.ANY)
IN_VMEM = pl.BlockSpec(memory_space=pltpu.VMEM)
IN_SMEM = pl.BlockSpec(memory_space=pltpu.SMEM)
MIB = 1024 * 1024
TOKEN = jax.ShapeDtypeStruct((8, LANES), jnp.float32)


def pack_kernel(tokens, cotangent, ids, weights, block, ids_here, weights_here, sems):
    rows, width = tokens.shape
    small = (
        pltpu.make_async_copy(ids, ids_here, sems.at[0]),
        pltpu.make_async_copy(weights, weights_here, sems.at[1]),
    )
    large = (
        pltpu.make_async_copy(tokens, block.at[:, pl.ds(0, width)], sems.at[2]),
        pltpu.make_async_copy(cotangent, block.at[:, pl.ds(width, width)], sems.at[3]),
    )
    for copy in small + large:
        copy.start()
    for copy in small:
        copy.wait()
    expert = lax.broadcasted_iota(jnp.int32, (LANES, rows), 0)
    table = jnp.zeros((LANES, rows), jnp.float32)
    for k in range(ids.shape[0]):
        chosen = expert == ids_here[k : k + 1, :]
        table += jnp.where(chosen, weights_here[k : k + 1, :].astype(jnp.float32), 0.0)
    block[:, 2 * width :] = table.T.astype(jnp.bfloat16)
    for copy in large:
        copy.wait()


def pack(tokens, cotangent, ids, weights):
    rows, width = tokens.shape
    return pl.pallas_call(
        pack_kernel,
        out_shape=pltpu.VMEM((rows, 2 * width + LANES), jnp.bfloat16),
        in_specs=[ANYWHERE] * 4,
        out_specs=IN_VMEM,
        scratch_shapes=[
            pltpu.VMEM((ids.shape[1], rows), jnp.int32),
            pltpu.VMEM((ids.shape[1], rows), jnp.bfloat16),
            pltpu.SemaphoreType.DMA((4,)),
        ],
        compiler_params=pltpu.CompilerParams(vmem_limit_bytes=8 * MIB),
    )(*(in_hbm(a) for a in (tokens, cotangent, ids.T, weights.T)))


def in_hbm(a):
    return pltpu.with_memory_space_constraint(a, pltpu.HBM)


def in_vmem(a):
    return pltpu.with_memory_space_constraint(a, pltpu.VMEM)


def load_kernel(after_this, gate, up, down, gate_up, back, down_back, token, down_here, sems):
    del after_this
    token[...] = jnp.zeros_like(token)
    per_device, hidden = gate.shape[0], gate.shape[2]
    copies = []
    for e in range(per_device):
        copies.append(
            (
                pltpu.make_async_copy(down.at[e], down_here.at[e], sems.at[2, e]),
                pltpu.make_async_copy(gate.at[e], gate_up.at[e, :, pl.ds(0, hidden)], sems.at[0, e]),
                pltpu.make_async_copy(up.at[e], gate_up.at[e, :, pl.ds(hidden, hidden)], sems.at[1, e]),
            )
        )
    for three in copies:
        for copy in three:
            copy.start()
    for e, (first, second, third) in enumerate(copies):
        first.wait()
        down_back[:, e * hidden : (e + 1) * hidden] = down_here[e].T
        second.wait()
        third.wait()
        back[2 * e * hidden : 2 * (e + 1) * hidden, :] = gate_up[e].T


def load(after_this, gate, up, down):
    per_device, width, hidden = gate.shape
    return pl.pallas_call(
        load_kernel,
        out_shape=(
            pltpu.VMEM((per_device, width, 2 * hidden), jnp.bfloat16),
            pltpu.VMEM((2 * per_device * hidden, width), jnp.bfloat16),
            pltpu.VMEM((width, per_device * hidden), jnp.bfloat16),
            TOKEN,
        ),
        in_specs=[ANYWHERE] * 4,
        out_specs=(IN_VMEM,) * 4,
        scratch_shapes=[pltpu.VMEM(down.shape, jnp.bfloat16), pltpu.SemaphoreType.DMA((3, per_device))],
        compiler_params=pltpu.CompilerParams(vmem_limit_bytes=8 * MIB),
        cost_estimate=pl.CostEstimate(flops=1, bytes_accessed=24 * MIB, transcendentals=0),
    )(after_this, gate, up, down)


def experts_kernel(pieces, place, after_this, *refs):
    del after_this
    packed, refs = refs[:pieces], refs[pieces:]
    loaded, refs = (refs[:3], refs[3:6]), refs[6:]
    outs, token = refs[:pieces], refs[pieces]
    token[...] = jnp.zeros_like(token)
    per_device, width, both_hidden = loaded[0][0].shape
    hidden = both_hidden // 2
    x = jnp.concatenate([a[:, :width] for a in packed], axis=0)
    g = jnp.concatenate([a[:, width : 2 * width] for a in packed], axis=0)
    table = jnp.concatenate([a[:, 2 * width :] for a in packed], axis=0).astype(jnp.float32)
    lane = lax.broadcasted_iota(jnp.int32, table.shape, 1)
    route = jnp.zeros(table.shape, jnp.float32)
    grads = []
    for pair, (gate_up, _, down_back) in enumerate(loaded):
        backs = jnp.dot(g, down_back[...], preferred_element_type=jnp.float32)
        mine = []
        for at in range(per_device):
            back = backs[:, at * hidden : (at + 1) * hidden]
            column = place[0] + lax.rem(place[1] + pair * per_device + at, 2 * per_device)
            weight = jnp.sum(jnp.where(lane == column, table, 0.0), axis=1, keepdims=True)
            both = jnp.dot(x, gate_up[at], preferred_element_type=jnp.float32)
            gate_act, up_act = both[:, :hidden], both[:, hidden:]
            sig = jax.nn.sigmoid(gate_act)
            silu = gate_act * sig
            back_up = back * up_act
            route_grad = jnp.sum(back_up * silu, axis=1, keepdims=True)
            mine.append((weight * back_up * sig * (1.0 + gate_act * (1.0 - sig))).astype(jnp.bfloat16))
            mine.append((weight * back * silu).astype(jnp.bfloat16))
            route += jnp.where(lane == column, route_grad, 0.0)
        grads.append(jnp.concatenate(mine, axis=1))
    step = 4 * LANES

    def chunk(i, carry):
        part = pl.ds(pl.multiple_of(i * step, step), step)
        total = sum(
            jnp.dot(a, back[:, part], preferred_element_type=jnp.float32) for a, (_, back, _) in zip(grads, loaded)
        ).astype(jnp.bfloat16)
        start = 0
        for out in outs:
            out[:, part] = total[start : start + out.shape[0]]
            start += out.shape[0]
        return carry

    lax.fori_loop(0, width // step, chunk, 0)
    start = 0
    for out in outs:
        out[:, width:] = route[start : start + out.shape[0]].astype(out.dtype)
        start += out.shape[0]


def experts_call(place, after_this, packed, loaded):
    width = loaded[0].shape[1]
    return pl.pallas_call(
        functools.partial(experts_kernel, len(packed)),
        out_shape=[jax.ShapeDtypeStruct((a.shape[0], width + LANES), jnp.bfloat16) for a in packed] + [TOKEN],
        in_specs=[IN_SMEM, ANYWHERE] + [IN_VMEM] * (len(packed) + 6),
        out_specs=[IN_VMEM] * (len(packed) + 1),
        compiler_params=pltpu.CompilerParams(vmem_limit_bytes=12 * MIB),
        cost_estimate=pl.CostEstimate(flops=1, bytes_accessed=1, transcendentals=0),
    )(place, after_this, *(in_vmem(a) for a in packed), *loaded)


def finish_kernel(ids, mine, top0, top1, low0, low1, grad_tokens, grad_weights):
    rows, width = grad_tokens.shape
    cut = rows // 2
    routes = []
    for start, terms in ((0, (top0, top1)), (cut, (low0, low1))):
        summed = mine[start : start + cut, :].astype(jnp.float32)
        for term in terms:
            summed += term[...].astype(jnp.float32)
        grad_tokens[start : start + cut, :] = summed[:, :width].astype(grad_tokens.dtype)
        routes.append(summed[:, width:])
    route = jnp.concatenate(routes, axis=0).T
    expert = lax.broadcasted_iota(jnp.int32, route.shape, 0)
    found = [
        jnp.sum(jnp.where(expert == ids[k : k + 1, :], route, 0.0), axis=0, keepdims=True) for k in range(ids.shape[0])
    ]
    grad_weights[...] = jnp.concatenate(found, axis=0).astype(grad_weights.dtype)


def finish(ids, terms, width):
    rows, top = ids.shape
    grad_tokens, grad_weights = pl.pallas_call(
        finish_kernel,
        out_shape=(
            jax.ShapeDtypeStruct((rows, width), jnp.bfloat16),
            jax.ShapeDtypeStruct((top, rows), jnp.bfloat16),
        ),
        in_specs=[IN_VMEM] * 6,
        out_specs=(IN_VMEM, IN_VMEM),
        compiler_params=pltpu.CompilerParams(vmem_limit_bytes=12 * MIB),
    )(ids.T, *terms)
    return grad_tokens, grad_weights.T


def add_kernel(a, b, out):
    out[...] = (a[...].astype(jnp.float32) + b[...].astype(jnp.float32)).astype(out.dtype)


def added(a, b):
    return pl.pallas_call(
        add_kernel,
        out_shape=jax.ShapeDtypeStruct(a.shape, a.dtype),
        in_specs=[IN_VMEM] * 2,
        out_specs=IN_VMEM,
        compiler_params=pltpu.CompilerParams(vmem_limit_bytes=8 * MIB),
        cost_estimate=pl.CostEstimate(flops=1, bytes_accessed=1, transcendentals=0),
    )(a, b)


def ring_body(tokens, cotangent, expert_ids, route_weights, gate_weight, up_weight, down_weight):
    ring_total = lax.axis_size("grp")
    loc_total = lax.axis_size("loc")
    width = tokens.shape[1]
    per_device = gate_weight.shape[0]
    order = list(range(0, ring_total, 2)) + list(range(ring_total - 1, 0, -2))
    ahead = [(order[i], order[(i + 1) % ring_total]) for i in range(ring_total)]
    behind = [(b, a) for a, b in ahead]
    rank, loc = lax.axis_index("grp"), lax.axis_index("loc")

    def send(pair):
        return lax.ppermute(pair[0], "grp", ahead), lax.ppermute(pair[1], "grp", behind)

    def send_back(pair):
        return lax.ppermute(pair[0], "grp", behind), lax.ppermute(pair[1], "grp", ahead)

    def tie(pair, *others):
        return tuple(lax.optimization_barrier((a, *others))[0] for a in pair)

    own = (gate_weight, up_weight, down_weight)
    other = [lax.ppermute(a, "loc", [(i, loc_total - 1 - i) for i in range(loc_total)]) for a in own]
    block = pack(tokens, cotangent, expert_ids, route_weights)
    came = send((block, block))
    place = jnp.stack([rank * (loc_total * per_device), loc * per_device]).astype(jnp.int32)
    *loaded, loaded_own = load(place, *(in_hbm(a) for a in own))
    *others, last = load(loaded_own, *tie(other[:2], *came), other[2])
    loaded += others

    def call(after_this, *packed):
        *parts, token = experts_call(place, after_this, packed, loaded)
        return parts, token

    half, cut = ring_total // 2, block.shape[0] // 2

    def split(pair):
        return (pair[0][:cut], pair[1][cut:]), (pair[0][cut:], pair[1][:cut])

    long, short = split(came)
    long_next, short_next = send(tie(long, loaded_own, *other)), send(tie(short, loaded_own, *other))
    (mine,), last = call(last, block)
    filler = last
    parts, last = call(last, *came)
    ahead_terms, behind_terms = split(parts)
    long_terms, short_terms = [None, ahead_terms], [None, behind_terms]
    for s in range(2, half - 1):
        long, short = long_next, short_next
        long_next = send(tie(long, filler))
        short_next = send(tie(short, last))
        parts, last = call(last, long[0], short[0], long[1], short[1])
        long_terms.append((parts[0], parts[2]))
        short_terms.append((parts[1], parts[3]))
    long, short = long_next, short_next
    long_last = send(tie(long, last))
    parts, last = call(last, *long)
    long_terms.append(tuple(parts))
    parts, last = call(last, *short)
    short_back = send_back(parts)
    parts, last = call(last, *long_last)
    long_back = send_back(tie(parts, *short_back))
    for s in range(half - 1, 0, -1):
        if s < half - 1:
            short_back = send_back([added(a, b) for a, b in zip(short_terms[s], short_back)])
        long_back = send_back([added(a, b) for a, b in zip(long_terms[s], long_back)])
    return finish(expert_ids, (mine, long_back[0], short_back[1], short_back[0], long_back[1]), width)


def body(tokens, cotangent, expert_ids, route_weights, gate_weight, up_weight, down_weight):
    args = (tokens, cotangent, expert_ids, route_weights, gate_weight, up_weight, down_weight)
    ring_total, loc_total = lax.axis_size("grp"), lax.axis_size("loc")
    experts = ring_total * loc_total * gate_weight.shape[0]
    if loc_total == 2 and ring_total in (6, 8) and experts <= LANES and tokens.shape[0] % 32 == 0:
        return ring_body(*args)
    return routed_body(*args)


def solution(mesh):
    placed = (
        P(("rep", "grp", "loc"), None),
        P(("rep", "grp", "loc"), None),
        P(("rep", "grp", "loc"), None),
        P(("rep", "grp", "loc"), None),
        P(("grp", "loc"), None, None),
        P(("grp", "loc"), None, None),
        P(("grp", "loc"), None, None),
    )
    return jax.shard_map(
        body,
        mesh=mesh,
        in_specs=placed,
        out_specs=(P(("rep", "grp", "loc"), None), P(("rep", "grp", "loc"), None)),
        check_vma=False,
    )
```

```python
import functools

import jax
import jax.numpy as jnp
from jax import lax
from jax.experimental import pallas as pl
from jax.experimental.pallas import tpu as pltpu
from jax.sharding import PartitionSpec as P

TOP = 8
TOP_GROUPS = 4


def shortened(shard):
    return jax.tree.map(lambda a: a.astype(jnp.bfloat16) if a.dtype == jnp.float32 else a, shard)


def take_rows(values, indices, filler):
    return jnp.take(values, indices, axis=0, mode="fill", fill_value=filler)


def route_table(targets, dest_total, capacity):
    token_total = targets.shape[0]
    dest_iota = jnp.arange(dest_total, dtype=jnp.int32)
    reached = jnp.any(targets[:, :, None] == dest_iota[None, None, :], axis=1)
    ranked = jnp.cumsum(reached.astype(jnp.int32), axis=0) - 1
    slot_of = jnp.where(reached, ranked, capacity)
    dest_grid = jnp.broadcast_to(dest_iota[None, :], slot_of.shape)
    token_grid = jnp.broadcast_to(jnp.arange(token_total, dtype=jnp.int32)[:, None], slot_of.shape)
    sources = jnp.full((dest_total, capacity), token_total, jnp.int32)
    sources = sources.at[dest_grid, slot_of].set(token_grid, mode="drop")
    return (slot_of, sources)


def token_groups(group_ids, group_total):
    token_total = group_ids.shape[0]
    group_iota = jnp.arange(group_total, dtype=jnp.int32)
    reached = jnp.any(group_ids[:, :, None] == group_iota[None, None, :], axis=1)
    ranked = jnp.cumsum(reached.astype(jnp.int32), axis=1) - 1
    column = jnp.where(reached, ranked, TOP_GROUPS)
    token_grid = jnp.broadcast_to(jnp.arange(token_total, dtype=jnp.int32)[:, None], column.shape)
    listed = jnp.full((token_total, TOP_GROUPS), group_total, jnp.int32)
    return listed.at[token_grid, column].set(
        jnp.broadcast_to(group_iota[None, :], column.shape), mode="drop"
    )


def expert_pass(
    token_rows,
    grad_rows,
    id_rows,
    weight_rows,
    gate_weight,
    up_weight,
    down_weight,
    first_expert,
    capacity,
):
    row_total = token_rows.shape[0]
    local_total = gate_weight.shape[0]
    model_width = token_rows.shape[1]
    experts_here = first_expert + jnp.arange(local_total, dtype=jnp.int32)
    matched = id_rows[None, :, :] == experts_here[:, None, None]
    chosen = jnp.any(matched, axis=2)
    weight_of = jnp.sum(
        jnp.where(matched, weight_rows.astype(jnp.float32)[None, :, :], 0.0), axis=2
    )
    ranked = jnp.cumsum(chosen.astype(jnp.int32), axis=1) - 1
    slot_of = jnp.where(chosen, ranked, capacity)
    expert_grid = jnp.broadcast_to(jnp.arange(local_total, dtype=jnp.int32)[:, None], slot_of.shape)
    row_grid = jnp.broadcast_to(jnp.arange(row_total, dtype=jnp.int32)[None, :], slot_of.shape)
    picks = (
        jnp.full((local_total, capacity), row_total, jnp.int32)
        .at[expert_grid, slot_of]
        .set(row_grid, mode="drop")
    )
    buffer_x = take_rows(token_rows, picks, 0)
    buffer_g = take_rows(grad_rows, picks, 0)
    buffer_w = jnp.take_along_axis(weight_of, picks, axis=1, mode="fill", fill_value=0.0)
    gate_act = jnp.einsum("ecd,edf->ecf", buffer_x, gate_weight, preferred_element_type=jnp.float32)
    up_act = jnp.einsum("ecd,edf->ecf", buffer_x, up_weight, preferred_element_type=jnp.float32)
    back_grad = jnp.einsum(
        "ecd,efd->ecf", buffer_g, down_weight, preferred_element_type=jnp.float32
    )
    sigmoid_val = jax.nn.sigmoid(gate_act)
    silu_val = gate_act * sigmoid_val
    route_grad = jnp.sum(back_grad * silu_val * up_act, axis=2)
    hidden_grad = buffer_w[:, :, None] * back_grad
    gate_grad = (
        hidden_grad * up_act * sigmoid_val * (1.0 + gate_act * (1.0 - sigmoid_val))
    ).astype(jnp.bfloat16)
    up_grad = (hidden_grad * silu_val).astype(jnp.bfloat16)
    input_grad = jnp.einsum(
        "ecf,edf->ecd", gate_grad, gate_weight, preferred_element_type=jnp.float32
    )
    input_grad = input_grad + jnp.einsum(
        "ecf,edf->ecd", up_grad, up_weight, preferred_element_type=jnp.float32
    )
    partial_value = jnp.zeros((row_total, model_width), jnp.float32)
    partial_value = partial_value.at[picks.reshape(-1)].add(
        input_grad.reshape(-1, model_width), mode="drop"
    )
    cap_grid = jnp.broadcast_to(jnp.arange(local_total, dtype=jnp.int32)[:, None], picks.shape)
    route_per = (
        jnp.zeros((local_total, row_total), jnp.float32)
        .at[cap_grid, picks]
        .add(route_grad, mode="drop")
    )
    route_rows = jnp.sum(jnp.where(matched, route_per[:, :, None], 0.0), axis=0)
    return (partial_value, route_rows)


def routed_body(tokens, cotangent, expert_ids, route_weights, gate_weight, up_weight, down_weight):
    group_total = lax.axis_size("grp")
    loc_total = lax.axis_size("loc")
    token_total = tokens.shape[0]
    model_width = tokens.shape[1]
    per_device = gate_weight.shape[0]
    per_group = per_device * loc_total
    group_cap = 6 * token_total // group_total
    expert_cap = 3 * token_total * loc_total
    device_rank = lax.axis_index("grp") * loc_total + lax.axis_index("loc")
    first_expert = device_rank * per_device
    group_ids = expert_ids // per_group
    listed = token_groups(group_ids, group_total)
    slot_range = jnp.arange(TOP, dtype=jnp.int32)[None, :]
    slot_of, sources = route_table(group_ids, group_total, group_cap)
    send_x = take_rows(tokens, sources, 0)
    send_g = take_rows(cotangent, sources, 0)
    send_ids = take_rows(expert_ids, sources, -1)
    send_w = take_rows(route_weights, sources, 0)
    recv_x, recv_g, recv_ids, recv_w = (
        lax.all_to_all(send_x, "grp", split_axis=0, concat_axis=0, tiled=True),
        lax.all_to_all(send_g, "grp", split_axis=0, concat_axis=0, tiled=True),
        lax.all_to_all(send_ids, "grp", split_axis=0, concat_axis=0, tiled=True),
        lax.all_to_all(send_w, "grp", split_axis=0, concat_axis=0, tiled=True),
    )
    row_total = group_total * group_cap
    shared_x, shared_g, shared_ids, shared_w = (
        lax.all_gather(recv_x.reshape(row_total, model_width), "loc", axis=0, tiled=True),
        lax.all_gather(recv_g.reshape(row_total, model_width), "loc", axis=0, tiled=True),
        lax.all_gather(shortened(recv_ids.reshape(row_total, TOP)), "loc", axis=0, tiled=True),
        lax.all_gather(recv_w.reshape(row_total, TOP), "loc", axis=0, tiled=True),
    )
    partial_value, route_rows = expert_pass(
        shared_x,
        shared_g,
        shared_ids,
        shared_w,
        gate_weight,
        up_weight,
        down_weight,
        first_expert,
        expert_cap,
    )
    summed, route_sum = (
        lax.psum_scatter(partial_value, "loc", scatter_dimension=0, tiled=True),
        lax.psum_scatter(route_rows, "loc", scatter_dimension=0, tiled=True),
    )
    group_part = summed.astype(jnp.bfloat16).reshape(group_total, group_cap, model_width)
    route_part = route_sum.astype(jnp.bfloat16).reshape(group_total, group_cap, TOP)
    back_terms, back_route = (
        lax.all_to_all(group_part, "grp", split_axis=0, concat_axis=0, tiled=True),
        lax.all_to_all(route_part, "grp", split_axis=0, concat_axis=0, tiled=True),
    )
    slot_pad = jnp.concatenate([slot_of, jnp.full((token_total, 1), group_cap, jnp.int32)], axis=1)
    found = jnp.take_along_axis(slot_pad, listed, axis=1)
    position = jnp.where(found < group_cap, listed * group_cap + found, row_total)
    pieces = take_rows(back_terms.reshape(row_total, model_width), position, 0)
    grad_tokens = jnp.sum(pieces.astype(jnp.float32), axis=1).astype(jnp.bfloat16)
    slot_found = jnp.take_along_axis(slot_of, group_ids, axis=1)
    route_index = (group_ids * group_cap + slot_found) * TOP + slot_range
    grad_weights = back_route.reshape(row_total * TOP)[route_index]
    return (grad_tokens, grad_weights)


LANES = 128
NT = (((1,), (1,)), ((), ()))
ANYWHERE = pl.BlockSpec(memory_space=pl.ANY)
IN_VMEM = pl.BlockSpec(memory_space=pltpu.VMEM)
IN_SMEM = pl.BlockSpec(memory_space=pltpu.SMEM)
MIB = 1024 * 1024
TOKEN = jax.ShapeDtypeStruct((8, LANES), jnp.float32)


def pack_kernel(per_group, tokens, cotangent, ids, weights, block, order, ids_here, weights_here, rows_here, sems):
    rows, width = tokens.shape
    first_expert = (lax.axis_size("grp") - 1 - lax.axis_index("grp")) * per_group
    small = (
        pltpu.make_async_copy(ids, ids_here, sems.at[0]),
        pltpu.make_async_copy(weights, weights_here, sems.at[1]),
    )
    large = (
        pltpu.make_async_copy(tokens, rows_here.at[:, pl.ds(0, width)], sems.at[2]),
        pltpu.make_async_copy(cotangent, rows_here.at[:, pl.ds(width, width)], sems.at[3]),
    )
    for copy in small + large:
        copy.start()
    for copy in small:
        copy.wait()
    sublane = lax.broadcasted_iota(jnp.int32, (LANES, rows), 0)
    table = jnp.zeros((LANES, rows), jnp.float32)
    named = jnp.zeros((1, rows), jnp.float32)
    for k in range(ids.shape[0]):
        chosen = ids_here[k : k + 1, :]
        table += jnp.where(sublane == chosen, weights_here[k : k + 1, :].astype(jnp.float32), 0.0)
        inside = (chosen >= first_expert) & (chosen < first_expert + per_group)
        named = jnp.maximum(named, jnp.where(inside, 1.0, 0.0))
    from_row = lax.broadcasted_iota(jnp.int32, (rows, rows), 0)
    to_row = lax.broadcasted_iota(jnp.int32, (rows, rows), 1)
    upper = jnp.where(from_row <= to_row, 1.0, 0.0).astype(jnp.bfloat16)
    spread = jnp.broadcast_to(named, (16, rows)).astype(jnp.bfloat16)
    count = jnp.dot(spread, upper, preferred_element_type=jnp.float32)[:1].astype(jnp.int32)
    total = jnp.max(count, axis=1, keepdims=True)
    first = lax.shift_right_logical(total + 1, 1)
    at = lax.broadcasted_iota(jnp.int32, (1, rows), 1)
    rank = count - 1
    named_to = jnp.where(rank < first, rank, rows - total + rank)
    target = jnp.where(named > 0.0, named_to, first + at - count)
    order_here = jnp.where(from_row == target, 1.0, 0.0).astype(jnp.bfloat16)
    order[...] = order_here
    block[:, 2 * width :] = lax.dot_general(
        order_here, table.astype(jnp.bfloat16), NT, preferred_element_type=jnp.float32
    ).astype(jnp.bfloat16)
    for part, copy in enumerate(large):
        copy.wait()
        lanes = slice(part * width, (part + 1) * width)
        block[:, lanes] = jnp.dot(order_here, rows_here[:, lanes], preferred_element_type=jnp.float32).astype(jnp.bfloat16)


def pack(per_group, tokens, cotangent, ids, weights):
    rows, width = tokens.shape
    return pl.pallas_call(
        functools.partial(pack_kernel, per_group),
        out_shape=(
            pltpu.VMEM((rows, 2 * width + LANES), jnp.bfloat16),
            jax.ShapeDtypeStruct((rows, rows), jnp.bfloat16),
        ),
        in_specs=[ANYWHERE] * 4,
        out_specs=(IN_VMEM, IN_VMEM),
        scratch_shapes=[
            pltpu.VMEM((ids.shape[1], rows), jnp.int32),
            pltpu.VMEM((ids.shape[1], rows), jnp.bfloat16),
            pltpu.VMEM((rows, 2 * width), jnp.bfloat16),
            pltpu.SemaphoreType.DMA((4,)),
        ],
        compiler_params=pltpu.CompilerParams(vmem_limit_bytes=12 * MIB),
    )(*(in_hbm(a) for a in (tokens, cotangent, ids.T, weights.T)))


def in_hbm(a):
    return pltpu.with_memory_space_constraint(a, pltpu.HBM)


def in_vmem(a):
    return pltpu.with_memory_space_constraint(a, pltpu.VMEM)


def load_kernel(after_this, gate, up, down, gate_up, back, down_back, token, down_here, sems):
    del after_this
    token[...] = jnp.zeros_like(token)
    per_device, hidden = gate.shape[0], gate.shape[2]
    copies = []
    for e in range(per_device):
        copies.append(
            (
                pltpu.make_async_copy(down.at[e], down_here.at[e], sems.at[2, e]),
                pltpu.make_async_copy(gate.at[e], gate_up.at[e, :, pl.ds(0, hidden)], sems.at[0, e]),
                pltpu.make_async_copy(up.at[e], gate_up.at[e, :, pl.ds(hidden, hidden)], sems.at[1, e]),
            )
        )
    for three in copies:
        for copy in three:
            copy.start()
    for e, (first, second, third) in enumerate(copies):
        first.wait()
        down_back[:, e * hidden : (e + 1) * hidden] = down_here[e].T
        second.wait()
        third.wait()
        back[2 * e * hidden : 2 * (e + 1) * hidden, :] = gate_up[e].T


def load(after_this, gate, up, down):
    per_device, width, hidden = gate.shape
    return pl.pallas_call(
        load_kernel,
        out_shape=(
            pltpu.VMEM((per_device, width, 2 * hidden), jnp.bfloat16),
            pltpu.VMEM((2 * per_device * hidden, width), jnp.bfloat16),
            pltpu.VMEM((width, per_device * hidden), jnp.bfloat16),
            TOKEN,
        ),
        in_specs=[ANYWHERE] * 4,
        out_specs=(IN_VMEM,) * 4,
        scratch_shapes=[pltpu.VMEM(down.shape, jnp.bfloat16), pltpu.SemaphoreType.DMA((3, per_device))],
        compiler_params=pltpu.CompilerParams(vmem_limit_bytes=8 * MIB),
        cost_estimate=pl.CostEstimate(flops=1, bytes_accessed=24 * MIB, transcendentals=0),
    )(after_this, gate, up, down)


def experts_kernel(pieces, place, after_this, *refs):
    del after_this
    packed, refs = refs[:pieces], refs[pieces:]
    loaded, refs = (refs[:3], refs[3:6]), refs[6:]
    outs, token = refs[:pieces], refs[pieces]
    token[...] = jnp.zeros_like(token)
    per_device, width, both_hidden = loaded[0][0].shape
    hidden = both_hidden // 2
    x = jnp.concatenate([a[:, :width] for a in packed], axis=0)
    g = jnp.concatenate([a[:, width : 2 * width] for a in packed], axis=0)
    table = jnp.concatenate([a[:, 2 * width :] for a in packed], axis=0).astype(jnp.float32)
    lane = lax.broadcasted_iota(jnp.int32, table.shape, 1)
    route = jnp.zeros(table.shape, jnp.float32)
    grads = []
    for pair, (gate_up, _, down_back) in enumerate(loaded):
        backs = jnp.dot(g, down_back[...], preferred_element_type=jnp.float32)
        mine = []
        for at in range(per_device):
            back = backs[:, at * hidden : (at + 1) * hidden]
            column = place[0] + lax.rem(place[1] + pair * per_device + at, 2 * per_device)
            weight = jnp.sum(jnp.where(lane == column, table, 0.0), axis=1, keepdims=True)
            both = jnp.dot(x, gate_up[at], preferred_element_type=jnp.float32)
            gate_act, up_act = both[:, :hidden], both[:, hidden:]
            sig = jax.nn.sigmoid(gate_act)
            silu = gate_act * sig
            back_up = back * up_act
            route_grad = jnp.sum(back_up * silu, axis=1, keepdims=True)
            mine.append((weight * back_up * sig * (1.0 + gate_act * (1.0 - sig))).astype(jnp.bfloat16))
            mine.append((weight * back * silu).astype(jnp.bfloat16))
            route += jnp.where(lane == column, route_grad, 0.0)
        grads.append(jnp.concatenate(mine, axis=1))
    step = 4 * LANES

    def chunk(i, carry):
        part = pl.ds(pl.multiple_of(i * step, step), step)
        total = sum(
            jnp.dot(a, back[:, part], preferred_element_type=jnp.float32) for a, (_, back, _) in zip(grads, loaded)
        ).astype(jnp.bfloat16)
        start = 0
        for out in outs:
            out[:, part] = total[start : start + out.shape[0]]
            start += out.shape[0]
        return carry

    lax.fori_loop(0, width // step, chunk, 0)
    start = 0
    for out in outs:
        out[:, width:] = route[start : start + out.shape[0]].astype(out.dtype)
        start += out.shape[0]


def experts_call(place, after_this, packed, loaded):
    width = loaded[0].shape[1]
    return pl.pallas_call(
        functools.partial(experts_kernel, len(packed)),
        out_shape=[jax.ShapeDtypeStruct((a.shape[0], width + LANES), jnp.bfloat16) for a in packed] + [TOKEN],
        in_specs=[IN_SMEM, ANYWHERE] + [IN_VMEM] * (len(packed) + 6),
        out_specs=[IN_VMEM] * (len(packed) + 1),
        compiler_params=pltpu.CompilerParams(vmem_limit_bytes=12 * MIB),
        cost_estimate=pl.CostEstimate(flops=1, bytes_accessed=1, transcendentals=0),
    )(place, after_this, *(in_vmem(a) for a in packed), *loaded)


def finish_kernel(ids, order, mine, top0, top1, low0, low1, grad_tokens, grad_weights):
    rows, width = grad_tokens.shape
    cut = rows // 2
    halves = []
    for start, terms in ((0, (top0, top1)), (cut, (low0, low1))):
        summed = mine[start : start + cut, :].astype(jnp.float32)
        for term in terms:
            summed += term[...].astype(jnp.float32)
        halves.append(summed.astype(jnp.bfloat16))
    summed = jnp.concatenate(halves, axis=0)
    back = order[...].T
    grad_tokens[...] = jnp.dot(back, summed[:, :width], preferred_element_type=jnp.float32).astype(grad_tokens.dtype)
    route = jnp.dot(back, summed[:, width:], preferred_element_type=jnp.float32).T
    expert = lax.broadcasted_iota(jnp.int32, route.shape, 0)
    found = [
        jnp.sum(jnp.where(expert == ids[k : k + 1, :], route, 0.0), axis=0, keepdims=True) for k in range(ids.shape[0])
    ]
    grad_weights[...] = jnp.concatenate(found, axis=0).astype(grad_weights.dtype)


def finish(ids, terms, width):
    rows, top = ids.shape
    grad_tokens, grad_weights = pl.pallas_call(
        finish_kernel,
        out_shape=(
            jax.ShapeDtypeStruct((rows, width), jnp.bfloat16),
            jax.ShapeDtypeStruct((top, rows), jnp.bfloat16),
        ),
        in_specs=[IN_VMEM] * 7,
        out_specs=(IN_VMEM, IN_VMEM),
        compiler_params=pltpu.CompilerParams(vmem_limit_bytes=12 * MIB),
    )(ids.T, *terms)
    return grad_tokens, grad_weights.T


def add_kernel(start, a, b, out):
    rows = b.shape[0]
    if start:
        out[:start, :] = a[:start, :]
    if start + rows < a.shape[0]:
        out[start + rows :, :] = a[start + rows :, :]
    part = slice(start, start + rows)
    out[part, :] = (a[part, :].astype(jnp.float32) + b[...].astype(jnp.float32)).astype(out.dtype)


def added(a, b, start=0):
    return pl.pallas_call(
        functools.partial(add_kernel, start),
        out_shape=jax.ShapeDtypeStruct(a.shape, a.dtype),
        in_specs=[IN_VMEM] * 2,
        out_specs=IN_VMEM,
        compiler_params=pltpu.CompilerParams(vmem_limit_bytes=8 * MIB),
        cost_estimate=pl.CostEstimate(flops=1, bytes_accessed=1, transcendentals=0),
    )(a, b)


def ring_body(tokens, cotangent, expert_ids, route_weights, gate_weight, up_weight, down_weight):
    ring_total = lax.axis_size("grp")
    loc_total = lax.axis_size("loc")
    width = tokens.shape[1]
    per_device = gate_weight.shape[0]
    order = list(range(0, ring_total, 2)) + list(range(ring_total - 1, 0, -2))
    ahead = [(order[i], order[(i + 1) % ring_total]) for i in range(ring_total)]
    behind = [(b, a) for a, b in ahead]
    rank, loc = lax.axis_index("grp"), lax.axis_index("loc")

    def send(pair):
        return lax.ppermute(pair[0], "grp", ahead), lax.ppermute(pair[1], "grp", behind)

    def send_back(pair):
        return lax.ppermute(pair[0], "grp", behind), lax.ppermute(pair[1], "grp", ahead)

    def tie(pair, *others):
        return tuple(lax.optimization_barrier((a, *others))[0] for a in pair)

    own = (gate_weight, up_weight, down_weight)
    other = [lax.ppermute(a, "loc", [(i, loc_total - 1 - i) for i in range(loc_total)]) for a in own]
    per_group = loc_total * per_device
    place = jnp.stack([rank * per_group, loc * per_device]).astype(jnp.int32)
    block, rows_order = pack(per_group, tokens, cotangent, expert_ids, route_weights)
    came = send((block, block))
    *loaded, loaded_own = load(place, *(in_hbm(a) for a in own))
    *others, last = load(loaded_own, *tie(other[:2], *came), other[2])
    loaded += others

    def call(after_this, *packed):
        *parts, token = experts_call(place, after_this, packed, loaded)
        return parts, token

    half, cut = ring_total // 2, block.shape[0] // 2
    most = 3 * block.shape[0] // ring_total

    def split(pair):
        return (pair[0][:cut], pair[1][cut:]), (pair[0][cut:], pair[1][:cut])

    long, short = split(came)
    long_next, short_next = send(tie(long, loaded_own, *other)), send(tie(short, loaded_own, *other))
    (mine,), last = call(last, block)
    filler = last
    parts, last = call(last, *came)
    ahead_terms, behind_terms = split(parts)
    long_terms, short_terms = [None, ahead_terms], [None, behind_terms]
    for s in range(2, half - 1):
        long, short = long_next, short_next
        long_next = send(tie(long, filler))
        short_next = send(tie(short, last))
        parts, last = call(last, long[0], short[0], long[1], short[1])
        long_terms.append((parts[0], parts[2]))
        short_terms.append((parts[1], parts[3]))
    long, short = long_next, short_next
    long_last = send(tie((long[0][:most], long[1][cut - most :]), last))
    parts, last = call(last, *long)
    long_terms.append(tuple(parts))
    parts, last = call(last, *short)
    short_back = send_back(parts)
    parts, last = call(last, *long_last)
    long_back = send_back(tie(parts, *short_back))
    for s in range(half - 1, 0, -1):
        if s < half - 1:
            short_back = send_back([added(a, b) for a, b in zip(short_terms[s], short_back)])
        starts = (0, cut - most) if s == half - 1 else (0, 0)
        long_back = send_back([added(a, b, at) for a, b, at in zip(long_terms[s], long_back, starts)])
    return finish(expert_ids, (rows_order, mine, long_back[0], short_back[1], short_back[0], long_back[1]), width)


def body(tokens, cotangent, expert_ids, route_weights, gate_weight, up_weight, down_weight):
    args = (tokens, cotangent, expert_ids, route_weights, gate_weight, up_weight, down_weight)
    ring_total, loc_total = lax.axis_size("grp"), lax.axis_size("loc")
    experts = ring_total * loc_total * gate_weight.shape[0]
    if loc_total == 2 and ring_total in (6, 8) and experts <= LANES and tokens.shape[0] % 32 == 0:
        return ring_body(*args)
    return routed_body(*args)


def solution(mesh):
    placed = (
        P(("rep", "grp", "loc"), None),
        P(("rep", "grp", "loc"), None),
        P(("rep", "grp", "loc"), None),
        P(("rep", "grp", "loc"), None),
        P(("grp", "loc"), None, None),
        P(("grp", "loc"), None, None),
        P(("grp", "loc"), None, None),
    )
    return jax.shard_map(
        body,
        mesh=mesh,
        in_specs=placed,
        out_specs=(P(("rep", "grp", "loc"), None), P(("rep", "grp", "loc"), None)),
        check_vma=False,
    )
```

```python
import functools

import jax
import jax.numpy as jnp
from jax import lax
from jax.experimental import pallas as pl
from jax.experimental.pallas import tpu as pltpu
from jax.sharding import PartitionSpec as P

TOP = 8
TOP_GROUPS = 4


def shortened(shard):
    return jax.tree.map(lambda a: a.astype(jnp.bfloat16) if a.dtype == jnp.float32 else a, shard)


def take_rows(values, indices, filler):
    return jnp.take(values, indices, axis=0, mode="fill", fill_value=filler)


def route_table(targets, dest_total, capacity):
    token_total = targets.shape[0]
    dest_iota = jnp.arange(dest_total, dtype=jnp.int32)
    reached = jnp.any(targets[:, :, None] == dest_iota[None, None, :], axis=1)
    ranked = jnp.cumsum(reached.astype(jnp.int32), axis=0) - 1
    slot_of = jnp.where(reached, ranked, capacity)
    dest_grid = jnp.broadcast_to(dest_iota[None, :], slot_of.shape)
    token_grid = jnp.broadcast_to(jnp.arange(token_total, dtype=jnp.int32)[:, None], slot_of.shape)
    sources = jnp.full((dest_total, capacity), token_total, jnp.int32)
    sources = sources.at[dest_grid, slot_of].set(token_grid, mode="drop")
    return (slot_of, sources)


def token_groups(group_ids, group_total):
    token_total = group_ids.shape[0]
    group_iota = jnp.arange(group_total, dtype=jnp.int32)
    reached = jnp.any(group_ids[:, :, None] == group_iota[None, None, :], axis=1)
    ranked = jnp.cumsum(reached.astype(jnp.int32), axis=1) - 1
    column = jnp.where(reached, ranked, TOP_GROUPS)
    token_grid = jnp.broadcast_to(jnp.arange(token_total, dtype=jnp.int32)[:, None], column.shape)
    listed = jnp.full((token_total, TOP_GROUPS), group_total, jnp.int32)
    return listed.at[token_grid, column].set(
        jnp.broadcast_to(group_iota[None, :], column.shape), mode="drop"
    )


def expert_pass(
    token_rows,
    grad_rows,
    id_rows,
    weight_rows,
    gate_weight,
    up_weight,
    down_weight,
    first_expert,
    capacity,
):
    row_total = token_rows.shape[0]
    local_total = gate_weight.shape[0]
    model_width = token_rows.shape[1]
    experts_here = first_expert + jnp.arange(local_total, dtype=jnp.int32)
    matched = id_rows[None, :, :] == experts_here[:, None, None]
    chosen = jnp.any(matched, axis=2)
    weight_of = jnp.sum(
        jnp.where(matched, weight_rows.astype(jnp.float32)[None, :, :], 0.0), axis=2
    )
    ranked = jnp.cumsum(chosen.astype(jnp.int32), axis=1) - 1
    slot_of = jnp.where(chosen, ranked, capacity)
    expert_grid = jnp.broadcast_to(jnp.arange(local_total, dtype=jnp.int32)[:, None], slot_of.shape)
    row_grid = jnp.broadcast_to(jnp.arange(row_total, dtype=jnp.int32)[None, :], slot_of.shape)
    picks = (
        jnp.full((local_total, capacity), row_total, jnp.int32)
        .at[expert_grid, slot_of]
        .set(row_grid, mode="drop")
    )
    buffer_x = take_rows(token_rows, picks, 0)
    buffer_g = take_rows(grad_rows, picks, 0)
    buffer_w = jnp.take_along_axis(weight_of, picks, axis=1, mode="fill", fill_value=0.0)
    gate_act = jnp.einsum("ecd,edf->ecf", buffer_x, gate_weight, preferred_element_type=jnp.float32)
    up_act = jnp.einsum("ecd,edf->ecf", buffer_x, up_weight, preferred_element_type=jnp.float32)
    back_grad = jnp.einsum(
        "ecd,efd->ecf", buffer_g, down_weight, preferred_element_type=jnp.float32
    )
    sigmoid_val = jax.nn.sigmoid(gate_act)
    silu_val = gate_act * sigmoid_val
    route_grad = jnp.sum(back_grad * silu_val * up_act, axis=2)
    hidden_grad = buffer_w[:, :, None] * back_grad
    gate_grad = (
        hidden_grad * up_act * sigmoid_val * (1.0 + gate_act * (1.0 - sigmoid_val))
    ).astype(jnp.bfloat16)
    up_grad = (hidden_grad * silu_val).astype(jnp.bfloat16)
    input_grad = jnp.einsum(
        "ecf,edf->ecd", gate_grad, gate_weight, preferred_element_type=jnp.float32
    )
    input_grad = input_grad + jnp.einsum(
        "ecf,edf->ecd", up_grad, up_weight, preferred_element_type=jnp.float32
    )
    partial_value = jnp.zeros((row_total, model_width), jnp.float32)
    partial_value = partial_value.at[picks.reshape(-1)].add(
        input_grad.reshape(-1, model_width), mode="drop"
    )
    cap_grid = jnp.broadcast_to(jnp.arange(local_total, dtype=jnp.int32)[:, None], picks.shape)
    route_per = (
        jnp.zeros((local_total, row_total), jnp.float32)
        .at[cap_grid, picks]
        .add(route_grad, mode="drop")
    )
    route_rows = jnp.sum(jnp.where(matched, route_per[:, :, None], 0.0), axis=0)
    return (partial_value, route_rows)


def routed_body(tokens, cotangent, expert_ids, route_weights, gate_weight, up_weight, down_weight):
    group_total = lax.axis_size("grp")
    loc_total = lax.axis_size("loc")
    token_total = tokens.shape[0]
    model_width = tokens.shape[1]
    per_device = gate_weight.shape[0]
    per_group = per_device * loc_total
    group_cap = 6 * token_total // group_total
    expert_cap = 3 * token_total * loc_total
    device_rank = lax.axis_index("grp") * loc_total + lax.axis_index("loc")
    first_expert = device_rank * per_device
    group_ids = expert_ids // per_group
    listed = token_groups(group_ids, group_total)
    slot_range = jnp.arange(TOP, dtype=jnp.int32)[None, :]
    slot_of, sources = route_table(group_ids, group_total, group_cap)
    send_x = take_rows(tokens, sources, 0)
    send_g = take_rows(cotangent, sources, 0)
    send_ids = take_rows(expert_ids, sources, -1)
    send_w = take_rows(route_weights, sources, 0)
    recv_x, recv_g, recv_ids, recv_w = (
        lax.all_to_all(send_x, "grp", split_axis=0, concat_axis=0, tiled=True),
        lax.all_to_all(send_g, "grp", split_axis=0, concat_axis=0, tiled=True),
        lax.all_to_all(send_ids, "grp", split_axis=0, concat_axis=0, tiled=True),
        lax.all_to_all(send_w, "grp", split_axis=0, concat_axis=0, tiled=True),
    )
    row_total = group_total * group_cap
    shared_x, shared_g, shared_ids, shared_w = (
        lax.all_gather(recv_x.reshape(row_total, model_width), "loc", axis=0, tiled=True),
        lax.all_gather(recv_g.reshape(row_total, model_width), "loc", axis=0, tiled=True),
        lax.all_gather(shortened(recv_ids.reshape(row_total, TOP)), "loc", axis=0, tiled=True),
        lax.all_gather(recv_w.reshape(row_total, TOP), "loc", axis=0, tiled=True),
    )
    partial_value, route_rows = expert_pass(
        shared_x,
        shared_g,
        shared_ids,
        shared_w,
        gate_weight,
        up_weight,
        down_weight,
        first_expert,
        expert_cap,
    )
    summed, route_sum = (
        lax.psum_scatter(partial_value, "loc", scatter_dimension=0, tiled=True),
        lax.psum_scatter(route_rows, "loc", scatter_dimension=0, tiled=True),
    )
    group_part = summed.astype(jnp.bfloat16).reshape(group_total, group_cap, model_width)
    route_part = route_sum.astype(jnp.bfloat16).reshape(group_total, group_cap, TOP)
    back_terms, back_route = (
        lax.all_to_all(group_part, "grp", split_axis=0, concat_axis=0, tiled=True),
        lax.all_to_all(route_part, "grp", split_axis=0, concat_axis=0, tiled=True),
    )
    slot_pad = jnp.concatenate([slot_of, jnp.full((token_total, 1), group_cap, jnp.int32)], axis=1)
    found = jnp.take_along_axis(slot_pad, listed, axis=1)
    position = jnp.where(found < group_cap, listed * group_cap + found, row_total)
    pieces = take_rows(back_terms.reshape(row_total, model_width), position, 0)
    grad_tokens = jnp.sum(pieces.astype(jnp.float32), axis=1).astype(jnp.bfloat16)
    slot_found = jnp.take_along_axis(slot_of, group_ids, axis=1)
    route_index = (group_ids * group_cap + slot_found) * TOP + slot_range
    grad_weights = back_route.reshape(row_total * TOP)[route_index]
    return (grad_tokens, grad_weights)


LANES = 128
NT = (((1,), (1,)), ((), ()))
ANYWHERE = pl.BlockSpec(memory_space=pl.ANY)
IN_VMEM = pl.BlockSpec(memory_space=pltpu.VMEM)
IN_SMEM = pl.BlockSpec(memory_space=pltpu.SMEM)
MIB = 1024 * 1024
TOKEN = jax.ShapeDtypeStruct((8, LANES), jnp.float32)


def ring_rank(steps):
    total, rank = lax.axis_size("grp"), lax.axis_index("grp")
    half = lax.shift_right_logical(rank + 1, 1)
    place = jnp.where(lax.rem(rank, 2) == 0, half, total - half) + steps
    place = jnp.where(place >= total, place - total, place)
    return jnp.where(2 * place < total, 2 * place, 2 * (total - place) - 1)


def pack_kernel(per_group, tokens, cotangent, ids, weights, *refs):
    up_block, down_block, table_out, *orders, ids_here, weights_here, rows_here, sems = refs
    rows, width = tokens.shape
    half = lax.axis_size("grp") // 2
    small = (
        pltpu.make_async_copy(ids, ids_here, sems.at[0]),
        pltpu.make_async_copy(weights, weights_here, sems.at[1]),
    )
    large = (
        pltpu.make_async_copy(tokens, rows_here.at[:, pl.ds(0, width)], sems.at[2]),
        pltpu.make_async_copy(cotangent, rows_here.at[:, pl.ds(width, width)], sems.at[3]),
    )
    for copy in small + large:
        copy.start()
    for copy in small:
        copy.wait()
    first_experts = [ring_rank(steps) * per_group for steps in (half - 1, half + 1, half)]
    sublane = lax.broadcasted_iota(jnp.int32, (LANES, rows), 0)
    table = jnp.zeros((LANES, rows), jnp.float32)
    named = [jnp.zeros((1, rows), jnp.int32) for _ in first_experts]
    for k in range(ids.shape[0]):
        chosen = ids_here[k : k + 1, :]
        table += jnp.where(sublane == chosen, weights_here[k : k + 1, :].astype(jnp.float32), 0.0)
        named = [
            n | jnp.where((chosen >= first) & (chosen < first + per_group), 1, 0)
            for n, first in zip(named, first_experts)
        ]
    from_row = lax.broadcasted_iota(jnp.int32, (rows, rows), 0)
    to_row = lax.broadcasted_iota(jnp.int32, (rows, rows), 1)
    upper = jnp.where(from_row <= to_row, 1.0, 0.0).astype(jnp.bfloat16)
    sixteen = lax.broadcasted_iota(jnp.int32, (16, rows), 0)

    def ranks(flags):
        stacked = jnp.zeros((16, rows), jnp.float32)
        for i, flag in enumerate(flags):
            stacked = jnp.where(sixteen == i, flag.astype(jnp.float32), stacked)
        stacked = stacked.astype(jnp.bfloat16)
        counts = jnp.dot(stacked, upper, preferred_element_type=jnp.float32).astype(jnp.int32)
        totals = jnp.dot(stacked, jnp.ones_like(upper), preferred_element_type=jnp.float32).astype(jnp.int32)
        rows_of = range(len(flags))
        return [counts[i : i + 1, :] - 1 for i in rows_of], [totals[i : i + 1, :] for i in rows_of]

    up, down, across = named
    kinds = (across * up * (1 - down), across * (1 - up) * (1 - down), across * up * down, across * (1 - up) * down)
    (only_up, neither, both, only_down), (n_up, n_neither, n_both, n_down) = ranks(kinds)
    early = lax.shift_right_logical(n_neither + 1, 1)
    on_line = jnp.where(
        kinds[0] > 0,
        only_up,
        jnp.where(
            kinds[1] > 0,
            n_up + neither + jnp.where(neither < early, 0, n_both),
            jnp.where(kinds[2] > 0, n_up + early + both, n_up + n_neither + n_both + only_down),
        ),
    )
    middle = lax.shift_right_logical(n_up + n_neither + n_both + n_down + 1, 1)
    ahead = across * jnp.where(on_line < middle, 1, 0)
    firsts = (ahead, across - ahead)
    sets = []
    for first, near in zip(firsts, (up, down)):
        second = near * (1 - first)
        sets += [first, second, (1 - first) * (1 - second)]
    places, totals = ranks(sets)
    for i in range(2):
        target = jnp.where(
            sets[3 * i] > 0,
            places[3 * i],
            totals[3 * i]
            + jnp.where(sets[3 * i + 1] > 0, places[3 * i + 1], totals[3 * i + 1] + places[3 * i + 2]),
        )
        orders[i][...] = jnp.where(from_row == target, 1.0, 0.0).astype(jnp.bfloat16)
    table_out[...] = table.T.astype(jnp.bfloat16)
    blocks = up_block, down_block
    far = (sublane >= first_experts[2]) & (sublane < first_experts[2] + per_group)
    for block, order, first in zip(blocks, orders, firsts):
        mine = jnp.where(far & (first == 0), 0.0, table).astype(jnp.bfloat16)
        block[:, 2 * width :] = lax.dot_general(order[...], mine, NT, preferred_element_type=jnp.float32).astype(
            jnp.bfloat16
        )
    for copy in large:
        copy.wait()
    for block, order in zip(blocks, orders):
        for lanes in (slice(0, width), slice(width, 2 * width)):
            block[:, lanes] = jnp.dot(order[...], rows_here[:, lanes], preferred_element_type=jnp.float32).astype(
                jnp.bfloat16
            )


def pack(per_group, tokens, cotangent, ids, weights):
    rows, width = tokens.shape
    shape = (rows, 2 * width + LANES)
    order = jax.ShapeDtypeStruct((rows, rows), jnp.bfloat16)
    return pl.pallas_call(
        functools.partial(pack_kernel, per_group),
        out_shape=(
            jax.ShapeDtypeStruct(shape, jnp.bfloat16),
            jax.ShapeDtypeStruct(shape, jnp.bfloat16),
            jax.ShapeDtypeStruct((rows, LANES), jnp.bfloat16),
            order,
            order,
        ),
        in_specs=[ANYWHERE] * 4,
        out_specs=(IN_VMEM,) * 5,
        scratch_shapes=[
            pltpu.VMEM((ids.shape[1], rows), jnp.int32),
            pltpu.VMEM((ids.shape[1], rows), jnp.bfloat16),
            pltpu.VMEM((rows, 2 * width), jnp.bfloat16),
            pltpu.SemaphoreType.DMA((4,)),
        ],
        compiler_params=pltpu.CompilerParams(vmem_limit_bytes=7 * MIB),
    )(*(in_hbm(a) for a in (tokens, cotangent, ids.T, weights.T)))


def in_hbm(a):
    return pltpu.with_memory_space_constraint(a, pltpu.HBM)


def in_vmem(a):
    return pltpu.with_memory_space_constraint(a, pltpu.VMEM)


def load_kernel(after_this, gate, up, down, gate_up, back, down_back, token, down_here, sems):
    del after_this
    token[...] = jnp.zeros_like(token)
    per_device, hidden = gate.shape[0], gate.shape[2]
    copies = []
    for e in range(per_device):
        copies.append(
            (
                pltpu.make_async_copy(down.at[e], down_here.at[e], sems.at[2, e]),
                pltpu.make_async_copy(gate.at[e], gate_up.at[e, :, pl.ds(0, hidden)], sems.at[0, e]),
                pltpu.make_async_copy(up.at[e], gate_up.at[e, :, pl.ds(hidden, hidden)], sems.at[1, e]),
            )
        )
    for three in copies:
        for copy in three:
            copy.start()
    for e, (first, second, third) in enumerate(copies):
        first.wait()
        down_back[:, e * hidden : (e + 1) * hidden] = down_here[e].T
        second.wait()
        third.wait()
        back[2 * e * hidden : 2 * (e + 1) * hidden, :] = gate_up[e].T


def load(after_this, gate, up, down):
    per_device, width, hidden = gate.shape
    return pl.pallas_call(
        load_kernel,
        out_shape=(
            pltpu.VMEM((per_device, width, 2 * hidden), jnp.bfloat16),
            pltpu.VMEM((2 * per_device * hidden, width), jnp.bfloat16),
            pltpu.VMEM((width, per_device * hidden), jnp.bfloat16),
            TOKEN,
        ),
        in_specs=[ANYWHERE] * 4,
        out_specs=(IN_VMEM,) * 4,
        scratch_shapes=[pltpu.VMEM(down.shape, jnp.bfloat16), pltpu.SemaphoreType.DMA((3, per_device))],
        compiler_params=pltpu.CompilerParams(vmem_limit_bytes=8 * MIB),
        cost_estimate=pl.CostEstimate(flops=1, bytes_accessed=24 * MIB, transcendentals=0),
    )(after_this, gate, up, down)


def experts_kernel(inputs, pieces, unrolled, place, after_this, *refs):
    del after_this
    given, refs = refs[:inputs], refs[inputs:]
    loaded, refs = (refs[:3], refs[3:6]), refs[6:]
    outs, token = refs[:pieces], refs[pieces]
    token[...] = jnp.zeros_like(token)
    per_device, width, both_hidden = loaded[0][0].shape
    hidden = both_hidden // 2
    if inputs == pieces:
        x = jnp.concatenate([a[:, :width] for a in given], axis=0)
        g = jnp.concatenate([a[:, width : 2 * width] for a in given], axis=0)
        table = jnp.concatenate([a[:, 2 * width :] for a in given], axis=0)
    else:
        x, g, table = (a[...] for a in given)
    spare = -x.shape[0] % LANES
    if spare:
        x, g, table = (jnp.concatenate([a, jnp.zeros((spare, a.shape[1]), a.dtype)], axis=0) for a in (x, g, table))
    table = table.astype(jnp.float32)
    lane = lax.broadcasted_iota(jnp.int32, table.shape, 1)
    route = jnp.zeros(table.shape, jnp.float32)
    grads = []
    for pair, (gate_up, _, down_back) in enumerate(loaded):
        backs = jnp.dot(g, down_back[...], preferred_element_type=jnp.float32)
        mine = []
        for at in range(per_device):
            back = backs[:, at * hidden : (at + 1) * hidden]
            column = place[0] + lax.rem(place[1] + pair * per_device + at, 2 * per_device)
            weight = jnp.sum(jnp.where(lane == column, table, 0.0), axis=1, keepdims=True)
            both = jnp.dot(x, gate_up[at], preferred_element_type=jnp.float32)
            gate_act, up_act = both[:, :hidden], both[:, hidden:]
            sig = jax.nn.sigmoid(gate_act)
            silu = gate_act * sig
            back_up = back * up_act
            route_grad = jnp.sum(back_up * silu, axis=1, keepdims=True)
            mine.append((weight * back_up * sig * (1.0 + gate_act * (1.0 - sig))).astype(jnp.bfloat16))
            mine.append((weight * back * silu).astype(jnp.bfloat16))
            route += jnp.where((lane == column) & (weight > 0.0), route_grad, 0.0)
        grads.append(jnp.concatenate(mine, axis=1))
    step = 4 * LANES

    def chunk(i, carry):
        part = pl.ds(pl.multiple_of(i * step, step), step)
        total = sum(
            jnp.dot(a, back[:, part], preferred_element_type=jnp.float32) for a, (_, back, _) in zip(grads, loaded)
        ).astype(jnp.bfloat16)
        start = 0
        for out in outs:
            out[:, part] = total[start : start + out.shape[0]]
            start += out.shape[0]
        return carry

    lax.fori_loop(0, width // step, chunk, 0, unroll=unrolled)
    start = 0
    for out in outs:
        out[:, width:] = route[start : start + out.shape[0]].astype(out.dtype)
        start += out.shape[0]


def experts_call(place, after_this, given, rows, loaded, unrolled):
    width = loaded[0].shape[1]
    return pl.pallas_call(
        functools.partial(experts_kernel, len(given), len(rows), unrolled),
        out_shape=[jax.ShapeDtypeStruct((r, width + LANES), jnp.bfloat16) for r in rows] + [TOKEN],
        in_specs=[IN_SMEM, ANYWHERE] + [IN_VMEM] * (len(given) + 6),
        out_specs=[IN_VMEM] * (len(rows) + 1),
        compiler_params=pltpu.CompilerParams(vmem_limit_bytes=12 * MIB),
        cost_estimate=pl.CostEstimate(flops=1, bytes_accessed=1, transcendentals=0),
    )(place, after_this, *(in_vmem(a) for a in given), *loaded)


def finish_kernel(ids, order_up, order_down, mine, long_up, short_up, long_down, short_down, grad_tokens, grad_weights):
    width = grad_tokens.shape[1]
    backs = order_up[...].T, order_down[...].T
    came = tuple(jnp.concatenate([a[...], b[...]], axis=0) for a, b in ((long_up, short_up), (long_down, short_down)))
    summed = mine[...].astype(jnp.float32)
    for back, rows in zip(backs, came):
        summed += jnp.dot(back, rows, preferred_element_type=jnp.float32)
    grad_tokens[...] = summed[:, :width].astype(grad_tokens.dtype)
    route = summed[:, width:].T
    expert = lax.broadcasted_iota(jnp.int32, route.shape, 0)
    found = [
        jnp.sum(jnp.where(expert == ids[k : k + 1, :], route, 0.0), axis=0, keepdims=True) for k in range(ids.shape[0])
    ]
    grad_weights[...] = jnp.concatenate(found, axis=0).astype(grad_weights.dtype)


def finish(ids, terms, width):
    rows, top = ids.shape
    grad_tokens, grad_weights = pl.pallas_call(
        finish_kernel,
        out_shape=(
            jax.ShapeDtypeStruct((rows, width), jnp.bfloat16),
            jax.ShapeDtypeStruct((top, rows), jnp.bfloat16),
        ),
        in_specs=[IN_VMEM] * 8,
        out_specs=(IN_VMEM, IN_VMEM),
        compiler_params=pltpu.CompilerParams(vmem_limit_bytes=12 * MIB),
    )(ids.T, *terms)
    return grad_tokens, grad_weights.T


def add_kernel(a, b, out):
    rows = b.shape[0]
    if rows < a.shape[0]:
        out[rows:, :] = a[rows:, :]
    out[:rows, :] = (a[:rows, :].astype(jnp.float32) + b[...].astype(jnp.float32)).astype(out.dtype)


def added(a, b):
    return pl.pallas_call(
        add_kernel,
        out_shape=jax.ShapeDtypeStruct(a.shape, a.dtype),
        in_specs=[IN_VMEM] * 2,
        out_specs=IN_VMEM,
        compiler_params=pltpu.CompilerParams(vmem_limit_bytes=8 * MIB),
        cost_estimate=pl.CostEstimate(flops=1, bytes_accessed=1, transcendentals=0),
    )(a, b)


def ring_body(tokens, cotangent, expert_ids, route_weights, gate_weight, up_weight, down_weight):
    ring_total = lax.axis_size("grp")
    loc_total = lax.axis_size("loc")
    width = tokens.shape[1]
    per_device = gate_weight.shape[0]
    order = list(range(0, ring_total, 2)) + list(range(ring_total - 1, 0, -2))
    ahead = [(order[i], order[(i + 1) % ring_total]) for i in range(ring_total)]
    behind = [(b, a) for a, b in ahead]
    rank, loc = lax.axis_index("grp"), lax.axis_index("loc")

    def send(pair):
        return lax.ppermute(pair[0], "grp", ahead), lax.ppermute(pair[1], "grp", behind)

    def send_back(pair):
        return lax.ppermute(pair[0], "grp", behind), lax.ppermute(pair[1], "grp", ahead)

    def tie(pair, *others):
        return tuple(lax.optimization_barrier((a, *others))[0] for a in pair)

    own = (gate_weight, up_weight, down_weight)
    other = [lax.ppermute(a, "loc", [(i, loc_total - 1 - i) for i in range(loc_total)]) for a in own]
    per_group = loc_total * per_device
    place = jnp.stack([rank * per_group, loc * per_device]).astype(jnp.int32)
    *blocks, table, order_up, order_down = pack(per_group, tokens, cotangent, expert_ids, route_weights)
    came = send(blocks)
    *loaded, loaded_own = load(place, *(in_hbm(a) for a in own))
    *others, last = load(loaded_own, *tie(other[:2], *came), other[2])
    loaded += others

    def call(after_this, *packed, unrolled=False):
        rows = [a.shape[0] for a in packed]
        *parts, token = experts_call(place, after_this, packed, rows, loaded, unrolled)
        return parts, token

    block = tokens.shape[0]
    half, most = ring_total // 2, 6 * block // ring_total
    cut, last_short = most // 2, block // 2

    def split(pair):
        return [a[:cut] for a in pair], [a[cut:] for a in pair]

    long, short = split(came)
    long_next, short_next = send(tie(long, loaded_own, *other)), send(tie(short, loaded_own, *other))
    mine, last = experts_call(place, last, (tokens, cotangent, table), tokens.shape[:1], loaded, False)
    filler = last
    parts, last = call(last, *came)
    ahead_terms, behind_terms = split(parts)
    long_terms, short_terms = [None, ahead_terms], [None, behind_terms]
    for s in range(2, half - 1):
        long, short = long_next, short_next
        long_next = send(tie(long, filler))
        short_next = send(tie([a[:last_short] for a in short] if s + 2 == half else short, last))
        parts, last = call(last, long[0], short[0], long[1], short[1])
        long_terms.append((parts[0], parts[2]))
        short_terms.append((parts[1], parts[3]))
    long, short = long_next, short_next
    parts, last = call(last, *short)
    long_last = send(tie(long, last))
    short_back = send_back(parts)
    parts, last = call(last, *long)
    long_terms.append(tuple(parts))
    parts, last = call(last, *long_last, unrolled=True)
    long_back = send_back(tie(parts, *short_back))
    for s in range(half - 1, 0, -1):
        if s < half - 1:
            short_back = send_back([added(a, b) for a, b in zip(short_terms[s], short_back)])
        long_back = send_back([added(a, b) for a, b in zip(long_terms[s], long_back)])
    terms = (order_up, order_down, mine, long_back[0], short_back[0], long_back[1], short_back[1])
    return finish(expert_ids, terms, width)


def body(tokens, cotangent, expert_ids, route_weights, gate_weight, up_weight, down_weight):
    args = (tokens, cotangent, expert_ids, route_weights, gate_weight, up_weight, down_weight)
    ring_total, loc_total = lax.axis_size("grp"), lax.axis_size("loc")
    experts = ring_total * loc_total * gate_weight.shape[0]
    if loc_total == 2 and ring_total == 8 and experts <= LANES and tokens.shape[0] % 32 == 0:
        return ring_body(*args)
    return routed_body(*args)


def solution(mesh):
    placed = (
        P(("rep", "grp", "loc"), None),
        P(("rep", "grp", "loc"), None),
        P(("rep", "grp", "loc"), None),
        P(("rep", "grp", "loc"), None),
        P(("grp", "loc"), None, None),
        P(("grp", "loc"), None, None),
        P(("grp", "loc"), None, None),
    )
    return jax.shard_map(
        body,
        mesh=mesh,
        in_specs=placed,
        out_specs=(P(("rep", "grp", "loc"), None), P(("rep", "grp", "loc"), None)),
        check_vma=False,
    )
```

```python
import functools

import jax
import jax.numpy as jnp
from jax import lax
from jax.experimental import pallas as pl
from jax.experimental.pallas import tpu as pltpu
from jax.sharding import PartitionSpec as P

TOP = 8
TOP_GROUPS = 4


def shortened(shard):
    return jax.tree.map(lambda a: a.astype(jnp.bfloat16) if a.dtype == jnp.float32 else a, shard)


def take_rows(values, indices, filler):
    return jnp.take(values, indices, axis=0, mode="fill", fill_value=filler)


def route_table(targets, dest_total, capacity):
    token_total = targets.shape[0]
    dest_iota = jnp.arange(dest_total, dtype=jnp.int32)
    reached = jnp.any(targets[:, :, None] == dest_iota[None, None, :], axis=1)
    ranked = jnp.cumsum(reached.astype(jnp.int32), axis=0) - 1
    slot_of = jnp.where(reached, ranked, capacity)
    dest_grid = jnp.broadcast_to(dest_iota[None, :], slot_of.shape)
    token_grid = jnp.broadcast_to(jnp.arange(token_total, dtype=jnp.int32)[:, None], slot_of.shape)
    sources = jnp.full((dest_total, capacity), token_total, jnp.int32)
    sources = sources.at[dest_grid, slot_of].set(token_grid, mode="drop")
    return (slot_of, sources)


def token_groups(group_ids, group_total):
    token_total = group_ids.shape[0]
    group_iota = jnp.arange(group_total, dtype=jnp.int32)
    reached = jnp.any(group_ids[:, :, None] == group_iota[None, None, :], axis=1)
    ranked = jnp.cumsum(reached.astype(jnp.int32), axis=1) - 1
    column = jnp.where(reached, ranked, TOP_GROUPS)
    token_grid = jnp.broadcast_to(jnp.arange(token_total, dtype=jnp.int32)[:, None], column.shape)
    listed = jnp.full((token_total, TOP_GROUPS), group_total, jnp.int32)
    return listed.at[token_grid, column].set(
        jnp.broadcast_to(group_iota[None, :], column.shape), mode="drop"
    )


def expert_pass(
    token_rows,
    grad_rows,
    id_rows,
    weight_rows,
    gate_weight,
    up_weight,
    down_weight,
    first_expert,
    capacity,
):
    row_total = token_rows.shape[0]
    local_total = gate_weight.shape[0]
    model_width = token_rows.shape[1]
    experts_here = first_expert + jnp.arange(local_total, dtype=jnp.int32)
    matched = id_rows[None, :, :] == experts_here[:, None, None]
    chosen = jnp.any(matched, axis=2)
    weight_of = jnp.sum(
        jnp.where(matched, weight_rows.astype(jnp.float32)[None, :, :], 0.0), axis=2
    )
    ranked = jnp.cumsum(chosen.astype(jnp.int32), axis=1) - 1
    slot_of = jnp.where(chosen, ranked, capacity)
    expert_grid = jnp.broadcast_to(jnp.arange(local_total, dtype=jnp.int32)[:, None], slot_of.shape)
    row_grid = jnp.broadcast_to(jnp.arange(row_total, dtype=jnp.int32)[None, :], slot_of.shape)
    picks = (
        jnp.full((local_total, capacity), row_total, jnp.int32)
        .at[expert_grid, slot_of]
        .set(row_grid, mode="drop")
    )
    buffer_x = take_rows(token_rows, picks, 0)
    buffer_g = take_rows(grad_rows, picks, 0)
    buffer_w = jnp.take_along_axis(weight_of, picks, axis=1, mode="fill", fill_value=0.0)
    gate_act = jnp.einsum("ecd,edf->ecf", buffer_x, gate_weight, preferred_element_type=jnp.float32)
    up_act = jnp.einsum("ecd,edf->ecf", buffer_x, up_weight, preferred_element_type=jnp.float32)
    back_grad = jnp.einsum(
        "ecd,efd->ecf", buffer_g, down_weight, preferred_element_type=jnp.float32
    )
    sigmoid_val = jax.nn.sigmoid(gate_act)
    silu_val = gate_act * sigmoid_val
    route_grad = jnp.sum(back_grad * silu_val * up_act, axis=2)
    hidden_grad = buffer_w[:, :, None] * back_grad
    gate_grad = (
        hidden_grad * up_act * sigmoid_val * (1.0 + gate_act * (1.0 - sigmoid_val))
    ).astype(jnp.bfloat16)
    up_grad = (hidden_grad * silu_val).astype(jnp.bfloat16)
    input_grad = jnp.einsum(
        "ecf,edf->ecd", gate_grad, gate_weight, preferred_element_type=jnp.float32
    )
    input_grad = input_grad + jnp.einsum(
        "ecf,edf->ecd", up_grad, up_weight, preferred_element_type=jnp.float32
    )
    partial_value = jnp.zeros((row_total, model_width), jnp.float32)
    partial_value = partial_value.at[picks.reshape(-1)].add(
        input_grad.reshape(-1, model_width), mode="drop"
    )
    cap_grid = jnp.broadcast_to(jnp.arange(local_total, dtype=jnp.int32)[:, None], picks.shape)
    route_per = (
        jnp.zeros((local_total, row_total), jnp.float32)
        .at[cap_grid, picks]
        .add(route_grad, mode="drop")
    )
    route_rows = jnp.sum(jnp.where(matched, route_per[:, :, None], 0.0), axis=0)
    return (partial_value, route_rows)


def routed_body(tokens, cotangent, expert_ids, route_weights, gate_weight, up_weight, down_weight):
    group_total = lax.axis_size("grp")
    loc_total = lax.axis_size("loc")
    token_total = tokens.shape[0]
    model_width = tokens.shape[1]
    per_device = gate_weight.shape[0]
    per_group = per_device * loc_total
    group_cap = 6 * token_total // group_total
    expert_cap = 3 * token_total * loc_total
    device_rank = lax.axis_index("grp") * loc_total + lax.axis_index("loc")
    first_expert = device_rank * per_device
    group_ids = expert_ids // per_group
    listed = token_groups(group_ids, group_total)
    slot_range = jnp.arange(TOP, dtype=jnp.int32)[None, :]
    slot_of, sources = route_table(group_ids, group_total, group_cap)
    send_x = take_rows(tokens, sources, 0)
    send_g = take_rows(cotangent, sources, 0)
    send_ids = take_rows(expert_ids, sources, -1)
    send_w = take_rows(route_weights, sources, 0)
    recv_x, recv_g, recv_ids, recv_w = (
        lax.all_to_all(send_x, "grp", split_axis=0, concat_axis=0, tiled=True),
        lax.all_to_all(send_g, "grp", split_axis=0, concat_axis=0, tiled=True),
        lax.all_to_all(send_ids, "grp", split_axis=0, concat_axis=0, tiled=True),
        lax.all_to_all(send_w, "grp", split_axis=0, concat_axis=0, tiled=True),
    )
    row_total = group_total * group_cap
    shared_x, shared_g, shared_ids, shared_w = (
        lax.all_gather(recv_x.reshape(row_total, model_width), "loc", axis=0, tiled=True),
        lax.all_gather(recv_g.reshape(row_total, model_width), "loc", axis=0, tiled=True),
        lax.all_gather(shortened(recv_ids.reshape(row_total, TOP)), "loc", axis=0, tiled=True),
        lax.all_gather(recv_w.reshape(row_total, TOP), "loc", axis=0, tiled=True),
    )
    partial_value, route_rows = expert_pass(
        shared_x,
        shared_g,
        shared_ids,
        shared_w,
        gate_weight,
        up_weight,
        down_weight,
        first_expert,
        expert_cap,
    )
    summed, route_sum = (
        lax.psum_scatter(partial_value, "loc", scatter_dimension=0, tiled=True),
        lax.psum_scatter(route_rows, "loc", scatter_dimension=0, tiled=True),
    )
    group_part = summed.astype(jnp.bfloat16).reshape(group_total, group_cap, model_width)
    route_part = route_sum.astype(jnp.bfloat16).reshape(group_total, group_cap, TOP)
    back_terms, back_route = (
        lax.all_to_all(group_part, "grp", split_axis=0, concat_axis=0, tiled=True),
        lax.all_to_all(route_part, "grp", split_axis=0, concat_axis=0, tiled=True),
    )
    slot_pad = jnp.concatenate([slot_of, jnp.full((token_total, 1), group_cap, jnp.int32)], axis=1)
    found = jnp.take_along_axis(slot_pad, listed, axis=1)
    position = jnp.where(found < group_cap, listed * group_cap + found, row_total)
    pieces = take_rows(back_terms.reshape(row_total, model_width), position, 0)
    grad_tokens = jnp.sum(pieces.astype(jnp.float32), axis=1).astype(jnp.bfloat16)
    slot_found = jnp.take_along_axis(slot_of, group_ids, axis=1)
    route_index = (group_ids * group_cap + slot_found) * TOP + slot_range
    grad_weights = back_route.reshape(row_total * TOP)[route_index]
    return (grad_tokens, grad_weights)


LANES = 128
NT = (((1,), (1,)), ((), ()))
ANYWHERE = pl.BlockSpec(memory_space=pl.ANY)
IN_VMEM = pl.BlockSpec(memory_space=pltpu.VMEM)
IN_SMEM = pl.BlockSpec(memory_space=pltpu.SMEM)
MIB = 1024 * 1024
TOKEN = jax.ShapeDtypeStruct((8, LANES), jnp.float32)


def ring_rank(steps):
    total, rank = lax.axis_size("grp"), lax.axis_index("grp")
    half = lax.shift_right_logical(rank + 1, 1)
    place = jnp.where(lax.rem(rank, 2) == 0, half, total - half) + steps
    place = jnp.where(place >= total, place - total, place)
    return jnp.where(2 * place < total, 2 * place, 2 * (total - place) - 1)


def pack_kernel(per_group, tokens, cotangent, ids, weights, *refs):
    up_block, down_block, table_out, *orders, ids_here, weights_here, rows_here, sems = refs
    rows, width = tokens.shape
    half = lax.axis_size("grp") // 2
    small = (
        pltpu.make_async_copy(ids, ids_here, sems.at[0]),
        pltpu.make_async_copy(weights, weights_here, sems.at[1]),
    )
    large = (
        pltpu.make_async_copy(tokens, rows_here.at[:, pl.ds(0, width)], sems.at[2]),
        pltpu.make_async_copy(cotangent, rows_here.at[:, pl.ds(width, width)], sems.at[3]),
    )
    for copy in small + large:
        copy.start()
    for copy in small:
        copy.wait()
    first_experts = [ring_rank(steps) * per_group for steps in (half - 1, half + 1, half)]
    sublane = lax.broadcasted_iota(jnp.int32, (LANES, rows), 0)
    table = jnp.zeros((LANES, rows), jnp.float32)
    named = [jnp.zeros((1, rows), jnp.int32) for _ in first_experts]
    for k in range(ids.shape[0]):
        chosen = ids_here[k : k + 1, :]
        table += jnp.where(sublane == chosen, weights_here[k : k + 1, :].astype(jnp.float32), 0.0)
        named = [
            n | jnp.where((chosen >= first) & (chosen < first + per_group), 1, 0)
            for n, first in zip(named, first_experts)
        ]
    from_row = lax.broadcasted_iota(jnp.int32, (rows, rows), 0)
    to_row = lax.broadcasted_iota(jnp.int32, (rows, rows), 1)
    upper = jnp.where(from_row <= to_row, 1.0, 0.0).astype(jnp.bfloat16)
    sixteen = lax.broadcasted_iota(jnp.int32, (16, rows), 0)

    def ranks(flags):
        stacked = jnp.zeros((16, rows), jnp.float32)
        for i, flag in enumerate(flags):
            stacked = jnp.where(sixteen == i, flag.astype(jnp.float32), stacked)
        stacked = stacked.astype(jnp.bfloat16)
        counts = jnp.dot(stacked, upper, preferred_element_type=jnp.float32).astype(jnp.int32)
        totals = jnp.dot(stacked, jnp.ones_like(upper), preferred_element_type=jnp.float32).astype(jnp.int32)
        rows_of = range(len(flags))
        return [counts[i : i + 1, :] - 1 for i in rows_of], [totals[i : i + 1, :] for i in rows_of]

    up, down, across = named
    kinds = (across * up * (1 - down), across * (1 - up) * (1 - down), across * up * down, across * (1 - up) * down)
    (only_up, neither, both, only_down), (n_up, n_neither, n_both, n_down) = ranks(kinds)
    early = lax.shift_right_logical(n_neither + 1, 1)
    on_line = jnp.where(
        kinds[0] > 0,
        only_up,
        jnp.where(
            kinds[1] > 0,
            n_up + neither + jnp.where(neither < early, 0, n_both),
            jnp.where(kinds[2] > 0, n_up + early + both, n_up + n_neither + n_both + only_down),
        ),
    )
    middle = lax.shift_right_logical(n_up + n_neither + n_both + n_down + 1, 1)
    ahead = across * jnp.where(on_line < middle, 1, 0)
    firsts = (ahead, across - ahead)
    sets = []
    for first, near in zip(firsts, (up, down)):
        second = near * (1 - first)
        sets += [first, second, (1 - first) * (1 - second)]
    places, totals = ranks(sets)
    for i in range(2):
        target = jnp.where(
            sets[3 * i] > 0,
            places[3 * i],
            totals[3 * i]
            + jnp.where(sets[3 * i + 1] > 0, places[3 * i + 1], totals[3 * i + 1] + places[3 * i + 2]),
        )
        orders[i][...] = jnp.where(from_row == target, 1.0, 0.0).astype(jnp.bfloat16)
    table_out[...] = table.T.astype(jnp.bfloat16)
    blocks = up_block, down_block
    far = (sublane >= first_experts[2]) & (sublane < first_experts[2] + per_group)
    for block, order, first in zip(blocks, orders, firsts):
        mine = jnp.where(far & (first == 0), 0.0, table).astype(jnp.bfloat16)
        block[:, 2 * width :] = lax.dot_general(order[...], mine, NT, preferred_element_type=jnp.float32).astype(
            jnp.bfloat16
        )
    for copy in large:
        copy.wait()
    for block, order in zip(blocks, orders):
        for lanes in (slice(0, width), slice(width, 2 * width)):
            block[:, lanes] = jnp.dot(order[...], rows_here[:, lanes], preferred_element_type=jnp.float32).astype(
                jnp.bfloat16
            )


def pack(per_group, tokens, cotangent, ids, weights):
    rows, width = tokens.shape
    shape = (rows, 2 * width + LANES)
    order = jax.ShapeDtypeStruct((rows, rows), jnp.bfloat16)
    return pl.pallas_call(
        functools.partial(pack_kernel, per_group),
        out_shape=(
            jax.ShapeDtypeStruct(shape, jnp.bfloat16),
            jax.ShapeDtypeStruct(shape, jnp.bfloat16),
            jax.ShapeDtypeStruct((rows, LANES), jnp.bfloat16),
            order,
            order,
        ),
        in_specs=[ANYWHERE] * 4,
        out_specs=(IN_VMEM,) * 5,
        scratch_shapes=[
            pltpu.VMEM((ids.shape[1], rows), jnp.int32),
            pltpu.VMEM((ids.shape[1], rows), jnp.bfloat16),
            pltpu.VMEM((rows, 2 * width), jnp.bfloat16),
            pltpu.SemaphoreType.DMA((4,)),
        ],
        compiler_params=pltpu.CompilerParams(vmem_limit_bytes=7 * MIB),
    )(*(in_hbm(a) for a in (tokens, cotangent, ids.T, weights.T)))


def in_hbm(a):
    return pltpu.with_memory_space_constraint(a, pltpu.HBM)


def in_vmem(a):
    return pltpu.with_memory_space_constraint(a, pltpu.VMEM)


def load_kernel(after_this, gate, up, down, gate_up, back, down_back, token, down_here, sems):
    del after_this
    token[...] = jnp.zeros_like(token)
    per_device, hidden = gate.shape[0], gate.shape[2]
    copies = []
    for e in range(per_device):
        copies.append(
            (
                pltpu.make_async_copy(down.at[e], down_here.at[e], sems.at[2, e]),
                pltpu.make_async_copy(gate.at[e], gate_up.at[e, :, pl.ds(0, hidden)], sems.at[0, e]),
                pltpu.make_async_copy(up.at[e], gate_up.at[e, :, pl.ds(hidden, hidden)], sems.at[1, e]),
            )
        )
    for three in copies:
        for copy in three:
            copy.start()
    for e, (first, second, third) in enumerate(copies):
        first.wait()
        down_back[:, e * hidden : (e + 1) * hidden] = down_here[e].T
        second.wait()
        third.wait()
        back[2 * e * hidden : 2 * (e + 1) * hidden, :] = gate_up[e].T


def load(after_this, gate, up, down):
    per_device, width, hidden = gate.shape
    return pl.pallas_call(
        load_kernel,
        out_shape=(
            pltpu.VMEM((per_device, width, 2 * hidden), jnp.bfloat16),
            pltpu.VMEM((2 * per_device * hidden, width), jnp.bfloat16),
            pltpu.VMEM((width, per_device * hidden), jnp.bfloat16),
            TOKEN,
        ),
        in_specs=[ANYWHERE] * 4,
        out_specs=(IN_VMEM,) * 4,
        scratch_shapes=[pltpu.VMEM(down.shape, jnp.bfloat16), pltpu.SemaphoreType.DMA((3, per_device))],
        compiler_params=pltpu.CompilerParams(vmem_limit_bytes=8 * MIB),
        cost_estimate=pl.CostEstimate(flops=1, bytes_accessed=24 * MIB, transcendentals=0),
    )(after_this, gate, up, down)


def experts_kernel(inputs, pieces, unrolled, place, after_this, *refs):
    del after_this
    given, refs = refs[:inputs], refs[inputs:]
    loaded, refs = (refs[:3], refs[3:6]), refs[6:]
    outs, token = refs[:pieces], refs[pieces]
    token[...] = jnp.zeros_like(token)
    per_device, width, both_hidden = loaded[0][0].shape
    hidden = both_hidden // 2
    if given[0].shape[1] > width:
        x = jnp.concatenate([a[:, :width] for a in given], axis=0)
        g = jnp.concatenate([a[:, width : 2 * width] for a in given], axis=0)
        table = jnp.concatenate([a[:, 2 * width :] for a in given], axis=0)
    else:
        x, g, table = (a[...] for a in given)
    spare = -x.shape[0] % (LANES // 2)
    if spare:
        x, g, table = (jnp.concatenate([a, jnp.zeros((spare, a.shape[1]), a.dtype)], axis=0) for a in (x, g, table))
    table = table.astype(jnp.float32)
    lane = lax.broadcasted_iota(jnp.int32, table.shape, 1)
    route = jnp.zeros(table.shape, jnp.float32)
    grads = []
    for pair, (gate_up, _, down_back) in enumerate(loaded):
        backs = jnp.dot(g, down_back[...], preferred_element_type=jnp.float32)
        mine = []
        for at in range(per_device):
            back = backs[:, at * hidden : (at + 1) * hidden]
            column = place[0] + lax.rem(place[1] + pair * per_device + at, 2 * per_device)
            weight = jnp.sum(jnp.where(lane == column, table, 0.0), axis=1, keepdims=True)
            both = jnp.dot(x, gate_up[at], preferred_element_type=jnp.float32)
            gate_act, up_act = both[:, :hidden], both[:, hidden:]
            sig = jax.nn.sigmoid(gate_act)
            silu = gate_act * sig
            back_up = back * up_act
            route_grad = jnp.sum(back_up * silu, axis=1, keepdims=True)
            mine.append((weight * back_up * sig * (1.0 + gate_act * (1.0 - sig))).astype(jnp.bfloat16))
            mine.append((weight * back * silu).astype(jnp.bfloat16))
            route += jnp.where((lane == column) & (weight > 0.0), route_grad, 0.0)
        grads.append(jnp.concatenate(mine, axis=1))
    step = 4 * LANES

    def chunk(i, carry):
        part = pl.ds(pl.multiple_of(i * step, step), step)
        total = sum(
            jnp.dot(a, back[:, part], preferred_element_type=jnp.float32) for a, (_, back, _) in zip(grads, loaded)
        ).astype(jnp.bfloat16)
        start = 0
        for out in outs:
            out[:, part] = total[start : start + out.shape[0]]
            start += out.shape[0]
        return carry

    lax.fori_loop(0, width // step, chunk, 0, unroll=unrolled)
    start = 0
    for out in outs:
        out[:, width:] = route[start : start + out.shape[0]].astype(out.dtype)
        start += out.shape[0]


def experts_call(place, after_this, given, rows, loaded, unrolled):
    width = loaded[0].shape[1]
    return pl.pallas_call(
        functools.partial(experts_kernel, len(given), len(rows), unrolled),
        out_shape=[jax.ShapeDtypeStruct((r, width + LANES), jnp.bfloat16) for r in rows] + [TOKEN],
        in_specs=[IN_SMEM, ANYWHERE] + [IN_VMEM] * (len(given) + 6),
        out_specs=[IN_VMEM] * (len(rows) + 1),
        compiler_params=pltpu.CompilerParams(vmem_limit_bytes=12 * MIB),
        cost_estimate=pl.CostEstimate(flops=1, bytes_accessed=1, transcendentals=0),
    )(place, after_this, *(in_vmem(a) for a in given), *loaded)


def finish_kernel(ids, order_up, order_down, mine, long_up, short_up, long_down, short_down, grad_tokens, grad_weights):
    width = grad_tokens.shape[1]
    backs = order_up[...].T, order_down[...].T
    came = tuple(jnp.concatenate([a[...], b[...]], axis=0) for a, b in ((long_up, short_up), (long_down, short_down)))
    summed = mine[...].astype(jnp.float32)
    for back, rows in zip(backs, came):
        summed += jnp.dot(back, rows, preferred_element_type=jnp.float32)
    grad_tokens[...] = summed[:, :width].astype(grad_tokens.dtype)
    route = summed[:, width:].T
    expert = lax.broadcasted_iota(jnp.int32, route.shape, 0)
    found = [
        jnp.sum(jnp.where(expert == ids[k : k + 1, :], route, 0.0), axis=0, keepdims=True) for k in range(ids.shape[0])
    ]
    grad_weights[...] = jnp.concatenate(found, axis=0).astype(grad_weights.dtype)


def finish(ids, terms, width):
    rows, top = ids.shape
    grad_tokens, grad_weights = pl.pallas_call(
        finish_kernel,
        out_shape=(
            jax.ShapeDtypeStruct((rows, width), jnp.bfloat16),
            jax.ShapeDtypeStruct((top, rows), jnp.bfloat16),
        ),
        in_specs=[IN_VMEM] * 8,
        out_specs=(IN_VMEM, IN_VMEM),
        compiler_params=pltpu.CompilerParams(vmem_limit_bytes=12 * MIB),
    )(ids.T, *terms)
    return grad_tokens, grad_weights.T


def add_kernel(a, b, out):
    rows = b.shape[0]
    if rows < a.shape[0]:
        out[rows:, :] = a[rows:, :]
    out[:rows, :] = (a[:rows, :].astype(jnp.float32) + b[...].astype(jnp.float32)).astype(out.dtype)


def join_kernel(a, b, out):
    rows = a.shape[0]
    out[:rows, :] = a[...]
    out[rows:, :] = b[...]


def joined(a, b):
    return pl.pallas_call(
        join_kernel,
        out_shape=jax.ShapeDtypeStruct((a.shape[0] + b.shape[0], a.shape[1]), a.dtype),
        in_specs=[IN_VMEM] * 2,
        out_specs=IN_VMEM,
        compiler_params=pltpu.CompilerParams(vmem_limit_bytes=8 * MIB),
        cost_estimate=pl.CostEstimate(flops=1, bytes_accessed=1, transcendentals=0),
    )(a, b)


def added(a, b):
    return pl.pallas_call(
        add_kernel,
        out_shape=jax.ShapeDtypeStruct(a.shape, a.dtype),
        in_specs=[IN_VMEM] * 2,
        out_specs=IN_VMEM,
        compiler_params=pltpu.CompilerParams(vmem_limit_bytes=8 * MIB),
        cost_estimate=pl.CostEstimate(flops=1, bytes_accessed=1, transcendentals=0),
    )(a, b)


def ring_body(tokens, cotangent, expert_ids, route_weights, gate_weight, up_weight, down_weight):
    ring_total = lax.axis_size("grp")
    loc_total = lax.axis_size("loc")
    width = tokens.shape[1]
    per_device = gate_weight.shape[0]
    order = list(range(0, ring_total, 2)) + list(range(ring_total - 1, 0, -2))
    ahead = [(order[i], order[(i + 1) % ring_total]) for i in range(ring_total)]
    behind = [(b, a) for a, b in ahead]
    rank, loc = lax.axis_index("grp"), lax.axis_index("loc")

    def send(pair):
        return lax.ppermute(pair[0], "grp", ahead), lax.ppermute(pair[1], "grp", behind)

    def send_back(pair):
        return lax.ppermute(pair[0], "grp", behind), lax.ppermute(pair[1], "grp", ahead)

    def tie(pair, *others):
        return tuple(lax.optimization_barrier((a, *others))[0] for a in pair)

    own = (gate_weight, up_weight, down_weight)
    other = [lax.ppermute(a, "loc", [(i, loc_total - 1 - i) for i in range(loc_total)]) for a in own]
    per_group = loc_total * per_device
    place = jnp.stack([rank * per_group, loc * per_device]).astype(jnp.int32)
    *blocks, table, order_up, order_down = pack(per_group, tokens, cotangent, expert_ids, route_weights)
    came = send(blocks)
    *loaded, loaded_own = load(place, *(in_hbm(a) for a in own))
    *others, last = load(loaded_own, *tie(other[:2], *came), other[2])
    loaded += others

    def call(after_this, rows, *packed, unrolled=False):
        *parts, token = experts_call(place, after_this, packed, rows, loaded, unrolled)
        return parts, token

    block = tokens.shape[0]
    half, most = ring_total // 2, 6 * block // ring_total
    half_block, cut = block // 2, most // 2
    rest, needed = block - cut, (block + most) // 2 - half_block
    long, short = [a[:half_block] for a in came], [a[half_block:] for a in came]
    long_next, short_next = send(tie(long, loaded_own, *other)), send(tie(short, loaded_own, *other))
    mine, last = experts_call(place, last, (tokens, cotangent, table), tokens.shape[:1], loaded, False)
    filler = last
    parts, last = call(last, (block, block), *came)
    long_terms, short_terms = [None, [a[:cut] for a in parts]], [None, [a[cut:] for a in parts]]
    for s in range(2, half - 1):
        long, short = long_next, short_next
        long_next = send(tie(long, filler))
        short_next = send(tie([a[:needed] for a in short] if s + 2 == half else short, last))
        parts, last = call(last, (cut, rest, cut, rest), long[0], short[0], long[1], short[1])
        long_terms.append((parts[0], parts[2]))
        short_terms.append((parts[1], parts[3]))
    long, short = long_next, short_next
    long_last = send(tie([a[:cut] for a in long], last))
    parts, last = call(last, (cut, half_block - cut) * 2, *long)
    long_terms.append((parts[0], parts[2]))
    lower = parts[1], parts[3]
    parts, last = call(last, (needed, needed), *short, unrolled=True)
    short_back = send_back([joined(a, b) for a, b in zip(lower, parts)])
    parts, last = call(last, (cut, cut), *long_last, unrolled=True)
    long_back = send_back(tie(parts, *short_back))
    for s in range(half - 1, 0, -1):
        if s < half - 1:
            short_back = send_back([added(a, b) for a, b in zip(short_terms[s], short_back)])
        long_back = send_back([added(a, b) for a, b in zip(long_terms[s], long_back)])
    terms = (order_up, order_down, mine, long_back[0], short_back[0], long_back[1], short_back[1])
    return finish(expert_ids, terms, width)


def body(tokens, cotangent, expert_ids, route_weights, gate_weight, up_weight, down_weight):
    args = (tokens, cotangent, expert_ids, route_weights, gate_weight, up_weight, down_weight)
    ring_total, loc_total = lax.axis_size("grp"), lax.axis_size("loc")
    experts = ring_total * loc_total * gate_weight.shape[0]
    if loc_total == 2 and ring_total == 8 and experts <= LANES and tokens.shape[0] % 32 == 0:
        return ring_body(*args)
    return routed_body(*args)


def solution(mesh):
    placed = (
        P(("rep", "grp", "loc"), None),
        P(("rep", "grp", "loc"), None),
        P(("rep", "grp", "loc"), None),
        P(("rep", "grp", "loc"), None),
        P(("grp", "loc"), None, None),
        P(("grp", "loc"), None, None),
        P(("grp", "loc"), None, None),
    )
    return jax.shard_map(
        body,
        mesh=mesh,
        in_specs=placed,
        out_specs=(P(("rep", "grp", "loc"), None), P(("rep", "grp", "loc"), None)),
        check_vma=False,
    )
```

```python
import functools

import jax
import jax.numpy as jnp
from jax import lax
from jax.experimental import pallas as pl
from jax.experimental.pallas import tpu as pltpu
from jax.sharding import PartitionSpec as P

TOP = 8
TOP_GROUPS = 4


def shortened(shard):
    return jax.tree.map(lambda a: a.astype(jnp.bfloat16) if a.dtype == jnp.float32 else a, shard)


def take_rows(values, indices, filler):
    return jnp.take(values, indices, axis=0, mode="fill", fill_value=filler)


def route_table(targets, dest_total, capacity):
    token_total = targets.shape[0]
    dest_iota = jnp.arange(dest_total, dtype=jnp.int32)
    reached = jnp.any(targets[:, :, None] == dest_iota[None, None, :], axis=1)
    ranked = jnp.cumsum(reached.astype(jnp.int32), axis=0) - 1
    slot_of = jnp.where(reached, ranked, capacity)
    dest_grid = jnp.broadcast_to(dest_iota[None, :], slot_of.shape)
    token_grid = jnp.broadcast_to(jnp.arange(token_total, dtype=jnp.int32)[:, None], slot_of.shape)
    sources = jnp.full((dest_total, capacity), token_total, jnp.int32)
    sources = sources.at[dest_grid, slot_of].set(token_grid, mode="drop")
    return (slot_of, sources)


def token_groups(group_ids, group_total):
    token_total = group_ids.shape[0]
    group_iota = jnp.arange(group_total, dtype=jnp.int32)
    reached = jnp.any(group_ids[:, :, None] == group_iota[None, None, :], axis=1)
    ranked = jnp.cumsum(reached.astype(jnp.int32), axis=1) - 1
    column = jnp.where(reached, ranked, TOP_GROUPS)
    token_grid = jnp.broadcast_to(jnp.arange(token_total, dtype=jnp.int32)[:, None], column.shape)
    listed = jnp.full((token_total, TOP_GROUPS), group_total, jnp.int32)
    return listed.at[token_grid, column].set(
        jnp.broadcast_to(group_iota[None, :], column.shape), mode="drop"
    )


def expert_pass(
    token_rows,
    grad_rows,
    id_rows,
    weight_rows,
    gate_weight,
    up_weight,
    down_weight,
    first_expert,
    capacity,
):
    row_total = token_rows.shape[0]
    local_total = gate_weight.shape[0]
    model_width = token_rows.shape[1]
    experts_here = first_expert + jnp.arange(local_total, dtype=jnp.int32)
    matched = id_rows[None, :, :] == experts_here[:, None, None]
    chosen = jnp.any(matched, axis=2)
    weight_of = jnp.sum(
        jnp.where(matched, weight_rows.astype(jnp.float32)[None, :, :], 0.0), axis=2
    )
    ranked = jnp.cumsum(chosen.astype(jnp.int32), axis=1) - 1
    slot_of = jnp.where(chosen, ranked, capacity)
    expert_grid = jnp.broadcast_to(jnp.arange(local_total, dtype=jnp.int32)[:, None], slot_of.shape)
    row_grid = jnp.broadcast_to(jnp.arange(row_total, dtype=jnp.int32)[None, :], slot_of.shape)
    picks = (
        jnp.full((local_total, capacity), row_total, jnp.int32)
        .at[expert_grid, slot_of]
        .set(row_grid, mode="drop")
    )
    buffer_x = take_rows(token_rows, picks, 0)
    buffer_g = take_rows(grad_rows, picks, 0)
    buffer_w = jnp.take_along_axis(weight_of, picks, axis=1, mode="fill", fill_value=0.0)
    gate_act = jnp.einsum("ecd,edf->ecf", buffer_x, gate_weight, preferred_element_type=jnp.float32)
    up_act = jnp.einsum("ecd,edf->ecf", buffer_x, up_weight, preferred_element_type=jnp.float32)
    back_grad = jnp.einsum(
        "ecd,efd->ecf", buffer_g, down_weight, preferred_element_type=jnp.float32
    )
    sigmoid_val = jax.nn.sigmoid(gate_act)
    silu_val = gate_act * sigmoid_val
    route_grad = jnp.sum(back_grad * silu_val * up_act, axis=2)
    hidden_grad = buffer_w[:, :, None] * back_grad
    gate_grad = (
        hidden_grad * up_act * sigmoid_val * (1.0 + gate_act * (1.0 - sigmoid_val))
    ).astype(jnp.bfloat16)
    up_grad = (hidden_grad * silu_val).astype(jnp.bfloat16)
    input_grad = jnp.einsum(
        "ecf,edf->ecd", gate_grad, gate_weight, preferred_element_type=jnp.float32
    )
    input_grad = input_grad + jnp.einsum(
        "ecf,edf->ecd", up_grad, up_weight, preferred_element_type=jnp.float32
    )
    partial_value = jnp.zeros((row_total, model_width), jnp.float32)
    partial_value = partial_value.at[picks.reshape(-1)].add(
        input_grad.reshape(-1, model_width), mode="drop"
    )
    cap_grid = jnp.broadcast_to(jnp.arange(local_total, dtype=jnp.int32)[:, None], picks.shape)
    route_per = (
        jnp.zeros((local_total, row_total), jnp.float32)
        .at[cap_grid, picks]
        .add(route_grad, mode="drop")
    )
    route_rows = jnp.sum(jnp.where(matched, route_per[:, :, None], 0.0), axis=0)
    return (partial_value, route_rows)


def routed_body(tokens, cotangent, expert_ids, route_weights, gate_weight, up_weight, down_weight):
    group_total = lax.axis_size("grp")
    loc_total = lax.axis_size("loc")
    token_total = tokens.shape[0]
    model_width = tokens.shape[1]
    per_device = gate_weight.shape[0]
    per_group = per_device * loc_total
    group_cap = 6 * token_total // group_total
    expert_cap = 3 * token_total * loc_total
    device_rank = lax.axis_index("grp") * loc_total + lax.axis_index("loc")
    first_expert = device_rank * per_device
    group_ids = expert_ids // per_group
    listed = token_groups(group_ids, group_total)
    slot_range = jnp.arange(TOP, dtype=jnp.int32)[None, :]
    slot_of, sources = route_table(group_ids, group_total, group_cap)
    send_x = take_rows(tokens, sources, 0)
    send_g = take_rows(cotangent, sources, 0)
    send_ids = take_rows(expert_ids, sources, -1)
    send_w = take_rows(route_weights, sources, 0)
    recv_x, recv_g, recv_ids, recv_w = (
        lax.all_to_all(send_x, "grp", split_axis=0, concat_axis=0, tiled=True),
        lax.all_to_all(send_g, "grp", split_axis=0, concat_axis=0, tiled=True),
        lax.all_to_all(send_ids, "grp", split_axis=0, concat_axis=0, tiled=True),
        lax.all_to_all(send_w, "grp", split_axis=0, concat_axis=0, tiled=True),
    )
    row_total = group_total * group_cap
    shared_x, shared_g, shared_ids, shared_w = (
        lax.all_gather(recv_x.reshape(row_total, model_width), "loc", axis=0, tiled=True),
        lax.all_gather(recv_g.reshape(row_total, model_width), "loc", axis=0, tiled=True),
        lax.all_gather(shortened(recv_ids.reshape(row_total, TOP)), "loc", axis=0, tiled=True),
        lax.all_gather(recv_w.reshape(row_total, TOP), "loc", axis=0, tiled=True),
    )
    partial_value, route_rows = expert_pass(
        shared_x,
        shared_g,
        shared_ids,
        shared_w,
        gate_weight,
        up_weight,
        down_weight,
        first_expert,
        expert_cap,
    )
    summed, route_sum = (
        lax.psum_scatter(partial_value, "loc", scatter_dimension=0, tiled=True),
        lax.psum_scatter(route_rows, "loc", scatter_dimension=0, tiled=True),
    )
    group_part = summed.astype(jnp.bfloat16).reshape(group_total, group_cap, model_width)
    route_part = route_sum.astype(jnp.bfloat16).reshape(group_total, group_cap, TOP)
    back_terms, back_route = (
        lax.all_to_all(group_part, "grp", split_axis=0, concat_axis=0, tiled=True),
        lax.all_to_all(route_part, "grp", split_axis=0, concat_axis=0, tiled=True),
    )
    slot_pad = jnp.concatenate([slot_of, jnp.full((token_total, 1), group_cap, jnp.int32)], axis=1)
    found = jnp.take_along_axis(slot_pad, listed, axis=1)
    position = jnp.where(found < group_cap, listed * group_cap + found, row_total)
    pieces = take_rows(back_terms.reshape(row_total, model_width), position, 0)
    grad_tokens = jnp.sum(pieces.astype(jnp.float32), axis=1).astype(jnp.bfloat16)
    slot_found = jnp.take_along_axis(slot_of, group_ids, axis=1)
    route_index = (group_ids * group_cap + slot_found) * TOP + slot_range
    grad_weights = back_route.reshape(row_total * TOP)[route_index]
    return (grad_tokens, grad_weights)


LANES = 128
SLOT = 32
NT = (((1,), (1,)), ((), ()))
ANYWHERE = pl.BlockSpec(memory_space=pl.ANY)
IN_VMEM = pl.BlockSpec(memory_space=pltpu.VMEM)
IN_SMEM = pl.BlockSpec(memory_space=pltpu.SMEM)
MIB = 1024 * 1024
TOKEN = jax.ShapeDtypeStruct((8, LANES), jnp.float32)


def ring_rank(steps):
    total, rank = lax.axis_size("grp"), lax.axis_index("grp")
    half = lax.shift_right_logical(rank + 1, 1)
    place = jnp.where(lax.rem(rank, 2) == 0, half, total - half) + steps
    place = jnp.where(place >= total, place - total, place)
    return jnp.where(2 * place < total, 2 * place, 2 * (total - place) - 1)


def pack_kernel(per_group, tokens, cotangent, ids, weights, *refs):
    up_block, down_block, table_out, *orders, ids_here, weights_here, rows_here, sems = refs
    rows, width = tokens.shape
    half = lax.axis_size("grp") // 2
    small = (
        pltpu.make_async_copy(ids, ids_here, sems.at[0]),
        pltpu.make_async_copy(weights, weights_here, sems.at[1]),
    )
    large = (
        pltpu.make_async_copy(tokens, rows_here.at[:, pl.ds(0, width)], sems.at[2]),
        pltpu.make_async_copy(cotangent, rows_here.at[:, pl.ds(width, width)], sems.at[3]),
    )
    for copy in small + large:
        copy.start()
    for copy in small:
        copy.wait()
    first_experts = [ring_rank(steps) * per_group for steps in (half - 1, half + 1, half)]
    sublane = lax.broadcasted_iota(jnp.int32, (LANES, rows), 0)
    table = jnp.zeros((LANES, rows), jnp.float32)
    named = [jnp.zeros((1, rows), jnp.int32) for _ in first_experts]
    for k in range(ids.shape[0]):
        chosen = ids_here[k : k + 1, :]
        table += jnp.where(sublane == chosen, weights_here[k : k + 1, :].astype(jnp.float32), 0.0)
        named = [
            n | jnp.where((chosen >= first) & (chosen < first + per_group), 1, 0)
            for n, first in zip(named, first_experts)
        ]
    from_row = lax.broadcasted_iota(jnp.int32, (rows, rows), 0)
    to_row = lax.broadcasted_iota(jnp.int32, (rows, rows), 1)
    upper = jnp.where(from_row <= to_row, 1.0, 0.0).astype(jnp.bfloat16)
    sixteen = lax.broadcasted_iota(jnp.int32, (16, rows), 0)

    def ranks(flags):
        stacked = jnp.zeros((16, rows), jnp.float32)
        for i, flag in enumerate(flags):
            stacked = jnp.where(sixteen == i, flag.astype(jnp.float32), stacked)
        stacked = stacked.astype(jnp.bfloat16)
        counts = jnp.dot(stacked, upper, preferred_element_type=jnp.float32).astype(jnp.int32)
        totals = jnp.dot(stacked, jnp.ones_like(upper), preferred_element_type=jnp.float32).astype(jnp.int32)
        rows_of = range(len(flags))
        return [counts[i : i + 1, :] - 1 for i in rows_of], [totals[i : i + 1, :] for i in rows_of]

    up, down, across = named
    kinds = (across * up * (1 - down), across * (1 - up) * (1 - down), across * up * down, across * (1 - up) * down)
    (only_up, neither, both, only_down), (n_up, n_neither, n_both, n_down) = ranks(kinds)
    early = lax.shift_right_logical(n_neither + 1, 1)
    on_line = jnp.where(
        kinds[0] > 0,
        only_up,
        jnp.where(
            kinds[1] > 0,
            n_up + neither + jnp.where(neither < early, 0, n_both),
            jnp.where(kinds[2] > 0, n_up + early + both, n_up + n_neither + n_both + only_down),
        ),
    )
    middle = lax.shift_right_logical(n_up + n_neither + n_both + n_down + 1, 1)
    ahead = across * jnp.where(on_line < middle, 1, 0)
    firsts = (ahead, across - ahead)
    sets = []
    for first, near in zip(firsts, (up, down)):
        second = near * (1 - first)
        sets += [first, second, (1 - first) * (1 - second)]
    places, totals = ranks(sets)
    for i in range(2):
        target = jnp.where(
            sets[3 * i] > 0,
            places[3 * i],
            totals[3 * i]
            + jnp.where(sets[3 * i + 1] > 0, places[3 * i + 1], totals[3 * i + 1] + places[3 * i + 2]),
        )
        orders[i][...] = jnp.where(from_row == target, 1.0, 0.0).astype(jnp.bfloat16)
    table_out[...] = table.T.astype(jnp.bfloat16)
    blocks = up_block, down_block
    far = (sublane >= first_experts[2]) & (sublane < first_experts[2] + per_group)
    for block, order, first in zip(blocks, orders, firsts):
        mine = jnp.where(far & (first == 0), 0.0, table).astype(jnp.bfloat16)
        block[:, 2 * width :] = lax.dot_general(order[...], mine, NT, preferred_element_type=jnp.float32).astype(
            jnp.bfloat16
        )
    for copy in large:
        copy.wait()
    for block, order in zip(blocks, orders):
        for lanes in (slice(0, width), slice(width, 2 * width)):
            block[:, lanes] = jnp.dot(order[...], rows_here[:, lanes], preferred_element_type=jnp.float32).astype(
                jnp.bfloat16
            )


def pack(per_group, tokens, cotangent, ids, weights):
    rows, width = tokens.shape
    shape = (rows, 2 * width + LANES)
    order = jax.ShapeDtypeStruct((rows, rows), jnp.bfloat16)
    return pl.pallas_call(
        functools.partial(pack_kernel, per_group),
        out_shape=(
            jax.ShapeDtypeStruct(shape, jnp.bfloat16),
            jax.ShapeDtypeStruct(shape, jnp.bfloat16),
            jax.ShapeDtypeStruct((rows, LANES), jnp.bfloat16),
            order,
            order,
        ),
        in_specs=[ANYWHERE] * 4,
        out_specs=(IN_VMEM,) * 5,
        scratch_shapes=[
            pltpu.VMEM((ids.shape[1], rows), jnp.int32),
            pltpu.VMEM((ids.shape[1], rows), jnp.bfloat16),
            pltpu.VMEM((rows, 2 * width), jnp.bfloat16),
            pltpu.SemaphoreType.DMA((4,)),
        ],
        compiler_params=pltpu.CompilerParams(vmem_limit_bytes=7 * MIB),
    )(*(in_hbm(a) for a in (tokens, cotangent, ids.T, weights.T)))


def in_hbm(a):
    return pltpu.with_memory_space_constraint(a, pltpu.HBM)


def in_vmem(a):
    return pltpu.with_memory_space_constraint(a, pltpu.VMEM)


def load_kernel(after_this, gate, up, down, gate_up, back, down_back, token, down_here, sems):
    del after_this
    token[...] = jnp.zeros_like(token)
    per_device, hidden = gate.shape[0], gate.shape[2]
    copies = []
    for e in range(per_device):
        copies.append(
            (
                pltpu.make_async_copy(down.at[e], down_here.at[e], sems.at[2, e]),
                pltpu.make_async_copy(gate.at[e], gate_up.at[e, :, pl.ds(0, hidden)], sems.at[0, e]),
                pltpu.make_async_copy(up.at[e], gate_up.at[e, :, pl.ds(hidden, hidden)], sems.at[1, e]),
            )
        )
    for three in copies:
        for copy in three:
            copy.start()
    for e, (first, second, third) in enumerate(copies):
        first.wait()
        down_back[:, e * hidden : (e + 1) * hidden] = down_here[e].T
        second.wait()
        third.wait()
        back[2 * e * hidden : 2 * (e + 1) * hidden, :] = gate_up[e].T


def load(after_this, gate, up, down):
    per_device, width, hidden = gate.shape
    return pl.pallas_call(
        load_kernel,
        out_shape=(
            pltpu.VMEM((per_device, width, 2 * hidden), jnp.bfloat16),
            pltpu.VMEM((2 * per_device * hidden, width), jnp.bfloat16),
            pltpu.VMEM((width, per_device * hidden), jnp.bfloat16),
            TOKEN,
        ),
        in_specs=[ANYWHERE] * 4,
        out_specs=(IN_VMEM,) * 4,
        scratch_shapes=[pltpu.VMEM(down.shape, jnp.bfloat16), pltpu.SemaphoreType.DMA((3, per_device))],
        compiler_params=pltpu.CompilerParams(vmem_limit_bytes=8 * MIB),
        cost_estimate=pl.CostEstimate(flops=1, bytes_accessed=24 * MIB, transcendentals=0),
    )(after_this, gate, up, down)


def experts_kernel(inputs, plan, unrolled, place, after_this, *refs):
    del after_this
    given, refs = refs[:inputs], refs[inputs:]
    loaded, refs = (refs[:3], refs[3:6]), refs[6:]
    *outs, token = refs
    token[...] = jnp.zeros_like(token)
    per_device, width, both_hidden = loaded[0][0].shape
    hidden = both_hidden // 2
    if given[0].shape[1] > width:
        x = jnp.concatenate([a[:, :width] for a in given], axis=0)
        g = jnp.concatenate([a[:, width : 2 * width] for a in given], axis=0)
        table = jnp.concatenate([a[:, 2 * width :] for a in given], axis=0)
    else:
        x, g, table = (a[...] for a in given)
    spare = -x.shape[0] % (LANES // 2)
    if spare:
        x, g, table = (jnp.concatenate([a, jnp.zeros((spare, a.shape[1]), a.dtype)], axis=0) for a in (x, g, table))
    table = table.astype(jnp.float32)
    lane = lax.broadcasted_iota(jnp.int32, table.shape, 1)
    route = jnp.zeros(table.shape, jnp.float32)
    grads = []
    for pair, (gate_up, _, down_back) in enumerate(loaded):
        backs = jnp.dot(g, down_back[...], preferred_element_type=jnp.float32)
        mine = []
        for at in range(per_device):
            back = backs[:, at * hidden : (at + 1) * hidden]
            column = place[0] + lax.rem(place[1] + pair * per_device + at, 2 * per_device)
            weight = jnp.sum(jnp.where(lane == column, table, 0.0), axis=1, keepdims=True)
            both = jnp.dot(x, gate_up[at], preferred_element_type=jnp.float32)
            gate_act, up_act = both[:, :hidden], both[:, hidden:]
            sig = jax.nn.sigmoid(gate_act)
            silu = gate_act * sig
            back_up = back * up_act
            route_grad = jnp.sum(back_up * silu, axis=1, keepdims=True)
            mine.append((weight * back_up * sig * (1.0 + gate_act * (1.0 - sig))).astype(jnp.bfloat16))
            mine.append((weight * back * silu).astype(jnp.bfloat16))
            route += jnp.where((lane == column) & (weight > 0.0), route_grad, 0.0)
        grads.append(jnp.concatenate(mine, axis=1))
    step = 4 * LANES

    def chunk(i, carry):
        part = pl.ds(pl.multiple_of(i * step, step), step)
        total = sum(
            jnp.dot(a, back[:, part], preferred_element_type=jnp.float32) for a, (_, back, _) in zip(grads, loaded)
        ).astype(jnp.bfloat16)
        for out, start, rows in grads_at:
            out[:, part] = total[start : start + rows]
        return carry

    grads_at, routes_at = [], []
    start = at_out = 0
    for long, short, first in plan:
        if long:
            grads_at.append((outs[at_out], start, long))
            routes_at.append((outs[at_out], width, (start, long), (start + long, short, first)))
            at_out += 1
        if short:
            grads_at.append((outs[at_out], start + long, short))
            at_out += 1
            if not long:
                routes_at.append((outs[at_out], 0, (start, 0), (start, short, first)))
                at_out += 1
        start += long + short
    lax.fori_loop(0, width // step, chunk, 0, unroll=unrolled)
    for out, lanes, (start, long), (short_start, short, first) in routes_at:
        rows = out.shape[0]
        carried = route[start : start + long] if long else jnp.zeros((rows, LANES), jnp.float32)
        if short:
            split = min(short, rows - first)
            carried += shifted(route[short_start : short_start + split], 1, first, rows)
            if short > split:
                carried += shifted(route[short_start + split : short_start + short], 2, 0, rows)
        out[:, lanes : lanes + LANES] = carried.astype(out.dtype)


def shifted(route, slot, first, rows):
    moved = pltpu.roll(route, slot * SLOT, 1)
    parts = [moved]
    if first:
        parts.insert(0, jnp.zeros((first, LANES), route.dtype))
    if rows > first + route.shape[0]:
        parts.append(jnp.zeros((rows - first - route.shape[0], LANES), route.dtype))
    return jnp.concatenate(parts, axis=0) if len(parts) > 1 else moved


def experts_call(place, after_this, given, plan, loaded, unrolled):
    width = loaded[0].shape[1]
    shapes = []
    for long, short, _ in plan:
        shapes += [(long, width + LANES)] * (long > 0) + [(short, width)] * (short > 0)
        shapes += [(short, LANES)] * (not long)
    return pl.pallas_call(
        functools.partial(experts_kernel, len(given), plan, unrolled),
        out_shape=[jax.ShapeDtypeStruct(shape, jnp.bfloat16) for shape in shapes] + [TOKEN],
        in_specs=[IN_SMEM, ANYWHERE] + [IN_VMEM] * (len(given) + 6),
        out_specs=[IN_VMEM] * (len(shapes) + 1),
        compiler_params=pltpu.CompilerParams(vmem_limit_bytes=12 * MIB),
        cost_estimate=pl.CostEstimate(flops=1, bytes_accessed=1, transcendentals=0),
    )(place, after_this, *(in_vmem(a) for a in given), *loaded)


def finish_kernel(ids, order_up, order_down, mine, long_up, short_up, long_down, short_down, grad_tokens, grad_weights):
    width = grad_tokens.shape[1]
    backs = order_up[...].T, order_down[...].T
    summed = mine[:, :width].astype(jnp.float32)
    route = mine[:, width:].astype(jnp.float32)
    for back, long, short in zip(backs, (long_up, long_down), (short_up, short_down)):
        rows, spare = long.shape[0], short.shape[0] - long.shape[0]
        came = jnp.concatenate([long[:, :width], short[...]], axis=0)
        summed += jnp.dot(back, came, preferred_element_type=jnp.float32)
        carried = long[:, width:].astype(jnp.float32)
        first = lax.broadcasted_iota(jnp.int32, carried.shape, 1) < SLOT
        slots = [jnp.where(first, pltpu.roll(carried, (LANES - k * SLOT) % LANES, 1), 0.0) for k in range(3)]
        came = jnp.concatenate([slots[0], slots[1], slots[2][:spare]], axis=0).astype(jnp.bfloat16)
        route += jnp.dot(back, came, preferred_element_type=jnp.float32)
    grad_tokens[...] = summed.astype(grad_tokens.dtype)
    route = route.T
    expert = lax.broadcasted_iota(jnp.int32, route.shape, 0)
    found = [
        jnp.sum(jnp.where(expert == ids[k : k + 1, :], route, 0.0), axis=0, keepdims=True) for k in range(ids.shape[0])
    ]
    grad_weights[...] = jnp.concatenate(found, axis=0).astype(grad_weights.dtype)


def finish(ids, terms, width):
    rows, top = ids.shape
    grad_tokens, grad_weights = pl.pallas_call(
        finish_kernel,
        out_shape=(
            jax.ShapeDtypeStruct((rows, width), jnp.bfloat16),
            jax.ShapeDtypeStruct((top, rows), jnp.bfloat16),
        ),
        in_specs=[IN_VMEM] * 8,
        out_specs=(IN_VMEM, IN_VMEM),
        compiler_params=pltpu.CompilerParams(vmem_limit_bytes=12 * MIB),
    )(ids.T, *terms)
    return grad_tokens, grad_weights.T


def add_kernel(a, b, *refs):
    *more, out = refs
    rows = b.shape[0]
    if rows < a.shape[0]:
        out[rows:, :] = a[rows:, :]
    out[:rows, :] = (a[:rows, :].astype(jnp.float32) + b[...].astype(jnp.float32)).astype(out.dtype)
    for c in more:
        width = a.shape[1] - c.shape[1]
        total = a[:, width:].astype(jnp.float32) + b[:, width:].astype(jnp.float32) + c[...].astype(jnp.float32)
        out[:, width:] = total.astype(out.dtype)


def join_kernel(a, b, out):
    rows = a.shape[0]
    out[:rows, :] = a[...]
    out[rows:, :] = b[...]


def joined(a, b):
    return pl.pallas_call(
        join_kernel,
        out_shape=jax.ShapeDtypeStruct((a.shape[0] + b.shape[0], a.shape[1]), a.dtype),
        in_specs=[IN_VMEM] * 2,
        out_specs=IN_VMEM,
        compiler_params=pltpu.CompilerParams(vmem_limit_bytes=8 * MIB),
        cost_estimate=pl.CostEstimate(flops=1, bytes_accessed=1, transcendentals=0),
    )(a, b)


def added(a, b, *more):
    return pl.pallas_call(
        add_kernel,
        out_shape=jax.ShapeDtypeStruct(a.shape, a.dtype),
        in_specs=[IN_VMEM] * (2 + len(more)),
        out_specs=IN_VMEM,
        compiler_params=pltpu.CompilerParams(vmem_limit_bytes=8 * MIB),
        cost_estimate=pl.CostEstimate(flops=1, bytes_accessed=1, transcendentals=0),
    )(a, b, *more)


def ring_body(tokens, cotangent, expert_ids, route_weights, gate_weight, up_weight, down_weight):
    ring_total = lax.axis_size("grp")
    loc_total = lax.axis_size("loc")
    width = tokens.shape[1]
    per_device = gate_weight.shape[0]
    order = list(range(0, ring_total, 2)) + list(range(ring_total - 1, 0, -2))
    ahead = [(order[i], order[(i + 1) % ring_total]) for i in range(ring_total)]
    behind = [(b, a) for a, b in ahead]
    rank, loc = lax.axis_index("grp"), lax.axis_index("loc")

    def send(pair):
        return lax.ppermute(pair[0], "grp", ahead), lax.ppermute(pair[1], "grp", behind)

    def send_back(pair):
        return lax.ppermute(pair[0], "grp", behind), lax.ppermute(pair[1], "grp", ahead)

    def tie(pair, *others):
        return tuple(lax.optimization_barrier((a, *others))[0] for a in pair)

    own = (gate_weight, up_weight, down_weight)
    other = [lax.ppermute(a, "loc", [(i, loc_total - 1 - i) for i in range(loc_total)]) for a in own]
    per_group = loc_total * per_device
    place = jnp.stack([rank * per_group, loc * per_device]).astype(jnp.int32)
    *blocks, table, order_up, order_down = pack(per_group, tokens, cotangent, expert_ids, route_weights)
    came = send(blocks)
    *loaded, loaded_own = load(place, *(in_hbm(a) for a in own))
    *others, last = load(loaded_own, *tie(other[:2], *came), other[2])
    loaded += others

    def call(after_this, plan, *packed, unrolled=False):
        *parts, token = experts_call(place, after_this, packed, plan, loaded, unrolled)
        return parts, token

    block = tokens.shape[0]
    half, most = ring_total // 2, 6 * block // ring_total
    half_block, cut = block // 2, most // 2
    rest, needed, extra = block - cut, (block + most) // 2 - half_block, half_block - cut
    long, short = [a[:half_block] for a in came], [a[half_block:] for a in came]
    long_next, short_next = send(tie(long, loaded_own, *other)), send(tie(short, loaded_own, *other))
    own_plan = ((block, 0, 0),)
    mine, last = experts_call(place, last, (tokens, cotangent, table), own_plan, loaded, False)
    filler = last
    both_plan = ((cut, rest, 0),) * 2
    parts, last = call(last, both_plan, *came)
    long_terms, short_terms = [None, parts[0::2]], [None, parts[1::2]]
    for s in range(2, half - 1):
        long, short = long_next, short_next
        long_next = send(tie(long, filler))
        short_next = send(tie([a[:needed] for a in short] if s + 2 == half else short, last))
        parts, last = call(last, both_plan, long[0], short[0], long[1], short[1])
        long_terms.append(parts[0::2])
        short_terms.append(parts[1::2])
    long, short = long_next, short_next
    long_last = send(tie([a[:cut] for a in long], last))
    parts, last = call(last, ((cut, extra, 0),) * 2, *long)
    long_terms.append(parts[0::2])
    lower = parts[1::2]
    parts, last = call(last, ((0, needed, extra),) * 2, *short, unrolled=True)
    short_back = send_back([joined(a, b) for a, b in zip(lower, parts[0::2])])
    carried = parts[1::2]
    parts, last = call(last, ((cut, 0, 0),) * 2, *long_last, unrolled=True)
    long_back = send_back(tie(parts, *short_back))
    for s in range(half - 1, 0, -1):
        if s < half - 1:
            short_back = send_back([added(a, b) for a, b in zip(short_terms[s], short_back)])
            long_back = send_back([added(a, b) for a, b in zip(long_terms[s], long_back)])
        else:
            long_back = send_back([added(a, b, c) for a, b, c in zip(long_terms[s], long_back, carried)])
    terms = (order_up, order_down, mine, long_back[0], short_back[0], long_back[1], short_back[1])
    return finish(expert_ids, terms, width)


def body(tokens, cotangent, expert_ids, route_weights, gate_weight, up_weight, down_weight):
    args = (tokens, cotangent, expert_ids, route_weights, gate_weight, up_weight, down_weight)
    ring_total, loc_total = lax.axis_size("grp"), lax.axis_size("loc")
    experts = ring_total * loc_total * gate_weight.shape[0]
    if loc_total == 2 and ring_total == 8 and experts <= SLOT and tokens.shape[0] == LANES:
        return ring_body(*args)
    return routed_body(*args)


def solution(mesh):
    placed = (
        P(("rep", "grp", "loc"), None),
        P(("rep", "grp", "loc"), None),
        P(("rep", "grp", "loc"), None),
        P(("rep", "grp", "loc"), None),
        P(("grp", "loc"), None, None),
        P(("grp", "loc"), None, None),
        P(("grp", "loc"), None, None),
    )
    return jax.shard_map(
        body,
        mesh=mesh,
        in_specs=placed,
        out_specs=(P(("rep", "grp", "loc"), None), P(("rep", "grp", "loc"), None)),
        check_vma=False,
    )
```

```python
import functools

import jax
import jax.numpy as jnp
from jax import lax
from jax.experimental import pallas as pl
from jax.experimental.pallas import tpu as pltpu
from jax.sharding import PartitionSpec as P

TOP = 8
TOP_GROUPS = 4


def shortened(shard):
    return jax.tree.map(lambda a: a.astype(jnp.bfloat16) if a.dtype == jnp.float32 else a, shard)


def take_rows(values, indices, filler):
    return jnp.take(values, indices, axis=0, mode="fill", fill_value=filler)


def route_table(targets, dest_total, capacity):
    token_total = targets.shape[0]
    dest_iota = jnp.arange(dest_total, dtype=jnp.int32)
    reached = jnp.any(targets[:, :, None] == dest_iota[None, None, :], axis=1)
    ranked = jnp.cumsum(reached.astype(jnp.int32), axis=0) - 1
    slot_of = jnp.where(reached, ranked, capacity)
    dest_grid = jnp.broadcast_to(dest_iota[None, :], slot_of.shape)
    token_grid = jnp.broadcast_to(jnp.arange(token_total, dtype=jnp.int32)[:, None], slot_of.shape)
    sources = jnp.full((dest_total, capacity), token_total, jnp.int32)
    sources = sources.at[dest_grid, slot_of].set(token_grid, mode="drop")
    return (slot_of, sources)


def token_groups(group_ids, group_total):
    token_total = group_ids.shape[0]
    group_iota = jnp.arange(group_total, dtype=jnp.int32)
    reached = jnp.any(group_ids[:, :, None] == group_iota[None, None, :], axis=1)
    ranked = jnp.cumsum(reached.astype(jnp.int32), axis=1) - 1
    column = jnp.where(reached, ranked, TOP_GROUPS)
    token_grid = jnp.broadcast_to(jnp.arange(token_total, dtype=jnp.int32)[:, None], column.shape)
    listed = jnp.full((token_total, TOP_GROUPS), group_total, jnp.int32)
    return listed.at[token_grid, column].set(
        jnp.broadcast_to(group_iota[None, :], column.shape), mode="drop"
    )


def expert_pass(
    token_rows,
    grad_rows,
    id_rows,
    weight_rows,
    gate_weight,
    up_weight,
    down_weight,
    first_expert,
    capacity,
):
    row_total = token_rows.shape[0]
    local_total = gate_weight.shape[0]
    model_width = token_rows.shape[1]
    experts_here = first_expert + jnp.arange(local_total, dtype=jnp.int32)
    matched = id_rows[None, :, :] == experts_here[:, None, None]
    chosen = jnp.any(matched, axis=2)
    weight_of = jnp.sum(
        jnp.where(matched, weight_rows.astype(jnp.float32)[None, :, :], 0.0), axis=2
    )
    ranked = jnp.cumsum(chosen.astype(jnp.int32), axis=1) - 1
    slot_of = jnp.where(chosen, ranked, capacity)
    expert_grid = jnp.broadcast_to(jnp.arange(local_total, dtype=jnp.int32)[:, None], slot_of.shape)
    row_grid = jnp.broadcast_to(jnp.arange(row_total, dtype=jnp.int32)[None, :], slot_of.shape)
    picks = (
        jnp.full((local_total, capacity), row_total, jnp.int32)
        .at[expert_grid, slot_of]
        .set(row_grid, mode="drop")
    )
    buffer_x = take_rows(token_rows, picks, 0)
    buffer_g = take_rows(grad_rows, picks, 0)
    buffer_w = jnp.take_along_axis(weight_of, picks, axis=1, mode="fill", fill_value=0.0)
    gate_act = jnp.einsum("ecd,edf->ecf", buffer_x, gate_weight, preferred_element_type=jnp.float32)
    up_act = jnp.einsum("ecd,edf->ecf", buffer_x, up_weight, preferred_element_type=jnp.float32)
    back_grad = jnp.einsum(
        "ecd,efd->ecf", buffer_g, down_weight, preferred_element_type=jnp.float32
    )
    sigmoid_val = jax.nn.sigmoid(gate_act)
    silu_val = gate_act * sigmoid_val
    route_grad = jnp.sum(back_grad * silu_val * up_act, axis=2)
    hidden_grad = buffer_w[:, :, None] * back_grad
    gate_grad = (
        hidden_grad * up_act * sigmoid_val * (1.0 + gate_act * (1.0 - sigmoid_val))
    ).astype(jnp.bfloat16)
    up_grad = (hidden_grad * silu_val).astype(jnp.bfloat16)
    input_grad = jnp.einsum(
        "ecf,edf->ecd", gate_grad, gate_weight, preferred_element_type=jnp.float32
    )
    input_grad = input_grad + jnp.einsum(
        "ecf,edf->ecd", up_grad, up_weight, preferred_element_type=jnp.float32
    )
    partial_value = jnp.zeros((row_total, model_width), jnp.float32)
    partial_value = partial_value.at[picks.reshape(-1)].add(
        input_grad.reshape(-1, model_width), mode="drop"
    )
    cap_grid = jnp.broadcast_to(jnp.arange(local_total, dtype=jnp.int32)[:, None], picks.shape)
    route_per = (
        jnp.zeros((local_total, row_total), jnp.float32)
        .at[cap_grid, picks]
        .add(route_grad, mode="drop")
    )
    route_rows = jnp.sum(jnp.where(matched, route_per[:, :, None], 0.0), axis=0)
    return (partial_value, route_rows)


def routed_body(tokens, cotangent, expert_ids, route_weights, gate_weight, up_weight, down_weight):
    group_total = lax.axis_size("grp")
    loc_total = lax.axis_size("loc")
    token_total = tokens.shape[0]
    model_width = tokens.shape[1]
    per_device = gate_weight.shape[0]
    per_group = per_device * loc_total
    group_cap = 6 * token_total // group_total
    expert_cap = 3 * token_total * loc_total
    device_rank = lax.axis_index("grp") * loc_total + lax.axis_index("loc")
    first_expert = device_rank * per_device
    group_ids = expert_ids // per_group
    listed = token_groups(group_ids, group_total)
    slot_range = jnp.arange(TOP, dtype=jnp.int32)[None, :]
    slot_of, sources = route_table(group_ids, group_total, group_cap)
    send_x = take_rows(tokens, sources, 0)
    send_g = take_rows(cotangent, sources, 0)
    send_ids = take_rows(expert_ids, sources, -1)
    send_w = take_rows(route_weights, sources, 0)
    recv_x, recv_g, recv_ids, recv_w = (
        lax.all_to_all(send_x, "grp", split_axis=0, concat_axis=0, tiled=True),
        lax.all_to_all(send_g, "grp", split_axis=0, concat_axis=0, tiled=True),
        lax.all_to_all(send_ids, "grp", split_axis=0, concat_axis=0, tiled=True),
        lax.all_to_all(send_w, "grp", split_axis=0, concat_axis=0, tiled=True),
    )
    row_total = group_total * group_cap
    shared_x, shared_g, shared_ids, shared_w = (
        lax.all_gather(recv_x.reshape(row_total, model_width), "loc", axis=0, tiled=True),
        lax.all_gather(recv_g.reshape(row_total, model_width), "loc", axis=0, tiled=True),
        lax.all_gather(shortened(recv_ids.reshape(row_total, TOP)), "loc", axis=0, tiled=True),
        lax.all_gather(recv_w.reshape(row_total, TOP), "loc", axis=0, tiled=True),
    )
    partial_value, route_rows = expert_pass(
        shared_x,
        shared_g,
        shared_ids,
        shared_w,
        gate_weight,
        up_weight,
        down_weight,
        first_expert,
        expert_cap,
    )
    summed, route_sum = (
        lax.psum_scatter(partial_value, "loc", scatter_dimension=0, tiled=True),
        lax.psum_scatter(route_rows, "loc", scatter_dimension=0, tiled=True),
    )
    group_part = summed.astype(jnp.bfloat16).reshape(group_total, group_cap, model_width)
    route_part = route_sum.astype(jnp.bfloat16).reshape(group_total, group_cap, TOP)
    back_terms, back_route = (
        lax.all_to_all(group_part, "grp", split_axis=0, concat_axis=0, tiled=True),
        lax.all_to_all(route_part, "grp", split_axis=0, concat_axis=0, tiled=True),
    )
    slot_pad = jnp.concatenate([slot_of, jnp.full((token_total, 1), group_cap, jnp.int32)], axis=1)
    found = jnp.take_along_axis(slot_pad, listed, axis=1)
    position = jnp.where(found < group_cap, listed * group_cap + found, row_total)
    pieces = take_rows(back_terms.reshape(row_total, model_width), position, 0)
    grad_tokens = jnp.sum(pieces.astype(jnp.float32), axis=1).astype(jnp.bfloat16)
    slot_found = jnp.take_along_axis(slot_of, group_ids, axis=1)
    route_index = (group_ids * group_cap + slot_found) * TOP + slot_range
    grad_weights = back_route.reshape(row_total * TOP)[route_index]
    return (grad_tokens, grad_weights)


LANES = 128
SLOT = 32
NT = (((1,), (1,)), ((), ()))
ANYWHERE = pl.BlockSpec(memory_space=pl.ANY)
IN_VMEM = pl.BlockSpec(memory_space=pltpu.VMEM)
IN_SMEM = pl.BlockSpec(memory_space=pltpu.SMEM)
MIB = 1024 * 1024
TOKEN = jax.ShapeDtypeStruct((8, LANES), jnp.float32)


def ring_rank(steps):
    total, rank = lax.axis_size("grp"), lax.axis_index("grp")
    half = lax.shift_right_logical(rank + 1, 1)
    place = jnp.where(lax.rem(rank, 2) == 0, half, total - half) + steps
    place = jnp.where(place >= total, place - total, place)
    return jnp.where(2 * place < total, 2 * place, 2 * (total - place) - 1)


def pack_kernel(per_group, tokens, cotangent, ids, weights, *refs):
    outs, table_out, orders, (ids_here, weights_here, rows_here, *blocks, sems, out_sems) = refs[:2], refs[2], refs[3:5], refs[5:]
    rows, width = tokens.shape
    half = lax.axis_size("grp") // 2
    small = (
        pltpu.make_async_copy(ids, ids_here, sems.at[0]),
        pltpu.make_async_copy(weights, weights_here, sems.at[1]),
    )
    large = (
        pltpu.make_async_copy(tokens, rows_here.at[:, pl.ds(0, width)], sems.at[2]),
        pltpu.make_async_copy(cotangent, rows_here.at[:, pl.ds(width, width)], sems.at[3]),
    )
    for copy in small + large:
        copy.start()
    for copy in small:
        copy.wait()
    first_experts = [ring_rank(steps) * per_group for steps in (half - 1, half + 1, half)]
    sublane = lax.broadcasted_iota(jnp.int32, (LANES, rows), 0)
    table = jnp.zeros((LANES, rows), jnp.float32)
    named = [jnp.zeros((1, rows), jnp.int32) for _ in first_experts]
    for k in range(ids.shape[0]):
        chosen = ids_here[k : k + 1, :]
        table += jnp.where(sublane == chosen, weights_here[k : k + 1, :].astype(jnp.float32), 0.0)
        named = [
            n | jnp.where((chosen >= first) & (chosen < first + per_group), 1, 0)
            for n, first in zip(named, first_experts)
        ]
    from_row = lax.broadcasted_iota(jnp.int32, (rows, rows), 0)
    to_row = lax.broadcasted_iota(jnp.int32, (rows, rows), 1)
    upper = jnp.where(from_row <= to_row, 1.0, 0.0).astype(jnp.bfloat16)
    sixteen = lax.broadcasted_iota(jnp.int32, (16, rows), 0)

    def ranks(flags):
        stacked = jnp.zeros((16, rows), jnp.float32)
        for i, flag in enumerate(flags):
            stacked = jnp.where(sixteen == i, flag.astype(jnp.float32), stacked)
        stacked = stacked.astype(jnp.bfloat16)
        counts = jnp.dot(stacked, upper, preferred_element_type=jnp.float32).astype(jnp.int32)
        totals = jnp.dot(stacked, jnp.ones_like(upper), preferred_element_type=jnp.float32).astype(jnp.int32)
        rows_of = range(len(flags))
        return [counts[i : i + 1, :] - 1 for i in rows_of], [totals[i : i + 1, :] for i in rows_of]

    up, down, across = named
    kinds = (across * up * (1 - down), across * (1 - up) * (1 - down), across * up * down, across * (1 - up) * down)
    (only_up, neither, both, only_down), (n_up, n_neither, n_both, n_down) = ranks(kinds)
    early = lax.shift_right_logical(n_neither + 1, 1)
    on_line = jnp.where(
        kinds[0] > 0,
        only_up,
        jnp.where(
            kinds[1] > 0,
            n_up + neither + jnp.where(neither < early, 0, n_both),
            jnp.where(kinds[2] > 0, n_up + early + both, n_up + n_neither + n_both + only_down),
        ),
    )
    middle = lax.shift_right_logical(n_up + n_neither + n_both + n_down + 1, 1)
    ahead = across * jnp.where(on_line < middle, 1, 0)
    firsts = (ahead, across - ahead)
    sets = []
    for first, near in zip(firsts, (up, down)):
        second = near * (1 - first)
        sets += [first, second, (1 - first) * (1 - second)]
    places, totals = ranks(sets)
    for i in range(2):
        target = jnp.where(
            sets[3 * i] > 0,
            places[3 * i],
            totals[3 * i]
            + jnp.where(sets[3 * i + 1] > 0, places[3 * i + 1], totals[3 * i + 1] + places[3 * i + 2]),
        )
        orders[i][...] = jnp.where(from_row == target, 1.0, 0.0).astype(jnp.bfloat16)
    table_out[...] = table.T.astype(jnp.bfloat16)
    far = (sublane >= first_experts[2]) & (sublane < first_experts[2] + per_group)
    for block, order, first in zip(blocks, orders, firsts):
        mine = jnp.where(far & (first == 0), 0.0, table).astype(jnp.bfloat16)
        mine = lax.dot_general(order[...], mine, NT, preferred_element_type=jnp.float32)
        low = mine[rows // 2 :]
        block[: rows // 2, 2 * width :] = (mine[: rows // 2] + pltpu.roll(low, SLOT, 1)).astype(jnp.bfloat16)
        block[rows // 2 :, 2 * width :] = low.astype(jnp.bfloat16)
    going = []
    for half_at, copy in enumerate(large):
        copy.wait()
        lanes = slice(half_at * width, (half_at + 1) * width)
        sent = pl.ds(half_at * width, width + half_at * LANES)
        for way, (block, order, out) in enumerate(zip(blocks, orders, outs)):
            block[:, lanes] = jnp.dot(order[...], rows_here[:, lanes], preferred_element_type=jnp.float32).astype(
                jnp.bfloat16
            )
            going.append(pltpu.make_async_copy(block.at[:, sent], out.at[:, sent], out_sems.at[half_at, way]))
            going[-1].start()
    for copy in going:
        copy.wait()


def pack(per_group, tokens, cotangent, ids, weights):
    rows, width = tokens.shape
    shape = (rows, 2 * width + LANES)
    order = jax.ShapeDtypeStruct((rows, rows), jnp.bfloat16)
    return pl.pallas_call(
        functools.partial(pack_kernel, per_group),
        out_shape=(
            jax.ShapeDtypeStruct(shape, jnp.bfloat16),
            jax.ShapeDtypeStruct(shape, jnp.bfloat16),
            jax.ShapeDtypeStruct((rows, LANES), jnp.bfloat16),
            order,
            order,
        ),
        in_specs=[ANYWHERE] * 4,
        out_specs=(ANYWHERE, ANYWHERE, IN_VMEM, IN_VMEM, IN_VMEM),
        scratch_shapes=[
            pltpu.VMEM((ids.shape[1], rows), jnp.int32),
            pltpu.VMEM((ids.shape[1], rows), jnp.bfloat16),
            pltpu.VMEM((rows, 2 * width), jnp.bfloat16),
            pltpu.VMEM(shape, jnp.bfloat16),
            pltpu.VMEM(shape, jnp.bfloat16),
            pltpu.SemaphoreType.DMA((4,)),
            pltpu.SemaphoreType.DMA((2, 2)),
        ],
        compiler_params=pltpu.CompilerParams(vmem_limit_bytes=7 * MIB),
    )(*(in_hbm(a) for a in (tokens, cotangent, ids.T, weights.T)))


def in_hbm(a):
    return pltpu.with_memory_space_constraint(a, pltpu.HBM)


def in_vmem(a):
    return pltpu.with_memory_space_constraint(a, pltpu.VMEM)


def load_kernel(after_this, gate, up, down, gate_up, back, down_back, token, down_here, sems):
    del after_this
    token[...] = jnp.zeros_like(token)
    per_device, hidden = gate.shape[0], gate.shape[2]
    copies = []
    for e in range(per_device):
        copies.append(
            (
                pltpu.make_async_copy(down.at[e], down_here.at[e], sems.at[2, e]),
                pltpu.make_async_copy(gate.at[e], gate_up.at[e, :, pl.ds(0, hidden)], sems.at[0, e]),
                pltpu.make_async_copy(up.at[e], gate_up.at[e, :, pl.ds(hidden, hidden)], sems.at[1, e]),
            )
        )
    for three in copies:
        for copy in three:
            copy.start()
    for e, (first, second, third) in enumerate(copies):
        first.wait()
        down_back[:, e * hidden : (e + 1) * hidden] = down_here[e].T
        second.wait()
        third.wait()
        back[2 * e * hidden : 2 * (e + 1) * hidden, :] = gate_up[e].T


def load(after_this, gate, up, down):
    per_device, width, hidden = gate.shape
    return pl.pallas_call(
        load_kernel,
        out_shape=(
            pltpu.VMEM((per_device, width, 2 * hidden), jnp.bfloat16),
            pltpu.VMEM((2 * per_device * hidden, width), jnp.bfloat16),
            pltpu.VMEM((width, per_device * hidden), jnp.bfloat16),
            TOKEN,
        ),
        in_specs=[ANYWHERE] * 4,
        out_specs=(IN_VMEM,) * 4,
        scratch_shapes=[pltpu.VMEM(down.shape, jnp.bfloat16), pltpu.SemaphoreType.DMA((3, per_device))],
        compiler_params=pltpu.CompilerParams(vmem_limit_bytes=8 * MIB),
        cost_estimate=pl.CostEstimate(flops=1, bytes_accessed=24 * MIB, transcendentals=0),
    )(after_this, gate, up, down)


def experts_kernel(inputs, plan, unrolled, place, after_this, *refs):
    del after_this
    given, refs = refs[:inputs], refs[inputs:]
    loaded, refs = (refs[:3], refs[3:6]), refs[6:]
    *outs, token = refs
    token[...] = jnp.zeros_like(token)
    per_device, width, both_hidden = loaded[0][0].shape
    hidden = both_hidden // 2
    if given[0].shape[1] > width:
        tables = []
        for a in given:
            if a.shape[1] > 2 * width:
                tables.append(a[:, 2 * width :].astype(jnp.float32))
            else:
                tables.append(pltpu.roll(tables[-1], LANES - SLOT, 1)[: a.shape[0]])
        if not any(long for long, _, _ in plan):
            given, tables = given[1::2], tables[1::2]
        x = jnp.concatenate([a[:, :width] for a in given], axis=0)
        g = jnp.concatenate([a[:, width : 2 * width] for a in given], axis=0)
        table = jnp.concatenate(tables, axis=0)
    else:
        x, g, table = (a[...] for a in given)
    spare = -x.shape[0] % (LANES // 2)
    if spare:
        x, g, table = (jnp.concatenate([a, jnp.zeros((spare, a.shape[1]), a.dtype)], axis=0) for a in (x, g, table))
    table = table.astype(jnp.float32)
    lane = lax.broadcasted_iota(jnp.int32, table.shape, 1)
    route = jnp.zeros(table.shape, jnp.float32)
    grads = []
    for pair, (gate_up, _, down_back) in enumerate(loaded):
        backs = jnp.dot(g, down_back[...], preferred_element_type=jnp.float32)
        mine = []
        for at in range(per_device):
            back = backs[:, at * hidden : (at + 1) * hidden]
            column = place[0] + lax.rem(place[1] + pair * per_device + at, 2 * per_device)
            weight = jnp.sum(jnp.where(lane == column, table, 0.0), axis=1, keepdims=True)
            both = jnp.dot(x, gate_up[at], preferred_element_type=jnp.float32)
            gate_act, up_act = both[:, :hidden], both[:, hidden:]
            sig = jax.nn.sigmoid(gate_act)
            silu = gate_act * sig
            back_up = back * up_act
            route_grad = jnp.sum(back_up * silu, axis=1, keepdims=True)
            mine.append((weight * back_up * sig * (1.0 + gate_act * (1.0 - sig))).astype(jnp.bfloat16))
            mine.append((weight * back * silu).astype(jnp.bfloat16))
            route += jnp.where((lane == column) & (weight > 0.0), route_grad, 0.0)
        grads.append(jnp.concatenate(mine, axis=1))
    step = 4 * LANES

    def chunk(i, carry):
        part = pl.ds(pl.multiple_of(i * step, step), step)
        total = sum(
            jnp.dot(a, back[:, part], preferred_element_type=jnp.float32) for a, (_, back, _) in zip(grads, loaded)
        ).astype(jnp.bfloat16)
        for out, start, rows in grads_at:
            out[:, part] = total[start : start + rows]
        return carry

    grads_at, routes_at = [], []
    start = at_out = 0
    for long, short, first in plan:
        if long:
            grads_at.append((outs[at_out], start, long))
            routes_at.append((outs[at_out], width, (start, long), (start + long, short, first)))
            at_out += 1
        if short:
            grads_at.append((outs[at_out], start + long, short))
            at_out += 1
            if not long:
                routes_at.append((outs[at_out], 0, (start, 0), (start, short, first)))
                at_out += 1
        start += long + short
    lax.fori_loop(0, width // step, chunk, 0, unroll=unrolled)
    for out, lanes, (start, long), (short_start, short, first) in routes_at:
        rows = out.shape[0]
        carried = route[start : start + long] if long else jnp.zeros((rows, LANES), jnp.float32)
        if short:
            split = min(short, rows - first)
            carried += shifted(route[short_start : short_start + split], 1, first, rows)
            if short > split:
                carried += shifted(route[short_start + split : short_start + short], 2, 0, rows)
        out[:, lanes : lanes + LANES] = carried.astype(out.dtype)


def shifted(route, slot, first, rows):
    moved = pltpu.roll(route, slot * SLOT, 1)
    parts = [moved]
    if first:
        parts.insert(0, jnp.zeros((first, LANES), route.dtype))
    if rows > first + route.shape[0]:
        parts.append(jnp.zeros((rows - first - route.shape[0], LANES), route.dtype))
    return jnp.concatenate(parts, axis=0) if len(parts) > 1 else moved


def experts_call(place, after_this, given, plan, loaded, unrolled):
    width = loaded[0].shape[1]
    shapes = []
    for long, short, _ in plan:
        shapes += [(long, width + LANES)] * (long > 0) + [(short, width)] * (short > 0)
        shapes += [(short, LANES)] * (not long)
    return pl.pallas_call(
        functools.partial(experts_kernel, len(given), plan, unrolled),
        out_shape=[jax.ShapeDtypeStruct(shape, jnp.bfloat16) for shape in shapes] + [TOKEN],
        in_specs=[IN_SMEM, ANYWHERE] + [IN_VMEM] * (len(given) + 6),
        out_specs=[IN_VMEM] * (len(shapes) + 1),
        compiler_params=pltpu.CompilerParams(vmem_limit_bytes=12 * MIB),
        cost_estimate=pl.CostEstimate(flops=1, bytes_accessed=1, transcendentals=0),
    )(place, after_this, *(in_vmem(a) for a in given), *loaded)


def finish_kernel(ids, order_up, order_down, mine, long_up, short_up, long_down, short_down, grad_tokens, grad_weights):
    width = grad_tokens.shape[1]
    backs = order_up[...].T, order_down[...].T
    summed = mine[:, :width].astype(jnp.float32)
    route = mine[:, width:].astype(jnp.float32)
    for back, long, short in zip(backs, (long_up, long_down), (short_up, short_down)):
        rows, spare = long.shape[0], short.shape[0] - long.shape[0]
        came = jnp.concatenate([long[:, :width], short[...]], axis=0)
        summed += jnp.dot(back, came, preferred_element_type=jnp.float32)
        carried = long[:, width:].astype(jnp.float32)
        first = lax.broadcasted_iota(jnp.int32, carried.shape, 1) < SLOT
        slots = [jnp.where(first, pltpu.roll(carried, (LANES - k * SLOT) % LANES, 1), 0.0) for k in range(3)]
        came = jnp.concatenate([slots[0], slots[1], slots[2][:spare]], axis=0).astype(jnp.bfloat16)
        route += jnp.dot(back, came, preferred_element_type=jnp.float32)
    grad_tokens[...] = summed.astype(grad_tokens.dtype)
    route = route.T
    expert = lax.broadcasted_iota(jnp.int32, route.shape, 0)
    found = [
        jnp.sum(jnp.where(expert == ids[k : k + 1, :], route, 0.0), axis=0, keepdims=True) for k in range(ids.shape[0])
    ]
    grad_weights[...] = jnp.concatenate(found, axis=0).astype(grad_weights.dtype)


def finish(ids, terms, width):
    rows, top = ids.shape
    grad_tokens, grad_weights = pl.pallas_call(
        finish_kernel,
        out_shape=(
            jax.ShapeDtypeStruct((rows, width), jnp.bfloat16),
            jax.ShapeDtypeStruct((top, rows), jnp.bfloat16),
        ),
        in_specs=[IN_VMEM] * 8,
        out_specs=(IN_VMEM, IN_VMEM),
        compiler_params=pltpu.CompilerParams(vmem_limit_bytes=12 * MIB),
    )(ids.T, *terms)
    return grad_tokens, grad_weights.T


def add_kernel(a, b, *refs):
    *more, out = refs
    rows = b.shape[0]
    if rows < a.shape[0]:
        out[rows:, :] = a[rows:, :]
    out[:rows, :] = (a[:rows, :].astype(jnp.float32) + b[...].astype(jnp.float32)).astype(out.dtype)
    for c in more:
        width = a.shape[1] - c.shape[1]
        total = a[:, width:].astype(jnp.float32) + b[:, width:].astype(jnp.float32) + c[...].astype(jnp.float32)
        out[:, width:] = total.astype(out.dtype)


def join_kernel(a, b, out):
    rows = a.shape[0]
    out[:rows, :] = a[...]
    out[rows:, :] = b[...]


def joined(a, b):
    return pl.pallas_call(
        join_kernel,
        out_shape=jax.ShapeDtypeStruct((a.shape[0] + b.shape[0], a.shape[1]), a.dtype),
        in_specs=[IN_VMEM] * 2,
        out_specs=IN_VMEM,
        compiler_params=pltpu.CompilerParams(vmem_limit_bytes=8 * MIB),
        cost_estimate=pl.CostEstimate(flops=1, bytes_accessed=1, transcendentals=0),
    )(a, b)


def added(a, b, *more):
    return pl.pallas_call(
        add_kernel,
        out_shape=jax.ShapeDtypeStruct(a.shape, a.dtype),
        in_specs=[IN_VMEM] * (2 + len(more)),
        out_specs=IN_VMEM,
        compiler_params=pltpu.CompilerParams(vmem_limit_bytes=8 * MIB),
        cost_estimate=pl.CostEstimate(flops=1, bytes_accessed=1, transcendentals=0),
    )(a, b, *more)


def ring_body(tokens, cotangent, expert_ids, route_weights, gate_weight, up_weight, down_weight):
    ring_total = lax.axis_size("grp")
    loc_total = lax.axis_size("loc")
    width = tokens.shape[1]
    per_device = gate_weight.shape[0]
    order = list(range(0, ring_total, 2)) + list(range(ring_total - 1, 0, -2))
    ahead = [(order[i], order[(i + 1) % ring_total]) for i in range(ring_total)]
    behind = [(b, a) for a, b in ahead]
    rank, loc = lax.axis_index("grp"), lax.axis_index("loc")

    def send(pair):
        return lax.ppermute(pair[0], "grp", ahead), lax.ppermute(pair[1], "grp", behind)

    def send_back(pair):
        return lax.ppermute(pair[0], "grp", behind), lax.ppermute(pair[1], "grp", ahead)

    def tie(pair, *others):
        return tuple(lax.optimization_barrier((a, *others))[0] for a in pair)

    own = (gate_weight, up_weight, down_weight)
    other = [lax.ppermute(a, "loc", [(i, loc_total - 1 - i) for i in range(loc_total)]) for a in own]
    per_group = loc_total * per_device
    place = jnp.stack([rank * per_group, loc * per_device]).astype(jnp.int32)
    *blocks, table, order_up, order_down = pack(per_group, tokens, cotangent, expert_ids, route_weights)
    came = send(blocks)
    *loaded, loaded_own = load(place, *(in_hbm(a) for a in own))
    *others, last = load(loaded_own, *tie(other[:2], *came), other[2])
    loaded += others

    def call(after_this, plan, *packed, unrolled=False):
        *parts, token = experts_call(place, after_this, packed, plan, loaded, unrolled)
        return parts, token

    block = tokens.shape[0]
    half, most = ring_total // 2, 6 * block // ring_total
    half_block, cut = block // 2, most // 2
    rest, needed, extra = block - cut, (block + most) // 2 - half_block, half_block - cut
    long, short = [a[:half_block] for a in came], [a[half_block:, : 2 * width] for a in came]
    long_next, short_next = send(tie(long, loaded_own, *other)), send(tie(short, loaded_own, *other))
    own_plan = ((block, 0, 0),)
    mine, last = experts_call(place, last, (tokens, cotangent, table), own_plan, loaded, False)
    filler = last
    both_plan = ((cut, rest, 0),) * 2
    parts, last = call(last, both_plan, *came)
    long_terms, short_terms = [None, parts[0::2]], [None, parts[1::2]]
    for s in range(2, half - 1):
        long, short = long_next, short_next
        long_next = send(tie(long, filler))
        short_next = send(tie([a[:needed] for a in short] if s + 2 == half else short, last))
        parts, last = call(last, both_plan, long[0], short[0], long[1], short[1])
        long_terms.append(parts[0::2])
        short_terms.append(parts[1::2])
    long, short = long_next, short_next
    long_last = send(tie([a[:cut] for a in long], last))
    parts, last = call(last, ((cut, extra, 0),) * 2, *long)
    long_terms.append(parts[0::2])
    lower = parts[1::2]
    parts, last = call(last, ((0, needed, extra),) * 2, long[0], short[0], long[1], short[1], unrolled=True)
    short_back = send_back([joined(a, b) for a, b in zip(lower, parts[0::2])])
    carried = parts[1::2]
    parts, last = call(last, ((cut, 0, 0),) * 2, *long_last, unrolled=True)
    long_back = send_back(tie(parts, *short_back))
    for s in range(half - 1, 0, -1):
        if s < half - 1:
            short_back = send_back([added(a, b) for a, b in zip(short_terms[s], short_back)])
            long_back = send_back([added(a, b) for a, b in zip(long_terms[s], long_back)])
        else:
            long_back = send_back([added(a, b, c) for a, b, c in zip(long_terms[s], long_back, carried)])
    terms = (order_up, order_down, mine, long_back[0], short_back[0], long_back[1], short_back[1])
    return finish(expert_ids, terms, width)


def body(tokens, cotangent, expert_ids, route_weights, gate_weight, up_weight, down_weight):
    args = (tokens, cotangent, expert_ids, route_weights, gate_weight, up_weight, down_weight)
    ring_total, loc_total = lax.axis_size("grp"), lax.axis_size("loc")
    experts = ring_total * loc_total * gate_weight.shape[0]
    if loc_total == 2 and ring_total == 8 and experts <= SLOT and tokens.shape[0] == LANES:
        return ring_body(*args)
    return routed_body(*args)


def solution(mesh):
    placed = (
        P(("rep", "grp", "loc"), None),
        P(("rep", "grp", "loc"), None),
        P(("rep", "grp", "loc"), None),
        P(("rep", "grp", "loc"), None),
        P(("grp", "loc"), None, None),
        P(("grp", "loc"), None, None),
        P(("grp", "loc"), None, None),
    )
    return jax.shard_map(
        body,
        mesh=mesh,
        in_specs=placed,
        out_specs=(P(("rep", "grp", "loc"), None), P(("rep", "grp", "loc"), None)),
        check_vma=False,
    )
```

```python
import functools

import jax
import jax.numpy as jnp
from jax import lax
from jax.experimental import pallas as pl
from jax.experimental.pallas import tpu as pltpu
from jax.sharding import PartitionSpec as P

TOP = 8
TOP_GROUPS = 4


def shortened(shard):
    return jax.tree.map(lambda a: a.astype(jnp.bfloat16) if a.dtype == jnp.float32 else a, shard)


def take_rows(values, indices, filler):
    return jnp.take(values, indices, axis=0, mode="fill", fill_value=filler)


def route_table(targets, dest_total, capacity):
    token_total = targets.shape[0]
    dest_iota = jnp.arange(dest_total, dtype=jnp.int32)
    reached = jnp.any(targets[:, :, None] == dest_iota[None, None, :], axis=1)
    ranked = jnp.cumsum(reached.astype(jnp.int32), axis=0) - 1
    slot_of = jnp.where(reached, ranked, capacity)
    dest_grid = jnp.broadcast_to(dest_iota[None, :], slot_of.shape)
    token_grid = jnp.broadcast_to(jnp.arange(token_total, dtype=jnp.int32)[:, None], slot_of.shape)
    sources = jnp.full((dest_total, capacity), token_total, jnp.int32)
    sources = sources.at[dest_grid, slot_of].set(token_grid, mode="drop")
    return (slot_of, sources)


def token_groups(group_ids, group_total):
    token_total = group_ids.shape[0]
    group_iota = jnp.arange(group_total, dtype=jnp.int32)
    reached = jnp.any(group_ids[:, :, None] == group_iota[None, None, :], axis=1)
    ranked = jnp.cumsum(reached.astype(jnp.int32), axis=1) - 1
    column = jnp.where(reached, ranked, TOP_GROUPS)
    token_grid = jnp.broadcast_to(jnp.arange(token_total, dtype=jnp.int32)[:, None], column.shape)
    listed = jnp.full((token_total, TOP_GROUPS), group_total, jnp.int32)
    return listed.at[token_grid, column].set(
        jnp.broadcast_to(group_iota[None, :], column.shape), mode="drop"
    )


def expert_pass(
    token_rows,
    grad_rows,
    id_rows,
    weight_rows,
    gate_weight,
    up_weight,
    down_weight,
    first_expert,
    capacity,
):
    row_total = token_rows.shape[0]
    local_total = gate_weight.shape[0]
    model_width = token_rows.shape[1]
    experts_here = first_expert + jnp.arange(local_total, dtype=jnp.int32)
    matched = id_rows[None, :, :] == experts_here[:, None, None]
    chosen = jnp.any(matched, axis=2)
    weight_of = jnp.sum(
        jnp.where(matched, weight_rows.astype(jnp.float32)[None, :, :], 0.0), axis=2
    )
    ranked = jnp.cumsum(chosen.astype(jnp.int32), axis=1) - 1
    slot_of = jnp.where(chosen, ranked, capacity)
    expert_grid = jnp.broadcast_to(jnp.arange(local_total, dtype=jnp.int32)[:, None], slot_of.shape)
    row_grid = jnp.broadcast_to(jnp.arange(row_total, dtype=jnp.int32)[None, :], slot_of.shape)
    picks = (
        jnp.full((local_total, capacity), row_total, jnp.int32)
        .at[expert_grid, slot_of]
        .set(row_grid, mode="drop")
    )
    buffer_x = take_rows(token_rows, picks, 0)
    buffer_g = take_rows(grad_rows, picks, 0)
    buffer_w = jnp.take_along_axis(weight_of, picks, axis=1, mode="fill", fill_value=0.0)
    gate_act = jnp.einsum("ecd,edf->ecf", buffer_x, gate_weight, preferred_element_type=jnp.float32)
    up_act = jnp.einsum("ecd,edf->ecf", buffer_x, up_weight, preferred_element_type=jnp.float32)
    back_grad = jnp.einsum(
        "ecd,efd->ecf", buffer_g, down_weight, preferred_element_type=jnp.float32
    )
    sigmoid_val = jax.nn.sigmoid(gate_act)
    silu_val = gate_act * sigmoid_val
    route_grad = jnp.sum(back_grad * silu_val * up_act, axis=2)
    hidden_grad = buffer_w[:, :, None] * back_grad
    gate_grad = (
        hidden_grad * up_act * sigmoid_val * (1.0 + gate_act * (1.0 - sigmoid_val))
    ).astype(jnp.bfloat16)
    up_grad = (hidden_grad * silu_val).astype(jnp.bfloat16)
    input_grad = jnp.einsum(
        "ecf,edf->ecd", gate_grad, gate_weight, preferred_element_type=jnp.float32
    )
    input_grad = input_grad + jnp.einsum(
        "ecf,edf->ecd", up_grad, up_weight, preferred_element_type=jnp.float32
    )
    partial_value = jnp.zeros((row_total, model_width), jnp.float32)
    partial_value = partial_value.at[picks.reshape(-1)].add(
        input_grad.reshape(-1, model_width), mode="drop"
    )
    cap_grid = jnp.broadcast_to(jnp.arange(local_total, dtype=jnp.int32)[:, None], picks.shape)
    route_per = (
        jnp.zeros((local_total, row_total), jnp.float32)
        .at[cap_grid, picks]
        .add(route_grad, mode="drop")
    )
    route_rows = jnp.sum(jnp.where(matched, route_per[:, :, None], 0.0), axis=0)
    return (partial_value, route_rows)


def routed_body(tokens, cotangent, expert_ids, route_weights, gate_weight, up_weight, down_weight):
    group_total = lax.axis_size("grp")
    loc_total = lax.axis_size("loc")
    token_total = tokens.shape[0]
    model_width = tokens.shape[1]
    per_device = gate_weight.shape[0]
    per_group = per_device * loc_total
    group_cap = 6 * token_total // group_total
    expert_cap = 3 * token_total * loc_total
    device_rank = lax.axis_index("grp") * loc_total + lax.axis_index("loc")
    first_expert = device_rank * per_device
    group_ids = expert_ids // per_group
    listed = token_groups(group_ids, group_total)
    slot_range = jnp.arange(TOP, dtype=jnp.int32)[None, :]
    slot_of, sources = route_table(group_ids, group_total, group_cap)
    send_x = take_rows(tokens, sources, 0)
    send_g = take_rows(cotangent, sources, 0)
    send_ids = take_rows(expert_ids, sources, -1)
    send_w = take_rows(route_weights, sources, 0)
    recv_x, recv_g, recv_ids, recv_w = (
        lax.all_to_all(send_x, "grp", split_axis=0, concat_axis=0, tiled=True),
        lax.all_to_all(send_g, "grp", split_axis=0, concat_axis=0, tiled=True),
        lax.all_to_all(send_ids, "grp", split_axis=0, concat_axis=0, tiled=True),
        lax.all_to_all(send_w, "grp", split_axis=0, concat_axis=0, tiled=True),
    )
    row_total = group_total * group_cap
    shared_x, shared_g, shared_ids, shared_w = (
        lax.all_gather(recv_x.reshape(row_total, model_width), "loc", axis=0, tiled=True),
        lax.all_gather(recv_g.reshape(row_total, model_width), "loc", axis=0, tiled=True),
        lax.all_gather(shortened(recv_ids.reshape(row_total, TOP)), "loc", axis=0, tiled=True),
        lax.all_gather(recv_w.reshape(row_total, TOP), "loc", axis=0, tiled=True),
    )
    partial_value, route_rows = expert_pass(
        shared_x,
        shared_g,
        shared_ids,
        shared_w,
        gate_weight,
        up_weight,
        down_weight,
        first_expert,
        expert_cap,
    )
    summed, route_sum = (
        lax.psum_scatter(partial_value, "loc", scatter_dimension=0, tiled=True),
        lax.psum_scatter(route_rows, "loc", scatter_dimension=0, tiled=True),
    )
    group_part = summed.astype(jnp.bfloat16).reshape(group_total, group_cap, model_width)
    route_part = route_sum.astype(jnp.bfloat16).reshape(group_total, group_cap, TOP)
    back_terms, back_route = (
        lax.all_to_all(group_part, "grp", split_axis=0, concat_axis=0, tiled=True),
        lax.all_to_all(route_part, "grp", split_axis=0, concat_axis=0, tiled=True),
    )
    slot_pad = jnp.concatenate([slot_of, jnp.full((token_total, 1), group_cap, jnp.int32)], axis=1)
    found = jnp.take_along_axis(slot_pad, listed, axis=1)
    position = jnp.where(found < group_cap, listed * group_cap + found, row_total)
    pieces = take_rows(back_terms.reshape(row_total, model_width), position, 0)
    grad_tokens = jnp.sum(pieces.astype(jnp.float32), axis=1).astype(jnp.bfloat16)
    slot_found = jnp.take_along_axis(slot_of, group_ids, axis=1)
    route_index = (group_ids * group_cap + slot_found) * TOP + slot_range
    grad_weights = back_route.reshape(row_total * TOP)[route_index]
    return (grad_tokens, grad_weights)


LANES = 128
SLOT = 32
NT = (((1,), (1,)), ((), ()))
ANYWHERE = pl.BlockSpec(memory_space=pl.ANY)
IN_VMEM = pl.BlockSpec(memory_space=pltpu.VMEM)
IN_SMEM = pl.BlockSpec(memory_space=pltpu.SMEM)
MIB = 1024 * 1024
TOKEN = jax.ShapeDtypeStruct((8, LANES), jnp.float32)


def ring_rank(steps):
    total, rank = lax.axis_size("grp"), lax.axis_index("grp")
    half = lax.shift_right_logical(rank + 1, 1)
    place = jnp.where(lax.rem(rank, 2) == 0, half, total - half) + steps
    place = jnp.where(place >= total, place - total, place)
    return jnp.where(2 * place < total, 2 * place, 2 * (total - place) - 1)


def pack_kernel(per_group, tokens, cotangent, ids, weights, *refs):
    up_block, down_block, table_out, *orders, ids_here, weights_here, rows_here, sems = refs
    rows, width = tokens.shape
    half = lax.axis_size("grp") // 2
    small = (
        pltpu.make_async_copy(ids, ids_here, sems.at[0]),
        pltpu.make_async_copy(weights, weights_here, sems.at[1]),
    )
    large = (
        pltpu.make_async_copy(tokens, rows_here.at[:, pl.ds(0, width)], sems.at[2]),
        pltpu.make_async_copy(cotangent, rows_here.at[:, pl.ds(width, width)], sems.at[3]),
    )
    for copy in small + large:
        copy.start()
    for copy in small:
        copy.wait()
    first_experts = [ring_rank(steps) * per_group for steps in (half - 1, half + 1, half)]
    sublane = lax.broadcasted_iota(jnp.int32, (LANES, rows), 0)
    table = jnp.zeros((LANES, rows), jnp.float32)
    named = [jnp.zeros((1, rows), jnp.int32) for _ in first_experts]
    for k in range(ids.shape[0]):
        chosen = ids_here[k : k + 1, :]
        table += jnp.where(sublane == chosen, weights_here[k : k + 1, :].astype(jnp.float32), 0.0)
        named = [
            n | jnp.where((chosen >= first) & (chosen < first + per_group), 1, 0)
            for n, first in zip(named, first_experts)
        ]
    from_row = lax.broadcasted_iota(jnp.int32, (rows, rows), 0)
    to_row = lax.broadcasted_iota(jnp.int32, (rows, rows), 1)
    upper = jnp.where(from_row <= to_row, 1.0, 0.0).astype(jnp.bfloat16)
    sixteen = lax.broadcasted_iota(jnp.int32, (16, rows), 0)

    def ranks(flags):
        stacked = jnp.zeros((16, rows), jnp.float32)
        for i, flag in enumerate(flags):
            stacked = jnp.where(sixteen == i, flag.astype(jnp.float32), stacked)
        stacked = stacked.astype(jnp.bfloat16)
        counts = jnp.dot(stacked, upper, preferred_element_type=jnp.float32).astype(jnp.int32)
        totals = jnp.dot(stacked, jnp.ones_like(upper), preferred_element_type=jnp.float32).astype(jnp.int32)
        rows_of = range(len(flags))
        return [counts[i : i + 1, :] - 1 for i in rows_of], [totals[i : i + 1, :] for i in rows_of]

    up, down, across = named
    kinds = (across * up * (1 - down), across * (1 - up) * (1 - down), across * up * down, across * (1 - up) * down)
    (only_up, neither, both, only_down), (n_up, n_neither, n_both, n_down) = ranks(kinds)
    early = lax.shift_right_logical(n_neither + 1, 1)
    on_line = jnp.where(
        kinds[0] > 0,
        only_up,
        jnp.where(
            kinds[1] > 0,
            n_up + neither + jnp.where(neither < early, 0, n_both),
            jnp.where(kinds[2] > 0, n_up + early + both, n_up + n_neither + n_both + only_down),
        ),
    )
    middle = lax.shift_right_logical(n_up + n_neither + n_both + n_down + 1, 1)
    ahead = across * jnp.where(on_line < middle, 1, 0)
    firsts = (ahead, across - ahead)
    sets = []
    for first, near in zip(firsts, (up, down)):
        second = near * (1 - first)
        sets += [first, second, (1 - first) * (1 - second)]
    places, totals = ranks(sets)
    for i in range(2):
        target = jnp.where(
            sets[3 * i] > 0,
            places[3 * i],
            totals[3 * i]
            + jnp.where(sets[3 * i + 1] > 0, places[3 * i + 1], totals[3 * i + 1] + places[3 * i + 2]),
        )
        orders[i][...] = jnp.where(from_row == target, 1.0, 0.0).astype(jnp.bfloat16)
    table_out[...] = table.T.astype(jnp.bfloat16)
    blocks = up_block, down_block
    far = (sublane >= first_experts[2]) & (sublane < first_experts[2] + per_group)
    for block, order, first in zip(blocks, orders, firsts):
        mine = jnp.where(far & (first == 0), 0.0, table).astype(jnp.bfloat16)
        block[:, 2 * width :] = lax.dot_general(order[...], mine, NT, preferred_element_type=jnp.float32).astype(
            jnp.bfloat16
        )
    for copy in large:
        copy.wait()
    for block, order in zip(blocks, orders):
        for lanes in (slice(0, width), slice(width, 2 * width)):
            block[:, lanes] = jnp.dot(order[...], rows_here[:, lanes], preferred_element_type=jnp.float32).astype(
                jnp.bfloat16
            )


def pack(per_group, tokens, cotangent, ids, weights):
    rows, width = tokens.shape
    shape = (rows, 2 * width + LANES)
    order = jax.ShapeDtypeStruct((rows, rows), jnp.bfloat16)
    return pl.pallas_call(
        functools.partial(pack_kernel, per_group),
        out_shape=(
            jax.ShapeDtypeStruct(shape, jnp.bfloat16),
            jax.ShapeDtypeStruct(shape, jnp.bfloat16),
            jax.ShapeDtypeStruct((rows, LANES), jnp.bfloat16),
            order,
            order,
        ),
        in_specs=[ANYWHERE] * 4,
        out_specs=(IN_VMEM,) * 5,
        scratch_shapes=[
            pltpu.VMEM((ids.shape[1], rows), jnp.int32),
            pltpu.VMEM((ids.shape[1], rows), jnp.bfloat16),
            pltpu.VMEM((rows, 2 * width), jnp.bfloat16),
            pltpu.SemaphoreType.DMA((4,)),
        ],
        compiler_params=pltpu.CompilerParams(vmem_limit_bytes=7 * MIB),
    )(*(in_hbm(a) for a in (tokens, cotangent, ids.T, weights.T)))


def in_hbm(a):
    return pltpu.with_memory_space_constraint(a, pltpu.HBM)


def in_vmem(a):
    return pltpu.with_memory_space_constraint(a, pltpu.VMEM)


def load_kernel(after_this, gate, up, down, gate_up, back, down_back, token, down_here, sems):
    del after_this
    token[...] = jnp.zeros_like(token)
    per_device, hidden = gate.shape[0], gate.shape[2]
    copies = []
    for e in range(per_device):
        copies.append(
            (
                pltpu.make_async_copy(down.at[e], down_here.at[e], sems.at[2, e]),
                pltpu.make_async_copy(gate.at[e], gate_up.at[e, :, pl.ds(0, hidden)], sems.at[0, e]),
                pltpu.make_async_copy(up.at[e], gate_up.at[e, :, pl.ds(hidden, hidden)], sems.at[1, e]),
            )
        )
    for three in copies:
        for copy in three:
            copy.start()
    for e, (first, second, third) in enumerate(copies):
        first.wait()
        down_back[:, e * hidden : (e + 1) * hidden] = down_here[e].T
        second.wait()
        third.wait()
        back[2 * e * hidden : 2 * (e + 1) * hidden, :] = gate_up[e].T


def load(after_this, gate, up, down):
    per_device, width, hidden = gate.shape
    return pl.pallas_call(
        load_kernel,
        out_shape=(
            pltpu.VMEM((per_device, width, 2 * hidden), jnp.bfloat16),
            pltpu.VMEM((2 * per_device * hidden, width), jnp.bfloat16),
            pltpu.VMEM((width, per_device * hidden), jnp.bfloat16),
            TOKEN,
        ),
        in_specs=[ANYWHERE] * 4,
        out_specs=(IN_VMEM,) * 4,
        scratch_shapes=[pltpu.VMEM(down.shape, jnp.bfloat16), pltpu.SemaphoreType.DMA((3, per_device))],
        compiler_params=pltpu.CompilerParams(vmem_limit_bytes=8 * MIB),
        cost_estimate=pl.CostEstimate(flops=1, bytes_accessed=24 * MIB, transcendentals=0),
    )(after_this, gate, up, down)


def experts_kernel(inputs, plan, unrolled, place, after_this, *refs):
    del after_this
    given, refs = refs[:inputs], refs[inputs:]
    loaded, refs = (refs[:3], refs[3:6]), refs[6:]
    *outs, token = refs
    token[...] = jnp.zeros_like(token)
    per_device, width, both_hidden = loaded[0][0].shape
    hidden = both_hidden // 2
    if given[0].shape[1] > width:
        x = jnp.concatenate([a[:, :width] for a in given], axis=0)
        g = jnp.concatenate([a[:, width : 2 * width] for a in given], axis=0)
        table = jnp.concatenate([a[:, 2 * width :] for a in given], axis=0)
    else:
        x, g, table = (a[...] for a in given)
    spare = -x.shape[0] % (LANES // 2)
    if spare:
        x, g, table = (jnp.concatenate([a, jnp.zeros((spare, a.shape[1]), a.dtype)], axis=0) for a in (x, g, table))
    table = table.astype(jnp.float32)
    lane = lax.broadcasted_iota(jnp.int32, table.shape, 1)
    route = jnp.zeros(table.shape, jnp.float32)
    grads = []
    for pair, (gate_up, _, down_back) in enumerate(loaded):
        backs = jnp.dot(g, down_back[...], preferred_element_type=jnp.float32)
        mine = []
        for at in range(per_device):
            back = backs[:, at * hidden : (at + 1) * hidden]
            column = place[0] + lax.rem(place[1] + pair * per_device + at, 2 * per_device)
            weight = jnp.sum(jnp.where(lane == column, table, 0.0), axis=1, keepdims=True)
            both = jnp.dot(x, gate_up[at], preferred_element_type=jnp.float32)
            gate_act, up_act = both[:, :hidden], both[:, hidden:]
            sig = jax.nn.sigmoid(gate_act)
            silu = gate_act * sig
            back_up = back * up_act
            route_grad = jnp.sum(back_up * silu, axis=1, keepdims=True)
            mine.append((weight * back_up * sig * (1.0 + gate_act * (1.0 - sig))).astype(jnp.bfloat16))
            mine.append((weight * back * silu).astype(jnp.bfloat16))
            route += jnp.where((lane == column) & (weight > 0.0), route_grad, 0.0)
        grads.append(jnp.concatenate(mine, axis=1))
    step = 4 * LANES

    def chunk(i, carry):
        part = pl.ds(pl.multiple_of(i * step, step), step)
        total = sum(
            jnp.dot(a, back[:, part], preferred_element_type=jnp.float32) for a, (_, back, _) in zip(grads, loaded)
        ).astype(jnp.bfloat16)
        for out, start, rows in grads_at:
            out[:, part] = total[start : start + rows]
        return carry

    grads_at, routes_at = [], []
    start = at_out = 0
    for long, short, first in plan:
        if long:
            grads_at.append((outs[at_out], start, long))
            routes_at.append((outs[at_out], width, (start, long), (start + long, short, first)))
            at_out += 1
        if short:
            grads_at.append((outs[at_out], start + long, short))
            at_out += 1
            if not long:
                routes_at.append((outs[at_out], 0, (start, 0), (start, short, first)))
                at_out += 1
        start += long + short
    lax.fori_loop(0, width // step, chunk, 0, unroll=unrolled)
    for out, lanes, (start, long), (short_start, short, first) in routes_at:
        rows = out.shape[0]
        carried = route[start : start + long] if long else jnp.zeros((rows, LANES), jnp.float32)
        if short:
            split = min(short, rows - first)
            carried += shifted(route[short_start : short_start + split], 1, first, rows)
            if short > split:
                carried += shifted(route[short_start + split : short_start + short], 2, 0, rows)
        out[:, lanes : lanes + LANES] = carried.astype(out.dtype)


def shifted(route, slot, first, rows):
    moved = pltpu.roll(route, slot * SLOT, 1)
    parts = [moved]
    if first:
        parts.insert(0, jnp.zeros((first, LANES), route.dtype))
    if rows > first + route.shape[0]:
        parts.append(jnp.zeros((rows - first - route.shape[0], LANES), route.dtype))
    return jnp.concatenate(parts, axis=0) if len(parts) > 1 else moved


def experts_call(place, after_this, given, plan, loaded, unrolled):
    width = loaded[0].shape[1]
    shapes = []
    for long, short, _ in plan:
        shapes += [(long, width + LANES)] * (long > 0) + [(short, width)] * (short > 0)
        shapes += [(short, LANES)] * (not long)
    return pl.pallas_call(
        functools.partial(experts_kernel, len(given), plan, unrolled),
        out_shape=[jax.ShapeDtypeStruct(shape, jnp.bfloat16) for shape in shapes] + [TOKEN],
        in_specs=[IN_SMEM, ANYWHERE] + [IN_VMEM] * (len(given) + 6),
        out_specs=[IN_VMEM] * (len(shapes) + 1),
        compiler_params=pltpu.CompilerParams(vmem_limit_bytes=12 * MIB),
        cost_estimate=pl.CostEstimate(flops=1, bytes_accessed=1, transcendentals=0),
    )(place, after_this, *(in_vmem(a) for a in given), *loaded)


def finish_kernel(ids, order_up, order_down, mine, long_up, short_up, long_down, short_down, grad_tokens, grad_weights):
    width = grad_tokens.shape[1]
    backs = order_up[...].T, order_down[...].T
    summed = mine[:, :width].astype(jnp.float32)
    route = mine[:, width:].astype(jnp.float32)
    for back, long, short in zip(backs, (long_up, long_down), (short_up, short_down)):
        rows, spare = long.shape[0], short.shape[0] - long.shape[0]
        came = jnp.concatenate([long[:, :width], short[...]], axis=0)
        summed += jnp.dot(back, came, preferred_element_type=jnp.float32)
        carried = long[:, width:].astype(jnp.float32)
        first = lax.broadcasted_iota(jnp.int32, carried.shape, 1) < SLOT
        slots = [jnp.where(first, pltpu.roll(carried, (LANES - k * SLOT) % LANES, 1), 0.0) for k in range(3)]
        came = jnp.concatenate([slots[0], slots[1], slots[2][:spare]], axis=0).astype(jnp.bfloat16)
        route += jnp.dot(back, came, preferred_element_type=jnp.float32)
    grad_tokens[...] = summed.astype(grad_tokens.dtype)
    route = route.T
    expert = lax.broadcasted_iota(jnp.int32, route.shape, 0)
    found = [
        jnp.sum(jnp.where(expert == ids[k : k + 1, :], route, 0.0), axis=0, keepdims=True) for k in range(ids.shape[0])
    ]
    grad_weights[...] = jnp.concatenate(found, axis=0).astype(grad_weights.dtype)


def finish(ids, terms, width):
    rows, top = ids.shape
    grad_tokens, grad_weights = pl.pallas_call(
        finish_kernel,
        out_shape=(
            jax.ShapeDtypeStruct((rows, width), jnp.bfloat16),
            jax.ShapeDtypeStruct((top, rows), jnp.bfloat16),
        ),
        in_specs=[IN_VMEM] * 8,
        out_specs=(IN_VMEM, IN_VMEM),
        compiler_params=pltpu.CompilerParams(vmem_limit_bytes=12 * MIB),
    )(ids.T, *terms)
    return grad_tokens, grad_weights.T


def add_kernel(a, b, *refs):
    *more, out = refs
    rows = b.shape[0]
    if rows < a.shape[0]:
        out[rows:, :] = a[rows:, :]
    out[:rows, :] = (a[:rows, :].astype(jnp.float32) + b[...].astype(jnp.float32)).astype(out.dtype)
    for c in more:
        width = a.shape[1] - c.shape[1]
        total = a[:, width:].astype(jnp.float32) + b[:, width:].astype(jnp.float32) + c[...].astype(jnp.float32)
        out[:, width:] = total.astype(out.dtype)


def join_kernel(a, b, out):
    rows = a.shape[0]
    out[:rows, :] = a[...]
    out[rows:, :] = b[...]


def joined(a, b):
    return pl.pallas_call(
        join_kernel,
        out_shape=jax.ShapeDtypeStruct((a.shape[0] + b.shape[0], a.shape[1]), a.dtype),
        in_specs=[IN_VMEM] * 2,
        out_specs=IN_VMEM,
        compiler_params=pltpu.CompilerParams(vmem_limit_bytes=8 * MIB),
        cost_estimate=pl.CostEstimate(flops=1, bytes_accessed=1, transcendentals=0),
    )(a, b)


def added(a, b, *more):
    return pl.pallas_call(
        add_kernel,
        out_shape=jax.ShapeDtypeStruct(a.shape, a.dtype),
        in_specs=[IN_VMEM] * (2 + len(more)),
        out_specs=IN_VMEM,
        compiler_params=pltpu.CompilerParams(vmem_limit_bytes=8 * MIB),
        cost_estimate=pl.CostEstimate(flops=1, bytes_accessed=1, transcendentals=0),
    )(a, b, *more)


def ring_body(tokens, cotangent, expert_ids, route_weights, gate_weight, up_weight, down_weight):
    ring_total = lax.axis_size("grp")
    loc_total = lax.axis_size("loc")
    width = tokens.shape[1]
    per_device = gate_weight.shape[0]
    order = list(range(0, ring_total, 2)) + list(range(ring_total - 1, 0, -2))
    ahead = [(order[i], order[(i + 1) % ring_total]) for i in range(ring_total)]
    behind = [(b, a) for a, b in ahead]
    rank, loc = lax.axis_index("grp"), lax.axis_index("loc")

    def send(pair):
        return lax.ppermute(pair[0], "grp", ahead), lax.ppermute(pair[1], "grp", behind)

    def send_back(pair):
        return lax.ppermute(pair[0], "grp", behind), lax.ppermute(pair[1], "grp", ahead)

    def tie(pair, *others):
        return tuple(lax.optimization_barrier((a, *others))[0] for a in pair)

    own = (gate_weight, up_weight, down_weight)
    other = [lax.ppermute(a, "loc", [(i, loc_total - 1 - i) for i in range(loc_total)]) for a in own]
    per_group = loc_total * per_device
    place = jnp.stack([rank * per_group, loc * per_device]).astype(jnp.int32)
    *blocks, table, order_up, order_down = pack(per_group, tokens, cotangent, expert_ids, route_weights)
    came = send(blocks)
    *loaded, loaded_own = load(place, *(in_hbm(a) for a in own))
    *others, last = load(loaded_own, *tie(other[:2], *came), other[2])
    loaded += others

    def call(after_this, plan, *packed, unrolled=False):
        *parts, token = experts_call(place, after_this, packed, plan, loaded, unrolled)
        return parts, token

    block = tokens.shape[0]
    half, most = ring_total // 2, 6 * block // ring_total
    half_block, cut = block // 2, most // 2
    rest, needed, extra = block - cut, (block + most) // 2 - half_block, half_block - cut
    long, short = [a[:half_block] for a in came], [a[half_block:] for a in came]
    long_next, short_next = send(tie(long, loaded_own, *other)), send(tie(short, loaded_own, *other))
    own_plan = ((block, 0, 0),)
    mine, last = experts_call(place, last, (tokens, cotangent, table), own_plan, loaded, False)
    filler = last
    both_plan = ((cut, rest, 0),) * 2
    parts, last = call(last, both_plan, *came)
    long_terms, short_terms = [None, parts[0::2]], [None, parts[1::2]]
    for s in range(2, half - 1):
        long, short = long_next, short_next
        long_next = send(tie(long, filler))
        short_next = send(tie([a[:needed] for a in short] if s + 2 == half else short, last))
        parts, last = call(last, both_plan, long[0], short[0], long[1], short[1])
        long_terms.append(parts[0::2])
        short_terms.append(parts[1::2])
    long, short = long_next, short_next
    long_last = send(tie([a[:cut] for a in long], last))
    parts, last = call(last, ((cut, extra, 0),) * 2, *long)
    long_terms.append(parts[0::2])
    lower = parts[1::2]
    parts, last = call(last, ((0, needed, extra),) * 2, *short)
    short_back = send_back([joined(a, b) for a, b in zip(lower, parts[0::2])])
    carried = parts[1::2]
    parts, last = call(last, ((cut, 0, 0),) * 2, *long_last, unrolled=True)
    long_back = send_back(tie(parts, *short_back))
    for s in range(half - 1, 0, -1):
        if s < half - 1:
            short_back = send_back([added(a, b) for a, b in zip(short_terms[s], short_back)])
            long_back = send_back([added(a, b) for a, b in zip(long_terms[s], long_back)])
        else:
            long_back = send_back([added(a, b, c) for a, b, c in zip(long_terms[s], long_back, carried)])
    terms = (order_up, order_down, mine, long_back[0], short_back[0], long_back[1], short_back[1])
    return finish(expert_ids, terms, width)


def body(tokens, cotangent, expert_ids, route_weights, gate_weight, up_weight, down_weight):
    args = (tokens, cotangent, expert_ids, route_weights, gate_weight, up_weight, down_weight)
    ring_total, loc_total = lax.axis_size("grp"), lax.axis_size("loc")
    experts = ring_total * loc_total * gate_weight.shape[0]
    if loc_total == 2 and ring_total == 8 and experts <= SLOT and tokens.shape[0] == LANES:
        return ring_body(*args)
    return routed_body(*args)


def solution(mesh):
    placed = (
        P(("rep", "grp", "loc"), None),
        P(("rep", "grp", "loc"), None),
        P(("rep", "grp", "loc"), None),
        P(("rep", "grp", "loc"), None),
        P(("grp", "loc"), None, None),
        P(("grp", "loc"), None, None),
        P(("grp", "loc"), None, None),
    )
    return jax.shard_map(
        body,
        mesh=mesh,
        in_specs=placed,
        out_specs=(P(("rep", "grp", "loc"), None), P(("rep", "grp", "loc"), None)),
        check_vma=False,
    )
```
